128 devices in a mesh: dp: 4 (over y_hi, core), row: 4 (over x), col: 8 (over z, y_lo).
Axes of the slice: x: 4, y: 4 (y_hi: 2, y_lo: 2; y = y_hi * 2 + y_lo), z: 4, core: 2. Of those that a mesh axis runs over, the one named last changes fastest.
Arguments:
- input_map: bfloat16 [4, 64, 512, 256], P('dp', 'row', 'col'), may hold values from -6 to 6
- dw_kernel: bfloat16 [3, 3, 256], replicated, may hold values from -2 to 2
- gain_one: float32 [256], replicated, may hold values from 0.1 to 1.9
- w_qkv: bfloat16 [256, 768], replicated, may hold values from -4 to 4
- w_out: bfloat16 [256, 256], replicated, may hold values from -0.375 to 0.375
- gain_two: float32 [256], replicated, may hold values from 0.1 to 1.9
- w_up: bfloat16 [256, 1024], replicated, may hold values from -0.375 to 0.375
- w_down: bfloat16 [1024, 256], replicated, may hold values from -0.1875 to 0.1875
- cotangent: bfloat16 [4, 64, 512, 256], P('dp', 'row', 'col'), may hold values from -6 to 6
Outputs:
- input_grad: float32 [4, 64, 512, 256], P('dp', 'row', 'col')
- kernel_grad: float32 [3, 3, 256], replicated
- gain_one_grad: float32 [256], replicated
- qkv_grad: float32 [256, 768], replicated
- out_grad: float32 [256, 256], replicated
- gain_two_grad: float32 [256], replicated
- up_grad: float32 [256, 1024], replicated
- down_grad: float32 [1024, 256], replicated
The draws below stay inside these ranges and needn't reach their ends.
All inputs are finite; a program needn't handle non-finite values.
Results may differ from the reference program's by a relative error of at most 0.0085.
The reference program's roundings to bfloat16 on the way count: a program that leaves them out, or rounds other values in their place, can miss the bound.
Values may be sent and summed in bfloat16 or wider, within the bound.
No kernel may reach another device: no remote copies, remote signals or barrier semaphores. Data moves between devices by JAX's collectives and lax.ppermute only.
A program may use at most 128 MiB of HBM per device.

```python
import math
import jax
import jax.numpy as jnp
from jax import lax

HEADS = 8
C = 256
FF = 1024
GRID = 8
BATCH = 4
H = 64
W = 512
SPAN_H = 8
SPAN_W = 64
ALL_TOKENS = 131072


def draw_w_qkv(key, part):
    key = jax.random.fold_in(key, 7)
    head_dim = C // HEADS
    sampled = jax.random.normal(jax.random.fold_in(key, 1), (C, 3, HEADS, head_dim), jnp.float32) * (1.0 / math.sqrt(C))
    return jnp.clip(sampled, -4.0, 4.0).reshape(C, 3 * C).astype(jnp.bfloat16)


def levels(own_key, extent, cuts, low, largest):
    level = 1.0
    for position, blocks in cuts:
        heights = jax.random.uniform(jax.random.fold_in(jax.random.fold_in(own_key, 6), position), (blocks,), jnp.float32, low / len(cuts), largest / len(cuts))
        level = level * jnp.repeat(jnp.exp(heights), extent[position] // blocks).reshape((-1,) + (1,) * (len(extent) - 1 - position))
    return level


def normal_values(own_key, dims, spread, bound, cuts=(), held_as=jnp.bfloat16):
    entries = spread * jax.random.normal(own_key, dims, jnp.float32)
    if cuts:
        entries = entries * levels(own_key, dims, cuts, -0.22, 0.18)
    return jnp.clip(entries, -bound, bound).astype(held_as)


def setup_inputs(seed: int = 0) -> dict:
    splits = jax.random.split(jax.random.key(seed), 10)
    input_map = normal_values(splits[0], (BATCH, H, W, C), 1.0, 6.0, ((0, 4), (1, 4), (2, 8)))
    dw_kernel = normal_values(splits[1], (3, 3, C), 9 ** -0.5, 2.0)
    gain_one = jnp.clip(1.0 + 0.18 * jax.random.normal(splits[2], (C,), jnp.float32), 0.1, 1.9)
    w_qkv = draw_w_qkv(jax.random.fold_in(splits[9], 71), 0)
    w_out = normal_values(splits[4], (C, C), C ** -0.5, 0.375)
    gain_two = jnp.clip(1.0 + 0.18 * jax.random.normal(splits[5], (C,), jnp.float32), 0.1, 1.9)
    w_up = normal_values(splits[6], (C, FF), C ** -0.5, 0.375)
    w_down = normal_values(splits[7], (FF, C), FF ** -0.5, 0.1875)
    cotangent = normal_values(splits[8], (BATCH, H, W, C), 1.0, 6.0, ((0, 4), (1, 4), (2, 8)))
    return dict(input_map=input_map, dw_kernel=dw_kernel, gain_one=gain_one, w_qkv=w_qkv, w_out=w_out, gain_two=gain_two, w_up=w_up, w_down=w_down, cotangent=cotangent)


norm_eps = 1e-05
gelu_coef = 0.7978845608028654
cubic_coef = 0.044715

def depthwise(padded, dw_kernel):
    row_count = padded.shape[0] - 2
    col_count = padded.shape[1] - 2
    accumulated = padded[1:row_count + 1, 1:col_count + 1].astype(jnp.float32)
    for vertical in range(3):
        for lateral in range(3):
            accumulated = accumulated + dw_kernel[vertical, lateral].astype(jnp.float32) * padded[vertical:vertical + row_count, lateral:lateral + col_count].astype(jnp.float32)
    return accumulated

def depthwise_back(grad_pad, padded, dw_kernel):
    row_count = grad_pad.shape[0] - 2
    col_count = grad_pad.shape[1] - 2
    centre = grad_pad[1:row_count + 1, 1:col_count + 1].astype(jnp.float32)
    accumulated = centre
    kernel_terms = []
    for vertical in range(3):
        for lateral in range(3):
            accumulated = accumulated + dw_kernel[vertical, lateral].astype(jnp.float32) * grad_pad[2 - vertical:2 - vertical + row_count, 2 - lateral:2 - lateral + col_count].astype(jnp.float32)
            kernel_terms.append(lax.optimization_barrier(jnp.sum(centre * padded[vertical:vertical + row_count, lateral:lateral + col_count].astype(jnp.float32), axis=(0, 1))))
    return (accumulated, jnp.stack(kernel_terms).reshape(3, 3, -1))

def norm_forward(values, gain):
    values = values.astype(jnp.float32)
    center = values - lax.optimization_barrier(jnp.mean(values, axis=-1, keepdims=True))
    inverse = lax.rsqrt(lax.optimization_barrier(jnp.mean(center * center, axis=-1, keepdims=True)) + norm_eps)
    normed = center * inverse
    return (normed, inverse, (normed * gain).astype(jnp.bfloat16))

def norm_backward(upstream, normed, inverse, gain):
    gain_grad = lax.optimization_barrier(jnp.sum(upstream * normed, axis=tuple(range(upstream.ndim - 1))))
    scaled = upstream * gain
    inner = scaled - lax.optimization_barrier(jnp.mean(scaled, axis=-1, keepdims=True)) - normed * lax.optimization_barrier(jnp.mean(scaled * normed, axis=-1, keepdims=True))
    return (inverse * inner, gain_grad)

def attend_forward(grouped, w_qkv, gain_one):
    group_count, members, width = grouped.shape
    head_dim = width // HEADS
    normed, inverse, inputs = norm_forward(grouped, gain_one)
    projected = jnp.dot(inputs.reshape(-1, width), w_qkv, preferred_element_type=jnp.float32).astype(jnp.bfloat16)
    projected = projected.reshape(group_count, members, 3, HEADS, head_dim)
    query = projected[:, :, 0]
    keys = projected[:, :, 1]
    values = projected[:, :, 2]
    scores = jnp.einsum('gqhd,gkhd->ghqk', query.astype(jnp.float32), keys.astype(jnp.float32)) * (1.0 / math.sqrt(head_dim))
    peak = lax.optimization_barrier(jnp.max(scores, axis=-1, keepdims=True))
    expos = jnp.exp(scores - peak)
    probs = (expos / lax.optimization_barrier(jnp.sum(expos, axis=-1, keepdims=True))).astype(jnp.bfloat16)
    mixed = jnp.einsum('ghqk,gkhd->gqhd', probs.astype(jnp.float32), values.astype(jnp.float32)).astype(jnp.bfloat16)
    return (mixed.reshape(group_count, members, width), (normed, inverse, inputs, query, keys, values, probs))

def block_tail(start_rows, mixed_rows, cot_rows, w_out, gain_two, w_up, w_down):
    resid = start_rows.astype(jnp.float32) + jnp.dot(mixed_rows, w_out, preferred_element_type=jnp.float32)
    normed, inverse, inputs = norm_forward(resid, gain_two)
    pre = jnp.dot(inputs, w_up, preferred_element_type=jnp.float32)
    tangent = jnp.tanh(gelu_coef * (pre + cubic_coef * pre * pre * pre))
    act = (0.5 * pre * (1.0 + tangent)).astype(jnp.bfloat16)
    down_grad = jnp.dot(act.T, cot_rows, preferred_element_type=jnp.float32)
    act_grad = jnp.dot(cot_rows, w_down.T, preferred_element_type=jnp.float32)
    slope = 0.5 * (1.0 + tangent) + 0.5 * pre * (1.0 - tangent * tangent) * gelu_coef * (1.0 + 3.0 * cubic_coef * pre * pre)
    pre_grad = (act_grad * slope).astype(jnp.bfloat16)
    up_grad = jnp.dot(inputs.T, pre_grad, preferred_element_type=jnp.float32)
    in_grad = jnp.dot(pre_grad, w_up.T, preferred_element_type=jnp.float32)
    normed_back, gain_two_grad = norm_backward(in_grad, normed, inverse, gain_two)
    resid_grad = cot_rows.astype(jnp.float32) + normed_back
    resid_low = resid_grad.astype(jnp.bfloat16)
    out_grad = jnp.dot(mixed_rows.T, resid_low, preferred_element_type=jnp.float32)
    mixed_grad = jnp.dot(resid_low, w_out.T, preferred_element_type=jnp.float32).astype(jnp.bfloat16)
    return (resid_grad, mixed_grad, (out_grad, up_grad, down_grad, gain_two_grad))

def attend_backward(mixed_grad, saved, w_qkv, gain_one):
    normed, inverse, inputs, query, keys, values, probs = saved
    group_count, members, width = mixed_grad.shape
    head_dim = width // HEADS
    upstream = mixed_grad.reshape(group_count, members, HEADS, head_dim).astype(jnp.float32)
    probs_wide = probs.astype(jnp.float32)
    prob_grad = jnp.einsum('gqhd,gkhd->ghqk', upstream, values.astype(jnp.float32))
    value_grad = jnp.einsum('ghqk,gqhd->gkhd', probs_wide, upstream)
    score_grad = (probs_wide * (prob_grad - lax.optimization_barrier(jnp.sum(probs_wide * prob_grad, axis=-1, keepdims=True))) * (1.0 / math.sqrt(head_dim))).astype(jnp.bfloat16)
    score_wide = score_grad.astype(jnp.float32)
    query_grad = jnp.einsum('ghqk,gkhd->gqhd', score_wide, keys.astype(jnp.float32))
    key_grad = jnp.einsum('ghqk,gqhd->gkhd', score_wide, query.astype(jnp.float32))
    proj_grad = jnp.stack([query_grad, key_grad, value_grad], axis=2).astype(jnp.bfloat16).reshape(group_count * members, 3 * width)
    qkv_grad = jnp.dot(inputs.reshape(-1, width).T, proj_grad, preferred_element_type=jnp.float32)
    in_grad = jnp.dot(proj_grad, w_qkv.T, preferred_element_type=jnp.float32).reshape(group_count, members, width)
    normed_back, gain_one_grad = norm_backward(in_grad, normed, inverse, gain_one)
    return (normed_back, (qkv_grad, gain_one_grad))

def to_groups(field):
    batch_count, height, width_map, width = field.shape
    shaped = field.reshape(batch_count, GRID, SPAN_H, GRID, SPAN_W, width).transpose(0, 2, 4, 1, 3, 5)
    return shaped.reshape(batch_count * SPAN_H * SPAN_W, GRID * GRID, width)

def from_groups(grouped):
    width = grouped.shape[-1]
    shaped = grouped.reshape(BATCH, SPAN_H, SPAN_W, GRID, GRID, width).transpose(0, 3, 1, 4, 2, 5)
    return shaped.reshape(BATCH, GRID * SPAN_H, GRID * SPAN_W, width)

def reference(input_map, dw_kernel, gain_one, w_qkv, w_out, gain_two, w_up, w_down, cotangent):
    padded = jnp.pad(input_map, ((0, 0), (1, 1), (1, 1), (0, 0)))
    mixed_in = lax.map(lambda sample_map: depthwise(sample_map, dw_kernel).astype(jnp.bfloat16), padded)
    grouped = to_groups(mixed_in)
    cot_groups = to_groups(cotangent)
    group_total = grouped.shape[0]
    block = math.gcd(group_total, 256)
    stacked_in = grouped.reshape(group_total // block, block, GRID * GRID, C)
    stacked_cot = cot_groups.reshape(group_total // block, block, GRID * GRID, C)
    initial = (jnp.zeros((C, 3 * C), jnp.float32), jnp.zeros((C,), jnp.float32), jnp.zeros((C, C), jnp.float32), jnp.zeros((C, FF), jnp.float32), jnp.zeros((FF, C), jnp.float32), jnp.zeros((C,), jnp.float32))

    def advance(carry, pieces):
        block_in, block_cot = pieces
        mixed, saved = attend_forward(block_in, w_qkv, gain_one)
        token_count = block_in.shape[0] * block_in.shape[1]
        resid_grad, mixed_grad, tail = block_tail(block_in.reshape(token_count, C), mixed.reshape(token_count, C), block_cot.reshape(token_count, C), w_out, gain_two, w_up, w_down)
        normed_back, head = attend_backward(mixed_grad.reshape(block_in.shape), saved, w_qkv, gain_one)
        grad_block = resid_grad.reshape(block_in.shape) + normed_back
        return (jax.tree.map(lambda total, extra: total + extra, carry, head + tail), grad_block)
    sums, grad_blocks = lax.scan(advance, initial, (stacked_in, stacked_cot))
    grad_in = from_groups(grad_blocks.reshape(group_total, GRID * GRID, C))
    grad_pad = jnp.pad(grad_in, ((0, 0), (1, 1), (1, 1), (0, 0)))
    input_grad, kernel_parts = lax.map(lambda both_maps: depthwise_back(both_maps[0], both_maps[1], dw_kernel), (grad_pad, padded))
    factor = 1.0 / math.sqrt(ALL_TOKENS)
    kernel_grad = lax.optimization_barrier(jnp.sum(kernel_parts, axis=0)) * factor
    qkv_grad, gain_one_grad, out_grad, up_grad, down_grad, gain_two_grad = sums
    return (input_grad, kernel_grad, gain_one_grad * factor, qkv_grad * factor, out_grad * factor, gain_two_grad * factor, up_grad * factor, down_grad * factor)
```

```python
import math

import jax
import jax.numpy as jnp
import numpy as np
from jax import lax
from jax.experimental import pallas as pl
from jax.experimental.pallas import tpu as pltpu
from jax.sharding import Mesh
from jax.sharding import PartitionSpec as P

HEADS = 8
C = 256
FF = 1024
PIECE = 56
norm_eps = 1e-05
gelu_coef = 0.7978845608028654
cubic_coef = 0.044715
HEAD_SCALE = 1.0 / math.sqrt(C // HEADS)
TOKENS = 1024

F32 = jnp.float32
BF16 = jnp.bfloat16


def tile_to_columns():
    out = np.zeros((256, 256), np.float32)
    for col in range(16):
        for row in range(16):
            out[col * 16 + row, row * 16 + col] = 1
    return out


def sources_to_groups():
    out = np.zeros((3, 128, 128), np.float32)
    for p in range(8):
        for a in range(2):
            for e in range(8):
                for variant, shift in enumerate((0, -1, 1)):
                    if 0 <= e + shift < 8:
                        out[variant, p * 16 + a * 8 + e, (e + shift) * 16 + a * 8 + p] = 1
    return out


def groups_to_pieces():
    out = np.zeros((3, 8 * PIECE, 384), np.float32)

    def source(j, row, e):
        if row == 0:
            return 256 + j * 8 + e
        if row == 17:
            return 272 + j * 8 + e
        a, p = divmod(row - 1, 8)
        return (j * 8 + p) * 16 + a * 8 + e

    for c in range(8):
        for row in range(18):
            for slot in range(2):
                out[0, c * PIECE + slot * 18 + row, source(slot, row, c)] = 1
            if c + 1 < 8:
                out[1, c * PIECE + 36 + row, source(0, row, c + 1)] = 1
            if c - 1 >= 0:
                out[2, c * PIECE + 36 + row, source(1, row, c - 1)] = 1
    return out


def pieces_to_tile():
    main = np.zeros((288, 8 * PIECE), np.float32)
    right = np.zeros((144, 8 * PIECE), np.float32)
    left = np.zeros((144, 8 * PIECE), np.float32)
    for row in range(18):
        for q in range(16):
            main[row * 16 + q, (q // 2) * PIECE + (q % 2) * 18 + row] = 1
        right[row * 8, 36 + row] = 1
        left[row * 8 + 7, 7 * PIECE + 36 + row] = 1
    return main, right, left


def head_tables():
    spread = np.zeros((512, 64), np.float32)
    mask = np.zeros((512, C), np.float32)
    for k in range(64):
        for h in range(HEADS):
            spread[k * 8 + h, k] = 1
            mask[k * 8 + h, h * 32 : (h + 1) * 32] = 1
    return spread, spread.T.copy(), mask


def dot(a, b):
    return lax.dot_general(a, b, (((1,), (0,)), ((), ())), preferred_element_type=F32)


def dot_nt(a, b):
    return lax.dot_general(a, b, (((1,), (1,)), ((), ())), preferred_element_type=F32)


def dot_tn(a, b):
    return lax.dot_general(a, b, (((0,), (0,)), ((), ())), preferred_element_type=F32)


def norm(values):
    center = values - jnp.mean(values, axis=-1, keepdims=True)
    inverse = lax.rsqrt(jnp.mean(center * center, axis=-1, keepdims=True) + norm_eps)
    return center * inverse, inverse


def norm_back(upstream, normed, inverse, gain):
    scaled = upstream * gain
    return inverse * (
        scaled
        - jnp.mean(scaled, axis=-1, keepdims=True)
        - normed * jnp.mean(scaled * normed, axis=-1, keepdims=True)
    )


def fold_rows(values):
    return jnp.sum(values.reshape(-1, 8, values.shape[-1]), axis=0)


def over_keys(values, combine):
    out = combine(
        combine(values[:, 0:128], values[:, 128:256]),
        combine(values[:, 256:384], values[:, 384:512]),
    )
    for shift in (64, 32, 16, 8):
        out = combine(out, pltpu.roll(out, shift, axis=1))
    return jnp.concatenate([out] * 4, axis=1)


def pack_kernel(halo, x_ref, perm_ref, out_ref):
    perm = perm_ref[...]
    for block in range(4):
        tokens = x_ref[:, 16 * block : 16 * block + 16, :].reshape(256, C)
        columns = dot(perm, tokens).astype(BF16).reshape(16, 16, C)
        for i in range(16):
            q = 16 * block + i
            k, odd = divmod(q, 2)
            if not halo:
                out_ref[k, odd] = columns[i]
            elif odd:
                out_ref[k, 2] = columns[i]
                out_ref[(k + 1) % 32, 0] = columns[i]
            else:
                out_ref[k, 1] = columns[i]
                out_ref[(k - 1) % 32, 3] = columns[i]


def forward_kernel(
    place_ref, x_ref, cot_ref, perm_ref, dw_ref, gain_one_ref, w_qkv_ref, w_out_ref, gain_two_ref,
    w_up_ref, w_down_ref, spread_ref, mask_ref,
    xs_ref, in_ref, proj_ref, probs_ref, mixed_grad_ref, resid_grad_ref, keep_ref, send_ref,
    out_grad_ref, gain_grad_ref,
    cot_s, mixed_s, two_s, low_s, act_s, pre_s, sums_s,
):
    owner = place_ref[0]
    core = place_ref[1]
    first = perm_ref[jnp.where(owner == 0, 1, 0)]
    last = perm_ref[jnp.where(owner == 31, 2, 0)]
    plain = perm_ref[0]

    for r in range(4):
        for j in range(4):
            perm = first if j == 0 else (last if j == 3 else plain)
            tokens = x_ref[8 * r : 8 * r + 8, j].reshape(128, C)
            moved = dot(perm, tokens).astype(BF16).reshape(8, 16, C)
            for p in range(8):
                xs_ref[j, p + 1, 16 * r : 16 * r + 16, :] = moved[p]
    edge = jnp.zeros((8, C), F32)
    for j in range(4):
        lowest = xs_ref[j, 8].astype(F32)
        xs_ref[j, 0] = jnp.concatenate([edge, lowest[:56]], axis=0).astype(BF16)
        highest = xs_ref[j, 1].astype(F32)
        xs_ref[j, 9] = jnp.concatenate([highest[8:], edge], axis=0).astype(BF16)

    gain_one = gain_one_ref[...]

    def conv(g, carry):
        j, p = g // 8, g % 8
        total = xs_ref[j + 1, p + 1].astype(F32)
        for u in range(3):
            for v in range(3):
                total = total + dw_ref[3 * u + v : 3 * u + v + 1, :] * xs_ref[j + v, p + u].astype(F32)
        start = total.astype(BF16)
        rows = pl.ds(pl.multiple_of(g * 64, 64), 64)
        in_ref[rows, :] = start
        normed, _ = norm(start.astype(F32))
        two_s[rows, :] = (normed * gain_one).astype(BF16)
        return carry

    lax.fori_loop(0, 16, conv, 0)

    def project(i, carry):
        rows = pl.ds(pl.multiple_of(i * 256, 256), 256)
        proj_ref[rows, :] = dot(two_s[rows, :], w_qkv_ref[...]).astype(BF16)
        return carry

    lax.fori_loop(0, 4, project, 0)

    spread = spread_ref[...]
    mask = mask_ref[...]

    def attend(g, carry):
        rows = pl.ds(pl.multiple_of(g * 64, 64), 64)
        query = proj_ref[rows, 0:256]
        keys = dot(spread, proj_ref[rows, 256:512]).astype(BF16) * mask
        values = dot(spread, proj_ref[rows, 512:768]).astype(BF16) * mask
        scores = dot_nt(query, keys) * HEAD_SCALE
        expos = jnp.exp(scores - over_keys(scores, jnp.maximum))
        probs = (expos / over_keys(expos, jnp.add)).astype(BF16)
        probs_ref[rows, :] = probs
        mixed_s[rows, :] = dot(probs, values).astype(BF16)
        return carry

    lax.fori_loop(0, 16, attend, 0)

    for r in range(4):
        for j in range(2):
            tokens = cot_ref[8 * r : 8 * r + 8, j].reshape(128, C)
            moved = dot(plain, tokens).astype(BF16).reshape(8, 16, C)
            for p in range(8):
                cot_s[(j * 8 + p) * 64 + 16 * r : (j * 8 + p) * 64 + 16 * r + 16, :] = moved[p]

    gain_two = gain_two_ref[...]

    def tail(i, gain_grad):
        rows = pl.ds(pl.multiple_of(i * 128, 128), 128)
        cot = cot_s[rows, :]
        resid = in_ref[rows, :].astype(F32) + dot(mixed_s[rows, :], w_out_ref[...])
        normed, inverse = norm(resid)
        inputs = (normed * gain_two).astype(BF16)
        two_s[rows, :] = inputs
        pre = dot(inputs, w_up_ref[...])
        square = pre * pre
        tangent = jnp.tanh(gelu_coef * (pre + cubic_coef * square * pre))
        half = 0.5 * (1.0 + tangent)
        act_s[rows, :] = (pre * half).astype(BF16)
        slope = half + 0.5 * pre * (1.0 - tangent * tangent) * gelu_coef * (
            1.0 + 3.0 * cubic_coef * square
        )
        pre_grad = (dot_nt(cot, w_down_ref[...]) * slope).astype(BF16)
        pre_s[rows, :] = pre_grad
        in_grad = dot_nt(pre_grad, w_up_ref[...])
        resid_grad = cot.astype(F32) + norm_back(in_grad, normed, inverse, gain_two)
        resid_grad_ref[rows, :] = resid_grad
        low = resid_grad.astype(BF16)
        low_s[rows, :] = low
        mixed_grad_ref[rows, :] = dot_nt(low, w_out_ref[...]).astype(BF16)
        return gain_grad + fold_rows(in_grad * normed)

    gain_grad = lax.fori_loop(0, 8, tail, jnp.zeros((8, C), F32))
    gain_grad_ref[...] = gain_grad

    cot_turned = cot_s[...].T
    two_turned = two_s[...].T
    for block in range(4):
        columns = slice(256 * block, 256 * block + 256)
        down = dot(cot_turned, act_s[:, columns])
        sums_s[256 * block : 256 * block + 256, :] = down.T.astype(BF16)
        up = dot(two_turned, pre_s[:, columns])
        sums_s[1024 + 256 * block : 1280 + 256 * block, :] = up.astype(BF16)
    keep_ref[...] = sums_s[pl.ds(pl.multiple_of(core * 1024, 1024), 1024), :]
    send_ref[...] = sums_s[pl.ds(pl.multiple_of((1 - core) * 1024, 1024), 1024), :]
    out_grad_ref[...] = dot(mixed_s[...].T, low_s[...])


def backward_kernel(
    place_ref, xs_ref, in_ref, proj_ref, probs_ref, mixed_grad_ref, resid_grad_ref, out_grad_ref,
    gain_two_grad_ref, gain_one_ref, w_qkv_ref, spread_ref, gather_ref, mask_ref, perm_ref,
    pieces_ref, keep_ref, send_ref,
    proj_grad_s, inputs_s, grad_s, sums_s,
):
    owner = place_ref[0]
    core = place_ref[1]
    spread = spread_ref[...]
    gather = gather_ref[...]
    mask = mask_ref[...]

    def attend_back(g, carry):
        rows = pl.ds(pl.multiple_of(g * 64, 64), 64)
        query = proj_ref[rows, 0:256]
        keys = dot(spread, proj_ref[rows, 256:512]).astype(BF16) * mask
        values = dot(spread, proj_ref[rows, 512:768]).astype(BF16) * mask
        probs = probs_ref[rows, :]
        upstream = mixed_grad_ref[rows, :]
        wide = probs.astype(F32)
        prob_grad = dot_nt(upstream, values)
        score_grad = (
            wide * (prob_grad - over_keys(wide * prob_grad, jnp.add)) * HEAD_SCALE
        ).astype(BF16)
        proj_grad_s[rows, 0:256] = dot(score_grad, keys).astype(BF16)
        key_terms = dot_tn(score_grad, query).astype(BF16) * mask
        value_terms = dot_tn(probs, upstream).astype(BF16) * mask
        proj_grad_s[rows, 256:512] = dot(gather, key_terms).astype(BF16)
        proj_grad_s[rows, 512:768] = dot(gather, value_terms).astype(BF16)
        return carry

    lax.fori_loop(0, 16, attend_back, 0)

    gain_one = gain_one_ref[...]

    def head(i, gain_grad):
        rows = pl.ds(pl.multiple_of(i * 128, 128), 128)
        normed, inverse = norm(in_ref[rows, :].astype(F32))
        inputs_s[rows, :] = (normed * gain_one).astype(BF16)
        in_grad = dot_nt(proj_grad_s[rows, :], w_qkv_ref[...])
        grad_s[rows, :] = resid_grad_ref[rows, :] + norm_back(in_grad, normed, inverse, gain_one)
        return gain_grad + fold_rows(in_grad * normed)

    gain_grad = lax.fori_loop(0, 8, head, jnp.zeros((8, C), F32))

    which = jnp.where(owner == 0, 1.0, 0.0).astype(BF16)
    other = jnp.where(owner == 31, 1.0, 0.0).astype(BF16)
    perm = perm_ref[0] + perm_ref[1] * which + perm_ref[2] * other
    edge = jnp.zeros((8, C), F32)
    for r in range(4):
        parts = [grad_s[64 * g + 16 * r : 64 * g + 16 * r + 16, :] for g in range(16)]
        for j in range(2):
            lowest = 64 * (8 * j + 7) + 16 * r - 8
            parts.append(grad_s[lowest : lowest + 8, :] if r > 0 else edge)
        for j in range(2):
            highest = 64 * 8 * j + 16 * r + 16
            parts.append(grad_s[highest : highest + 8, :] if r < 3 else edge)
        parts.append(jnp.zeros((96, C), F32))
        tokens = jnp.concatenate(parts, axis=0).astype(BF16)
        pieces_ref[r] = dot(perm, tokens).astype(BF16)

    def taps(g, sums):
        j, p = g // 8, g % 8
        grad = grad_s[pl.ds(pl.multiple_of(g * 64, 64), 64), :]
        return tuple(
            sums[3 * u + v] + fold_rows(grad * xs_ref[j + v, p + u].astype(F32))
            for u in range(3)
            for v in range(3)
        )

    kernel_grad = lax.fori_loop(0, 16, taps, (jnp.zeros((8, C), F32),) * 9)

    inputs_turned = inputs_s[...].T
    for block in range(3):
        columns = slice(256 * block, 256 * block + 256)
        terms = dot(inputs_turned, proj_grad_s[:, columns]).astype(BF16)
        sums_s[256 * block : 256 * block + 256, 0:256] = terms
    sums_s[768:1024, 0:256] = out_grad_ref[...].astype(BF16)
    small = [jnp.sum(term, axis=0, keepdims=True) for term in kernel_grad]
    small.append(jnp.sum(gain_grad, axis=0, keepdims=True))
    small.append(jnp.sum(gain_two_grad_ref[...], axis=0, keepdims=True))
    small.append(jnp.zeros((5, C), F32))
    small = jnp.concatenate(small, axis=0).astype(BF16)
    sums_s[:, 256:384] = jnp.zeros((1024, 128), BF16)
    sums_s[0:16, 256:384] = small[:, 0:128]
    sums_s[16:32, 256:384] = small[:, 128:256]
    keep_ref[...] = sums_s[pl.ds(pl.multiple_of(core * 512, 512), 512), :]
    send_ref[...] = sums_s[pl.ds(pl.multiple_of((1 - core) * 512, 512), 512), :]


def total_kernel(factor, x_ref, out_ref):
    total = jnp.sum(x_ref[...].astype(F32), axis=0) * factor
    out_ref[...] = jnp.broadcast_to(total.astype(BF16)[None], out_ref.shape)


def tile_kernel(pieces_ref, main_ref, right_ref, left_ref, dw_ref, out_ref, wide):
    for block in range(4):
        columns = dot(main_ref[...], pieces_ref[block])
        wide[:, 8 + 16 * block : 24 + 16 * block, :] = columns.reshape(18, 16, C)
    wide[:, 72:80, :] = dot(right_ref[...], pieces_ref[0]).reshape(18, 8, C)
    wide[:, 0:8, :] = dot(left_ref[...], pieces_ref[3]).reshape(18, 8, C)

    def row(i, carry):
        rows = [wide[i + 2 - u] for u in range(3)]
        total = wide[i + 1, 8:72, :]
        for v in range(3):
            term = dw_ref[v : v + 1, :] * rows[0]
            for u in range(1, 3):
                term = term + dw_ref[3 * u + v : 3 * u + v + 1, :] * rows[u]
            total = total + term[9 - v : 73 - v, :]
        out_ref[0, i] = total
        return carry

    lax.fori_loop(0, 16, row, 0)


def outputs_kernel(
    place_ref, t_mine_ref, t_other_ref, q_mine_ref, q_other_ref,
    kernel_ref, gain_one_ref, qkv_ref, out_ref, gain_two_ref, up_ref, down_ref, halves,
):
    core = place_ref[1]

    def lower(mine, other):
        return jnp.where(core == 0, mine.astype(F32), other.astype(F32))

    def upper(mine, other):
        return jnp.where(core == 0, other.astype(F32), mine.astype(F32))

    down_ref[...] = lower(t_mine_ref[...], t_other_ref[...])
    for block in range(4):
        rows = slice(256 * block, 256 * block + 256)
        up_ref[:, rows] = upper(t_mine_ref[rows, :], t_other_ref[rows, :])
    qkv_ref[:, 0:256] = lower(q_mine_ref[0:256, 0:256], q_other_ref[0:256, 0:256])
    qkv_ref[:, 256:512] = lower(q_mine_ref[256:512, 0:256], q_other_ref[256:512, 0:256])
    qkv_ref[:, 512:768] = upper(q_mine_ref[0:256, 0:256], q_other_ref[0:256, 0:256])
    out_ref[...] = upper(q_mine_ref[256:512, 0:256], q_other_ref[256:512, 0:256])
    small = lower(q_mine_ref[0:32, 256:384], q_other_ref[0:32, 256:384])
    small = jnp.concatenate([small[0:16], small[16:32]], axis=1)
    kernel_ref[...] = small[0:9]
    gain_one_ref[...] = small[9:10]
    gain_two_ref[...] = small[10:11]


VMEM = pl.BlockSpec(memory_space=pltpu.VMEM)
SMEM = pl.BlockSpec(memory_space=pltpu.SMEM)


def call(kernel, outs, operands, scratch=(), scalars=0, flops=0, moved=0, limit=48):
    return pl.pallas_call(
        kernel,
        out_shape=tuple(jax.ShapeDtypeStruct(shape, dtype) for shape, dtype in outs),
        in_specs=[SMEM] * scalars + [VMEM] * (len(operands) - scalars),
        out_specs=tuple(VMEM for _ in outs),
        scratch_shapes=[pltpu.VMEM(shape, dtype) for shape, dtype in scratch],
        compiler_params=pltpu.CompilerParams(vmem_limit_bytes=limit * 2**20),
        cost_estimate=pl.CostEstimate(flops=flops, bytes_accessed=moved, transcendentals=0),
    )(*operands)


def local(input_map, dw_kernel, gain_one, w_qkv, w_out, gain_two, w_up, w_down, cotangent):
    tokens_axes = ("row", "col")
    sums_axes = ("yh", "row", "col")
    owner = lax.axis_index("row") * 8 + lax.axis_index("col")
    core = lax.axis_index("core")
    place = jnp.stack([owner, core]).astype(jnp.int32)
    dw_rows = dw_kernel.reshape(9, C).astype(F32)
    spread, gather, mask = (jnp.asarray(t, BF16) for t in head_tables())

    def exchange(stacked, axes):
        return lax.all_to_all(stacked, axes, split_axis=0, concat_axis=0, tiled=True)

    def swap(half):
        return lax.ppermute(half, "core", [(0, 1), (1, 0)])

    to_columns = jnp.asarray(tile_to_columns(), BF16)
    (packed,) = call(
        lambda *refs: pack_kernel(True, *refs),
        [((32, 4, 16, C), BF16)],
        [input_map[0], to_columns],
        flops=2 * 10**8,
        moved=2 * 10**6,
    )
    arrived = exchange(packed, tokens_axes)
    (packed_cot,) = call(
        lambda *refs: pack_kernel(False, *refs),
        [((32, 2, 16, C), BF16)],
        [cotangent[0], to_columns],
        flops=2 * 10**8,
        moved=2 * 10**6,
    )
    arrived_cot = exchange(packed_cot, tokens_axes)

    (
        xs, start, projected, probs, mixed_grad, resid_grad, t_keep, t_send, out_grad, gain_two_grad,
    ) = call(
        forward_kernel,
        [
            ((4, 10, 64, C), BF16),
            ((TOKENS, C), BF16),
            ((TOKENS, 3 * C), BF16),
            ((TOKENS, 512), BF16),
            ((TOKENS, C), BF16),
            ((TOKENS, C), F32),
            ((1024, C), BF16),
            ((1024, C), BF16),
            ((C, C), F32),
            ((8, C), F32),
        ],
        [
            place, arrived, arrived_cot, jnp.asarray(sources_to_groups(), BF16), dw_rows,
            gain_one.reshape(1, C), w_qkv, w_out, gain_two.reshape(1, C), w_up, w_down, spread, mask,
        ],
        [
            ((TOKENS, C), BF16),
            ((TOKENS, C), BF16),
            ((TOKENS, C), BF16),
            ((TOKENS, C), BF16),
            ((TOKENS, FF), BF16),
            ((TOKENS, FF), BF16),
            ((2048, C), BF16),
        ],
        scalars=1,
        flops=8 * 10**9,
        moved=12 * 10**6,
    )

    factor = 1.0 / math.sqrt(TOKENS * 128)

    def reduce_and_share(keep, send, rows, lanes):
        half = (keep.astype(F32) + swap(send).astype(F32)).astype(BF16)
        gathered = exchange(half.reshape(64, rows, lanes), sums_axes)
        (shared,) = call(
            lambda x_ref, out_ref: total_kernel(factor, x_ref, out_ref),
            [((64, rows, lanes), BF16)],
            [gathered],
            flops=10**6,
            moved=10**6,
        )
        mine = exchange(shared, sums_axes).reshape(64 * rows, lanes)
        return mine, swap(mine)

    t_mine, t_other = reduce_and_share(t_keep, t_send, 16, C)

    pieces, q_keep, q_send = call(
        backward_kernel,
        [((4, 8 * PIECE, C), BF16), ((512, 384), BF16), ((512, 384), BF16)],
        [
            place, xs, start, projected, probs, mixed_grad, resid_grad, out_grad, gain_two_grad,
            gain_one.reshape(1, C), w_qkv, spread, gather, mask, jnp.asarray(groups_to_pieces(), BF16),
        ],
        [
            ((TOKENS, 3 * C), BF16),
            ((TOKENS, C), BF16),
            ((TOKENS, C), F32),
            ((1024, 384), BF16),
        ],
        scalars=1,
        flops=5 * 10**9,
        moved=8 * 10**6,
    )
    q_mine, q_other = reduce_and_share(q_keep, q_send, 8, 384)

    back = exchange(pieces.reshape(32, PIECE, C), tokens_axes).reshape(4, 8 * PIECE, C)
    main, right, left = (jnp.asarray(t, BF16) for t in pieces_to_tile())
    (input_grad,) = call(
        tile_kernel,
        [((1, 16, 64, C), F32)],
        [back, main, right, left, dw_rows],
        [((18, 80, C), F32)],
        flops=10**9,
        moved=2 * 10**6,
    )
    kernel_grad, gain_one_grad, qkv_grad, out_sum, gain_two_sum, up_grad, down_grad = call(
        lambda *refs: outputs_kernel(*refs, None),
        [
            ((9, C), F32),
            ((1, C), F32),
            ((C, 3 * C), F32),
            ((C, C), F32),
            ((1, C), F32),
            ((C, FF), F32),
            ((FF, C), F32),
        ],
        [place, t_mine, t_other, q_mine, q_other],
        scalars=1,
        flops=10**6,
        moved=5 * 10**6,
    )
    return (
        input_grad,
        kernel_grad.reshape(3, 3, C),
        gain_one_grad.reshape(C),
        qkv_grad,
        out_sum,
        gain_two_sum.reshape(C),
        up_grad,
        down_grad,
    )


def solution(mesh):
    cores = Mesh(mesh.devices.reshape(2, 2, 4, 8), ("yh", "core", "row", "col"))
    split = P(("yh", "core"), "row", "col", None)
    in_specs = (split, P(), P(), P(), P(), P(), P(), P(), split)
    out_specs = (split, P(), P(), P(), P(), P(), P(), P())
    return jax.shard_map(local, mesh=cores, in_specs=in_specs, out_specs=out_specs, check_vma=False)
```

```python
import math

import jax
import jax.numpy as jnp
import numpy as np
from jax import lax
from jax.experimental import pallas as pl
from jax.experimental.pallas import tpu as pltpu
from jax.sharding import Mesh
from jax.sharding import PartitionSpec as P

HEADS = 8
C = 256
FF = 1024
PIECE = 56
norm_eps = 1e-05
gelu_coef = 0.7978845608028654
cubic_coef = 0.044715
HEAD_SCALE = 1.0 / math.sqrt(C // HEADS)
TOKENS = 1024
AHEAD = 4

F32 = jnp.float32
BF16 = jnp.bfloat16


def tile_to_columns():
    out = np.zeros((256, 256), np.float32)
    for col in range(16):
        for row in range(16):
            out[col * 16 + row, row * 16 + col] = 1
    return out


def sources_to_groups():
    out = np.zeros((3, 128, 128), np.float32)
    for p in range(8):
        for a in range(2):
            for e in range(8):
                for variant, shift in enumerate((0, -1, 1)):
                    if 0 <= e + shift < 8:
                        out[variant, p * 16 + a * 8 + e, (e + shift) * 16 + a * 8 + p] = 1
    return out


def groups_to_pieces():
    out = np.zeros((3, 8 * PIECE, 384), np.float32)

    def source(j, row, e):
        if row == 0:
            return 256 + j * 8 + e
        if row == 17:
            return 272 + j * 8 + e
        a, p = divmod(row - 1, 8)
        return (j * 8 + p) * 16 + a * 8 + e

    for c in range(8):
        for row in range(18):
            for slot in range(2):
                out[0, c * PIECE + slot * 18 + row, source(slot, row, c)] = 1
            if c + 1 < 8:
                out[1, c * PIECE + 36 + row, source(0, row, c + 1)] = 1
            if c - 1 >= 0:
                out[2, c * PIECE + 36 + row, source(1, row, c - 1)] = 1
    return out


def pieces_to_tile():
    main = np.zeros((288, 8 * PIECE), np.float32)
    right = np.zeros((144, 8 * PIECE), np.float32)
    left = np.zeros((144, 8 * PIECE), np.float32)
    for row in range(18):
        for q in range(16):
            main[row * 16 + q, (q // 2) * PIECE + (q % 2) * 18 + row] = 1
        right[row * 8, 36 + row] = 1
        left[row * 8 + 7, 7 * PIECE + 36 + row] = 1
    return main, right, left


def head_mask():
    mask = np.zeros((256, 128), np.float32)
    for h in range(4):
        mask[h * 64 : (h + 1) * 64, h * 32 : (h + 1) * 32] = 1
    return np.concatenate([mask, mask], axis=1)


def dot(a, b):
    return lax.dot_general(a, b, (((1,), (0,)), ((), ())), preferred_element_type=F32)


def dot_nt(a, b):
    return lax.dot_general(a, b, (((1,), (1,)), ((), ())), preferred_element_type=F32)


def dot_tn(a, b):
    return lax.dot_general(a, b, (((0,), (0,)), ((), ())), preferred_element_type=F32)


def norm(values):
    center = values - jnp.mean(values, axis=-1, keepdims=True)
    inverse = lax.rsqrt(jnp.mean(center * center, axis=-1, keepdims=True) + norm_eps)
    return center * inverse, inverse


def norm_back(upstream, normed, inverse, gain):
    scaled = upstream * gain
    return inverse * (
        scaled
        - jnp.mean(scaled, axis=-1, keepdims=True)
        - normed * jnp.mean(scaled * normed, axis=-1, keepdims=True)
    )


def fold_rows(values):
    return jnp.sum(values.reshape(-1, 8, values.shape[-1]), axis=0)


def side_by_side(rows):
    return jnp.concatenate([rows[0:64], rows[64:128]], axis=1)


def stacked(rows):
    return jnp.concatenate([rows[:, 0:128], rows[:, 128:256]], axis=0)


def block_diagonal(rows):
    zeros = jnp.zeros((64, 128), rows.dtype)
    upper = jnp.concatenate([rows[0:64], zeros], axis=1)
    return jnp.concatenate([upper, jnp.concatenate([zeros, rows[64:128]], axis=1)], axis=0)


def diagonal(blocks):
    return jnp.concatenate([blocks[0:64, 0:128], blocks[64:128, 128:256]], axis=0)


def by_head(rows, mask):
    return jnp.concatenate([side_by_side(rows)] * 4, axis=0) * mask


def attend_unit(query, key, value, mask):
    scores = dot_nt(by_head(key, mask), block_diagonal(query)).reshape(4, 64, 128) * HEAD_SCALE
    expos = jnp.exp(scores - jnp.max(scores, axis=1, keepdims=True))
    probs = expos * (1.0 / jnp.sum(expos, axis=1, keepdims=True))
    probs = probs.reshape(256, 128).astype(BF16)
    return probs, diagonal(dot_tn(probs, by_head(value, mask))).astype(BF16)


def attend_unit_back(query, key, value, probs, upstream, mask, wide_mask):
    wide = probs.astype(F32).reshape(4, 64, 128)
    upstream = block_diagonal(upstream)
    prob_grad = dot_nt(by_head(value, mask), upstream).reshape(4, 64, 128)
    centre = jnp.sum(wide * prob_grad, axis=1, keepdims=True)
    score_grad = (wide * (prob_grad - centre) * HEAD_SCALE).reshape(256, 128).astype(BF16)
    query_grad = diagonal(dot_tn(score_grad, by_head(key, mask)))
    key_grad = jnp.sum((dot(score_grad, block_diagonal(query)) * wide_mask).reshape(4, 64, 256), axis=0)
    value_grad = jnp.sum((dot(probs, upstream) * wide_mask).reshape(4, 64, 256), axis=0)
    return query_grad.astype(BF16), stacked(key_grad).astype(BF16), stacked(value_grad).astype(BF16)


def pack_kernel(x_ref, cot_ref, perm_ref, out_ref):
    perm = perm_ref[...]
    for block in range(4):
        tokens = x_ref[:, 16 * block : 16 * block + 16, :].reshape(256, C)
        columns = dot(perm, tokens).astype(BF16).reshape(16, 16, C)
        tokens = cot_ref[:, 16 * block : 16 * block + 16, :].reshape(256, C)
        cot_columns = dot(perm, tokens).astype(BF16).reshape(16, 16, C)
        for i in range(16):
            q = 16 * block + i
            k, odd = divmod(q, 2)
            out_ref[k, 4 + odd] = cot_columns[i]
            if odd:
                out_ref[k, 2] = columns[i]
                out_ref[(k + 1) % 32, 0] = columns[i]
            else:
                out_ref[k, 1] = columns[i]
                out_ref[(k - 1) % 32, 3] = columns[i]


def forward_kernel(
    place_ref, x_ref, perm_ref, dw_ref, gain_one_ref, w_qkv_ref, w_out_ref, gain_two_ref,
    w_up_ref, w_down_ref, mask_ref,
    xs_ref, in_ref, proj_ref, probs_ref, mixed_grad_ref, resid_grad_ref, sums_ref,
    out_grad_ref, gain_grad_ref,
    cot_s, mixed_s, two_s, low_s, act_s, pre_s,
):
    owner = place_ref[0]
    first = perm_ref[jnp.where(owner == 0, 1, 0)]
    last = perm_ref[jnp.where(owner == 31, 2, 0)]
    plain = perm_ref[0]

    for r in range(4):
        for j in range(4):
            perm = first if j == 0 else (last if j == 3 else plain)
            tokens = x_ref[8 * r : 8 * r + 8, j].reshape(128, C)
            moved = dot(perm, tokens).astype(BF16).reshape(8, 16, C)
            for p in range(8):
                xs_ref[j, p + 1, 16 * r : 16 * r + 16, :] = moved[p]
    edge = jnp.zeros((8, C), F32)
    for j in range(4):
        lowest = xs_ref[j, 8].astype(F32)
        xs_ref[j, 0] = jnp.concatenate([edge, lowest[:56]], axis=0).astype(BF16)
        highest = xs_ref[j, 1].astype(F32)
        xs_ref[j, 9] = jnp.concatenate([highest[8:], edge], axis=0).astype(BF16)

    gain_one = gain_one_ref[...]

    def conv(g, carry):
        j, p = g // 8, g % 8
        total = xs_ref[j + 1, p + 1].astype(F32)
        for u in range(3):
            for v in range(3):
                total = total + dw_ref[3 * u + v : 3 * u + v + 1, :] * xs_ref[j + v, p + u].astype(F32)
        start = total.astype(BF16)
        rows = pl.ds(pl.multiple_of(g * 64, 64), 64)
        in_ref[rows, :] = start
        normed, _ = norm(start.astype(F32))
        two_s[rows, :] = (normed * gain_one).astype(BF16)
        return carry

    lax.fori_loop(0, 16, conv, 0, unroll=16)

    def project(i, carry):
        rows = pl.ds(pl.multiple_of(i * 256, 256), 256)
        proj_ref[rows, :] = dot(two_s[rows, :], w_qkv_ref[...]).astype(BF16)
        return carry

    lax.fori_loop(0, 4, project, 0)

    mask = mask_ref[...]

    def attend(i, carry):
        units = []
        for n in range(AHEAD):
            pair = i * AHEAD + n
            rows = pl.ds(pl.multiple_of(pair * 128, 128), 128)
            for side in range(2):
                parts = [proj_ref[rows, 256 * m + 128 * side : 256 * m + 128 * side + 128] for m in range(3)]
                units.append((pair, rows, side, parts))
        results = [attend_unit(*parts, mask) for _, _, _, parts in units]
        for (pair, rows, side, _), (probs, mixed) in zip(units, results):
            probs_ref[2 * pair + side] = probs
            mixed_s[rows, 128 * side : 128 * side + 128] = mixed
        return carry

    lax.fori_loop(0, 8 // AHEAD, attend, 0)

    for r in range(4):
        for j in range(2):
            tokens = x_ref[8 * r : 8 * r + 8, 4 + j].reshape(128, C)
            moved = dot(plain, tokens).astype(BF16).reshape(8, 16, C)
            for p in range(8):
                cot_s[(j * 8 + p) * 64 + 16 * r : (j * 8 + p) * 64 + 16 * r + 16, :] = moved[p]

    gain_two = gain_two_ref[...]

    def tail(i, gain_grad):
        rows = pl.ds(pl.multiple_of(i * 512, 512), 512)
        cot = cot_s[rows, :]
        resid = in_ref[rows, :].astype(F32) + dot(mixed_s[rows, :], w_out_ref[...])
        normed, inverse = norm(resid)
        inputs = (normed * gain_two).astype(BF16)
        two_s[rows, :] = inputs
        pre = dot(inputs, w_up_ref[...])
        square = pre * pre
        tangent = jnp.tanh(gelu_coef * (pre + cubic_coef * square * pre))
        half = 0.5 * (1.0 + tangent)
        act_s[rows, :] = (pre * half).astype(BF16)
        slope = half + 0.5 * pre * (1.0 - tangent * tangent) * gelu_coef * (
            1.0 + 3.0 * cubic_coef * square
        )
        pre_grad = (dot_nt(cot, w_down_ref[...]) * slope).astype(BF16)
        pre_s[rows, :] = pre_grad
        in_grad = dot_nt(pre_grad, w_up_ref[...])
        resid_grad = cot.astype(F32) + norm_back(in_grad, normed, inverse, gain_two)
        resid_grad_ref[rows, :] = resid_grad
        low = resid_grad.astype(BF16)
        low_s[rows, :] = low
        mixed_grad_ref[rows, :] = dot_nt(low, w_out_ref[...]).astype(BF16)
        return gain_grad + fold_rows(in_grad * normed)

    gain_grad = lax.fori_loop(0, 2, tail, jnp.zeros((8, C), F32))
    gain_grad_ref[...] = gain_grad

    cot_turned = cot_s[...].T
    two_turned = two_s[...].T
    for block in range(4):
        columns = slice(256 * block, 256 * block + 256)
        down = dot(cot_turned, act_s[:, columns]).T.astype(BF16)
        up = dot(two_turned, pre_s[:, columns]).astype(BF16)
        for half in range(2):
            first = 2048 * half + 256 * block
            sums_ref[first : first + 256, :] = down[:, 128 * half : 128 * half + 128]
            sums_ref[first + 1024 : first + 1280, :] = up[:, 128 * half : 128 * half + 128]
    out_grad_ref[...] = dot(mixed_s[...].T, low_s[...])


def backward_kernel(
    place_ref, in_ref, proj_ref, probs_ref, mixed_grad_ref, resid_grad_ref, gain_one_ref, w_qkv_ref,
    mask_ref, perm_ref,
    pieces_ref, proj_grad_ref, inputs_ref, grad_ref, gain_grad_ref,
):
    owner = place_ref[0]
    mask = mask_ref[...]
    wide_mask = mask.astype(F32)

    def attend_back(i, carry):
        units = []
        for n in range(AHEAD):
            pair = i * AHEAD + n
            rows = pl.ds(pl.multiple_of(pair * 128, 128), 128)
            for side in range(2):
                lanes = slice(128 * side, 128 * side + 128)
                parts = [proj_ref[rows, 256 * m + 128 * side : 256 * m + 128 * side + 128] for m in range(3)]
                parts += [probs_ref[2 * pair + side], mixed_grad_ref[rows, lanes]]
                units.append((pair, rows, side, parts))
        results = [attend_unit_back(*parts, mask, wide_mask) for _, _, _, parts in units]
        for (_, rows, side, _), grads in zip(units, results):
            for m in range(3):
                proj_grad_ref[rows, 256 * m + 128 * side : 256 * m + 128 * side + 128] = grads[m]
        return carry

    lax.fori_loop(0, 8 // AHEAD, attend_back, 0)

    gain_one = gain_one_ref[...]

    def head(i, gain_grad):
        rows = pl.ds(pl.multiple_of(i * 512, 512), 512)
        normed, inverse = norm(in_ref[rows, :].astype(F32))
        inputs_ref[rows, :] = (normed * gain_one).astype(BF16)
        in_grad = dot_nt(proj_grad_ref[rows, :], w_qkv_ref[...])
        grad_ref[rows, :] = resid_grad_ref[rows, :] + norm_back(in_grad, normed, inverse, gain_one)
        return gain_grad + fold_rows(in_grad * normed)

    gain_grad_ref[...] = lax.fori_loop(0, 2, head, jnp.zeros((8, C), F32), unroll=2)

    which = jnp.where(owner == 0, 1.0, 0.0).astype(BF16)
    other = jnp.where(owner == 31, 1.0, 0.0).astype(BF16)
    perm = perm_ref[0] + perm_ref[1] * which + perm_ref[2] * other
    edge = jnp.zeros((8, C), F32)
    for r in range(4):
        parts = [grad_ref[64 * g + 16 * r : 64 * g + 16 * r + 16, :] for g in range(16)]
        for j in range(2):
            lowest = 64 * (8 * j + 7) + 16 * r - 8
            parts.append(grad_ref[lowest : lowest + 8, :] if r > 0 else edge)
        for j in range(2):
            highest = 64 * 8 * j + 16 * r + 16
            parts.append(grad_ref[highest : highest + 8, :] if r < 3 else edge)
        parts.append(jnp.zeros((96, C), F32))
        tokens = jnp.concatenate(parts, axis=0).astype(BF16)
        pieces_ref[r] = dot(perm, tokens).astype(BF16)


def sums_kernel(
    place_ref, xs_ref, inputs_ref, proj_grad_ref, grad_ref, gain_one_grad_ref, gain_two_grad_ref,
    out_grad_ref, tail_ref,
    keep_ref, send_ref,
    head_s, small_s,
):
    core = place_ref[1]

    def taps(g, sums):
        j, p = g // 8, g % 8
        grad = grad_ref[pl.ds(pl.multiple_of(g * 64, 64), 64), :]
        return tuple(
            sums[3 * u + v] + fold_rows(grad * xs_ref[j + v, p + u].astype(F32))
            for u in range(3)
            for v in range(3)
        )

    kernel_grad = lax.fori_loop(0, 16, taps, (jnp.zeros((8, C), F32),) * 9, unroll=4)

    inputs_turned = inputs_ref[...].T
    for block in range(4):
        if block < 3:
            terms = dot(inputs_turned, proj_grad_ref[:, 256 * block : 256 * block + 256])
        else:
            terms = out_grad_ref[...]
        for half in range(2):
            first = 1024 * half + 256 * block
            head_s[first : first + 256, :] = terms[:, 128 * half : 128 * half + 128].astype(BF16)
    small = [jnp.sum(term, axis=0, keepdims=True) for term in kernel_grad]
    small.append(jnp.sum(gain_one_grad_ref[...], axis=0, keepdims=True))
    small.append(jnp.sum(gain_two_grad_ref[...], axis=0, keepdims=True))
    small.append(jnp.zeros((5, C), F32))
    small = jnp.concatenate(small, axis=0)
    for half in range(2):
        small_s[16 * half : 16 * half + 16, :] = small[:, 128 * half : 128 * half + 128]
    zeros = jnp.zeros((8, 128), F32)
    for ref, half in ((keep_ref, core), (send_ref, 1 - core)):
        for k in range(64):
            parts = [
                tail_ref[pl.ds(pl.multiple_of(half * 2048 + 32 * k, 32), 32), :].astype(F32),
                head_s[pl.ds(pl.multiple_of(half * 1024 + 16 * k, 16), 16), :].astype(F32),
                small_s[pl.ds(pl.multiple_of(half * 16 + 8 * k, 8), 8), :] if k < 2 else zeros,
            ]
            ref[k] = jnp.concatenate(parts, axis=0).astype(BF16)


def total_kernel(factor, x_ref, out_ref):
    total = jnp.sum(x_ref[...].astype(F32), axis=0) * factor
    out_ref[...] = jnp.broadcast_to(total.astype(BF16)[None], out_ref.shape)


def tile_kernel(pieces_ref, main_ref, right_ref, left_ref, dw_ref, out_ref, wide):
    for block in range(4):
        columns = dot(main_ref[...], pieces_ref[block])
        wide[:, 8 + 16 * block : 24 + 16 * block, :] = columns.reshape(18, 16, C)
    wide[:, 72:80, :] = dot(right_ref[...], pieces_ref[0]).reshape(18, 8, C)
    wide[:, 0:8, :] = dot(left_ref[...], pieces_ref[3]).reshape(18, 8, C)

    def row(i, carry):
        rows = [wide[i + 2 - u] for u in range(3)]
        total = wide[i + 1, 8:72, :]
        for v in range(3):
            term = dw_ref[v : v + 1, :] * rows[0]
            for u in range(1, 3):
                term = term + dw_ref[3 * u + v : 3 * u + v + 1, :] * rows[u]
            total = total + term[9 - v : 73 - v, :]
        out_ref[0, i] = total
        return carry

    lax.fori_loop(0, 16, row, 0)


def outputs_kernel(
    place_ref, mine_ref, other_ref,
    kernel_ref, gain_one_ref, qkv_ref, out_ref, gain_two_ref, up_ref, down_ref,
):
    own = place_ref[1] == 0
    mine = mine_ref[...].astype(F32)
    other = other_ref[...].astype(F32)
    for half in range(2):
        lanes = slice(128 * half, 128 * half + 128)
        values = jnp.where(own, other, mine) if half else jnp.where(own, mine, other)
        tail = values[:, 0:32].reshape(2048, 128)
        head = values[:, 32:48].reshape(1024, 128)
        small = values[0:2, 48:56].reshape(16, 128)
        down_ref[:, lanes] = tail[0:1024]
        for block in range(4):
            first = 256 * block + 128 * half
            up_ref[:, first : first + 128] = tail[1024 + 256 * block : 1280 + 256 * block]
        for block in range(3):
            first = 256 * block + 128 * half
            qkv_ref[:, first : first + 128] = head[256 * block : 256 * block + 256]
        out_ref[:, lanes] = head[768:1024]
        for u in range(3):
            kernel_ref[u, :, lanes] = small[3 * u : 3 * u + 3]
        gain_one_ref[:, lanes] = small[9:10]
        gain_two_ref[:, lanes] = small[10:11]


VMEM = pl.BlockSpec(memory_space=pltpu.VMEM)
SMEM = pl.BlockSpec(memory_space=pltpu.SMEM)


def call(kernel, outs, operands, scratch=(), scalars=0, flops=0, moved=0, limit=24):
    return pl.pallas_call(
        kernel,
        out_shape=tuple(jax.ShapeDtypeStruct(shape, dtype) for shape, dtype in outs),
        in_specs=[SMEM] * scalars + [VMEM] * (len(operands) - scalars),
        out_specs=tuple(VMEM for _ in outs),
        scratch_shapes=[pltpu.VMEM(shape, dtype) for shape, dtype in scratch],
        compiler_params=pltpu.CompilerParams(vmem_limit_bytes=limit * 2**20),
        cost_estimate=pl.CostEstimate(flops=flops, bytes_accessed=moved, transcendentals=0),
    )(*operands)


def local(input_map, dw_kernel, gain_one, w_qkv, w_out, gain_two, w_up, w_down, cotangent):
    tokens_axes = ("row", "col")
    sums_axes = ("yh", "row", "col")
    owner = lax.axis_index("row") * 8 + lax.axis_index("col")
    core = lax.axis_index("core")
    place = jnp.stack([owner, core]).astype(jnp.int32)
    dw_rows = dw_kernel.reshape(9, C).astype(F32)
    mask = jnp.asarray(head_mask(), BF16)

    def exchange(stacked, axes):
        return lax.all_to_all(stacked, axes, split_axis=0, concat_axis=0, tiled=True)

    def swap(half):
        return lax.ppermute(half, "core", [(0, 1), (1, 0)])

    (packed,) = call(
        pack_kernel,
        [((32, 6, 16, C), BF16)],
        [input_map[0], cotangent[0], jnp.asarray(tile_to_columns(), BF16)],
        flops=4 * 10**8,
        moved=4 * 10**6,
        limit=60,
    )
    arrived = exchange(packed, tokens_axes)

    (
        xs, start, projected, probs, mixed_grad, resid_grad, tail_sums, out_grad, gain_two_grad,
    ) = call(
        forward_kernel,
        [
            ((4, 10, 64, C), BF16),
            ((TOKENS, C), BF16),
            ((TOKENS, 3 * C), BF16),
            ((16, 256, 128), BF16),
            ((TOKENS, C), BF16),
            ((TOKENS, C), F32),
            ((4096, 128), BF16),
            ((C, C), F32),
            ((8, C), F32),
        ],
        [
            place, arrived, jnp.asarray(sources_to_groups(), BF16), dw_rows,
            gain_one.reshape(1, C), w_qkv, w_out, gain_two.reshape(1, C), w_up, w_down, mask,
        ],
        [
            ((TOKENS, C), BF16),
            ((TOKENS, C), BF16),
            ((TOKENS, C), BF16),
            ((TOKENS, C), BF16),
            ((TOKENS, FF), BF16),
            ((TOKENS, FF), BF16),
        ],
        scalars=1,
        flops=8 * 10**9,
        moved=12 * 10**6,
        limit=40,
    )

    pieces, proj_grad, inputs, grad, gain_one_grad = call(
        backward_kernel,
        [
            ((4, 8 * PIECE, C), BF16),
            ((TOKENS, 3 * C), BF16),
            ((TOKENS, C), BF16),
            ((TOKENS, C), F32),
            ((8, C), F32),
        ],
        [
            place, start, projected, probs, mixed_grad, resid_grad, gain_one.reshape(1, C), w_qkv,
            mask, jnp.asarray(groups_to_pieces(), BF16),
        ],
        scalars=1,
        flops=5 * 10**9,
        moved=8 * 10**6,
        limit=32,
    )
    back = exchange(pieces.reshape(32, PIECE, C), tokens_axes).reshape(4, 8 * PIECE, C)

    keep, send = call(
        sums_kernel,
        [((64, 56, 128), BF16), ((64, 56, 128), BF16)],
        [place, xs, inputs, proj_grad, grad, gain_one_grad, gain_two_grad, out_grad, tail_sums],
        [((2048, 128), BF16), ((32, 128), F32)],
        scalars=1,
    )
    half = (keep.astype(F32) + swap(send).astype(F32)).astype(BF16)
    back, half = lax.optimization_barrier((back, half))
    main, right, left = (jnp.asarray(t, BF16) for t in pieces_to_tile())
    (input_grad,) = call(
        tile_kernel,
        [((1, 16, 64, C), F32)],
        [back, main, right, left, dw_rows],
        [((18, 80, C), F32)],
    )
    factor = 1.0 / math.sqrt(TOKENS * 128)
    (shared,) = call(
        lambda x_ref, out_ref: total_kernel(factor, x_ref, out_ref),
        [((64, 56, 128), BF16)],
        [exchange(half, sums_axes)],
        flops=10**6,
        moved=2 * 10**6,
    )
    shared, input_grad = lax.optimization_barrier((shared, input_grad))
    mine = exchange(shared, sums_axes)
    other = swap(mine)

    kernel_grad, gain_one_grad, qkv_grad, out_sum, gain_two_sum, up_grad, down_grad = call(
        outputs_kernel,
        [
            ((3, 3, C), F32),
            ((1, C), F32),
            ((C, 3 * C), F32),
            ((C, C), F32),
            ((1, C), F32),
            ((C, FF), F32),
            ((FF, C), F32),
        ],
        [place, mine, other],
        scalars=1,
        flops=10**6,
        moved=5 * 10**6,
    )
    return (
        input_grad,
        kernel_grad,
        gain_one_grad.reshape(C),
        qkv_grad,
        out_sum,
        gain_two_sum.reshape(C),
        up_grad,
        down_grad,
    )


def solution(mesh):
    cores = Mesh(mesh.devices.reshape(2, 2, 4, 8), ("yh", "core", "row", "col"))
    split = P(("yh", "core"), "row", "col", None)
    in_specs = (split, P(), P(), P(), P(), P(), P(), P(), split)
    out_specs = (split, P(), P(), P(), P(), P(), P(), P())
    return jax.shard_map(local, mesh=cores, in_specs=in_specs, out_specs=out_specs, check_vma=False)
```

```python
import math

import jax
import jax.numpy as jnp
import numpy as np
from jax import lax
from jax.experimental import pallas as pl
from jax.experimental.pallas import tpu as pltpu
from jax.sharding import Mesh
from jax.sharding import PartitionSpec as P

HEADS = 8
C = 256
FF = 1024
PIECE = 40
SUMS = 48
JOINED = PIECE + SUMS
SHARE = SUMS + 8
norm_eps = 1e-05
gelu_coef = 0.7978845608028654
cubic_coef = 0.044715
HEAD_SCALE = 1.0 / math.sqrt(C // HEADS)
TOKENS = 1024
AHEAD = 4

F32 = jnp.float32
BF16 = jnp.bfloat16


def tile_to_columns():
    out = np.zeros((256, 256), np.float32)
    for col in range(16):
        for row in range(16):
            out[col * 16 + row, row * 16 + col] = 1
    return out


def sources_to_groups():
    out = np.zeros((3, 128, 128), np.float32)
    for p in range(8):
        for a in range(2):
            for e in range(8):
                for variant, shift in enumerate((0, -1, 1)):
                    if 0 <= e + shift < 8:
                        out[variant, p * 16 + a * 8 + e, (e + shift) * 16 + a * 8 + p] = 1
    return out


def groups_to_pieces():
    out = np.zeros((8 * PIECE, 384), np.float32)
    for c in range(8):
        for j in range(2):
            out[c * PIECE + 18 * j, 256 + 8 * j + c] = 1
            out[c * PIECE + 18 * j + 17, 272 + 8 * j + c] = 1
            for row in range(16):
                a, p = divmod(row, 8)
                out[c * PIECE + 18 * j + 1 + row, (j * 8 + p) * 16 + a * 8 + c] = 1
        out[c * PIECE + 36, 288 + c] = 1
    return out


def pieces_to_tile():
    main = np.zeros((288, 8 * PIECE), np.float32)
    edges = np.zeros((2, 32, 8 * PIECE), np.float32)
    for row in range(18):
        for q in range(16):
            main[row * 16 + q, (q // 2) * PIECE + (q % 2) * 18 + row] = 1
        edges[0, row, row] = 1
        edges[1, row, 7 * PIECE + 18 + row] = 1
    return main, edges


def head_mask():
    mask = np.zeros((256, 128), np.float32)
    for h in range(4):
        mask[h * 64 : (h + 1) * 64, h * 32 : (h + 1) * 32] = 1
    return np.concatenate([mask, mask], axis=1)


def dot(a, b):
    return lax.dot_general(a, b, (((1,), (0,)), ((), ())), preferred_element_type=F32)


def dot_nt(a, b):
    return lax.dot_general(a, b, (((1,), (1,)), ((), ())), preferred_element_type=F32)


def dot_tn(a, b):
    return lax.dot_general(a, b, (((0,), (0,)), ((), ())), preferred_element_type=F32)


def norm(values):
    center = values - jnp.mean(values, axis=-1, keepdims=True)
    inverse = lax.rsqrt(jnp.mean(center * center, axis=-1, keepdims=True) + norm_eps)
    return center * inverse, inverse


def norm_back(upstream, normed, inverse, gain):
    scaled = upstream * gain
    return inverse * (
        scaled
        - jnp.mean(scaled, axis=-1, keepdims=True)
        - normed * jnp.mean(scaled * normed, axis=-1, keepdims=True)
    )


def fold_rows(values):
    return jnp.sum(values.reshape(-1, 8, values.shape[-1]), axis=0)


def side_by_side(rows):
    return jnp.concatenate([rows[0:64], rows[64:128]], axis=1)


def stacked(rows):
    return jnp.concatenate([rows[:, 0:128], rows[:, 128:256]], axis=0)


def block_diagonal(rows):
    zeros = jnp.zeros((64, 128), rows.dtype)
    upper = jnp.concatenate([rows[0:64], zeros], axis=1)
    return jnp.concatenate([upper, jnp.concatenate([zeros, rows[64:128]], axis=1)], axis=0)


def diagonal(blocks):
    return jnp.concatenate([blocks[0:64, 0:128], blocks[64:128, 128:256]], axis=0)


def by_head(rows, mask):
    return jnp.concatenate([side_by_side(rows)] * 4, axis=0) * mask


def attend_unit(query, key, value, mask):
    scores = dot_nt(by_head(key, mask), block_diagonal(query)).reshape(4, 64, 128) * HEAD_SCALE
    expos = jnp.exp(scores - jnp.max(scores, axis=1, keepdims=True))
    probs = expos * (1.0 / jnp.sum(expos, axis=1, keepdims=True))
    probs = probs.reshape(256, 128).astype(BF16)
    return probs, diagonal(dot_tn(probs, by_head(value, mask))).astype(BF16)


def attend_unit_back(query, key, value, probs, upstream, mask, wide_mask):
    wide = probs.astype(F32).reshape(4, 64, 128)
    upstream = block_diagonal(upstream)
    prob_grad = dot_nt(by_head(value, mask), upstream).reshape(4, 64, 128)
    centre = jnp.sum(wide * prob_grad, axis=1, keepdims=True)
    score_grad = (wide * (prob_grad - centre) * HEAD_SCALE).reshape(256, 128).astype(BF16)
    query_grad = diagonal(dot_tn(score_grad, by_head(key, mask)))
    key_grad = jnp.sum((dot(score_grad, block_diagonal(query)) * wide_mask).reshape(4, 64, 256), axis=0)
    value_grad = jnp.sum((dot(probs, upstream) * wide_mask).reshape(4, 64, 256), axis=0)
    return query_grad.astype(BF16), stacked(key_grad).astype(BF16), stacked(value_grad).astype(BF16)


def pack_kernel(x_ref, cot_ref, perm_ref, out_ref):
    perm = perm_ref[...]
    for block in range(4):
        tokens = x_ref[:, 16 * block : 16 * block + 16, :].reshape(256, C)
        columns = dot(perm, tokens).astype(BF16).reshape(16, 16, C)
        tokens = cot_ref[:, 16 * block : 16 * block + 16, :].reshape(256, C)
        cot_columns = dot(perm, tokens).astype(BF16).reshape(16, 16, C)
        for i in range(16):
            q = 16 * block + i
            k, odd = divmod(q, 2)
            out_ref[k, 4 + odd] = cot_columns[i]
            if odd:
                out_ref[k, 2] = columns[i]
                out_ref[(k + 1) % 32, 0] = columns[i]
            else:
                out_ref[k, 1] = columns[i]
                out_ref[(k - 1) % 32, 3] = columns[i]


def forward_kernel(
    place_ref, x_ref, perm_ref, dw_ref, gain_one_ref, w_qkv_ref, w_out_ref, gain_two_ref,
    w_up_ref, w_down_ref, mask_ref,
    xs_ref, in_ref, proj_ref, probs_ref, mixed_grad_ref, resid_grad_ref, sums_ref,
    out_grad_ref, gain_grad_ref,
    cot_s, mixed_s, two_s, low_s, act_s, pre_s,
):
    owner = place_ref[0]
    first = perm_ref[jnp.where(owner == 0, 1, 0)]
    last = perm_ref[jnp.where(owner == 31, 2, 0)]
    plain = perm_ref[0]

    for r in range(4):
        for j in range(4):
            perm = first if j == 0 else (last if j == 3 else plain)
            tokens = x_ref[8 * r : 8 * r + 8, j].reshape(128, C)
            moved = dot(perm, tokens).astype(BF16).reshape(8, 16, C)
            for p in range(8):
                xs_ref[j, p + 1, 16 * r : 16 * r + 16, :] = moved[p]
    edge = jnp.zeros((8, C), F32)
    for j in range(4):
        lowest = xs_ref[j, 8].astype(F32)
        xs_ref[j, 0] = jnp.concatenate([edge, lowest[:56]], axis=0).astype(BF16)
        highest = xs_ref[j, 1].astype(F32)
        xs_ref[j, 9] = jnp.concatenate([highest[8:], edge], axis=0).astype(BF16)

    gain_one = gain_one_ref[...]

    def conv(g, carry):
        j, p = g // 8, g % 8
        total = xs_ref[j + 1, p + 1].astype(F32)
        for u in range(3):
            for v in range(3):
                total = total + dw_ref[3 * u + v : 3 * u + v + 1, :] * xs_ref[j + v, p + u].astype(F32)
        start = total.astype(BF16)
        rows = pl.ds(pl.multiple_of(g * 64, 64), 64)
        in_ref[rows, :] = start
        normed, _ = norm(start.astype(F32))
        two_s[rows, :] = (normed * gain_one).astype(BF16)
        return carry

    lax.fori_loop(0, 16, conv, 0, unroll=16)

    def project(i, carry):
        rows = pl.ds(pl.multiple_of(i * 256, 256), 256)
        proj_ref[rows, :] = dot(two_s[rows, :], w_qkv_ref[...]).astype(BF16)
        return carry

    lax.fori_loop(0, 4, project, 0)

    mask = mask_ref[...]

    def attend(i, carry):
        units = []
        for n in range(AHEAD):
            pair = i * AHEAD + n
            rows = pl.ds(pl.multiple_of(pair * 128, 128), 128)
            for side in range(2):
                parts = [proj_ref[rows, 256 * m + 128 * side : 256 * m + 128 * side + 128] for m in range(3)]
                units.append((pair, rows, side, parts))
        results = [attend_unit(*parts, mask) for _, _, _, parts in units]
        for (pair, rows, side, _), (probs, mixed) in zip(units, results):
            probs_ref[2 * pair + side] = probs
            mixed_s[rows, 128 * side : 128 * side + 128] = mixed
        return carry

    lax.fori_loop(0, 8 // AHEAD, attend, 0)

    for r in range(4):
        for j in range(2):
            tokens = x_ref[8 * r : 8 * r + 8, 4 + j].reshape(128, C)
            moved = dot(plain, tokens).astype(BF16).reshape(8, 16, C)
            for p in range(8):
                cot_s[(j * 8 + p) * 64 + 16 * r : (j * 8 + p) * 64 + 16 * r + 16, :] = moved[p]

    gain_two = gain_two_ref[...]

    def tail(i, gain_grad):
        rows = pl.ds(pl.multiple_of(i * 512, 512), 512)
        cot = cot_s[rows, :]
        resid = in_ref[rows, :].astype(F32) + dot(mixed_s[rows, :], w_out_ref[...])
        normed, inverse = norm(resid)
        inputs = (normed * gain_two).astype(BF16)
        two_s[rows, :] = inputs
        pre = dot(inputs, w_up_ref[...])
        square = pre * pre
        tangent = jnp.tanh(gelu_coef * (pre + cubic_coef * square * pre))
        half = 0.5 * (1.0 + tangent)
        act_s[rows, :] = (pre * half).astype(BF16)
        slope = half + 0.5 * pre * (1.0 - tangent * tangent) * gelu_coef * (
            1.0 + 3.0 * cubic_coef * square
        )
        pre_grad = (dot_nt(cot, w_down_ref[...]) * slope).astype(BF16)
        pre_s[rows, :] = pre_grad
        in_grad = dot_nt(pre_grad, w_up_ref[...])
        resid_grad = cot.astype(F32) + norm_back(in_grad, normed, inverse, gain_two)
        resid_grad_ref[rows, :] = resid_grad
        low = resid_grad.astype(BF16)
        low_s[rows, :] = low
        mixed_grad_ref[rows, :] = dot_nt(low, w_out_ref[...]).astype(BF16)
        return gain_grad + fold_rows(in_grad * normed)

    gain_grad = lax.fori_loop(0, 2, tail, jnp.zeros((8, C), F32))
    gain_grad_ref[...] = gain_grad

    cot_turned = cot_s[...].T
    two_turned = two_s[...].T
    for block in range(4):
        columns = slice(256 * block, 256 * block + 256)
        down = dot(cot_turned, act_s[:, columns]).T.astype(BF16)
        up = dot(two_turned, pre_s[:, columns]).astype(BF16)
        sums_ref[256 * block : 256 * block + 256, :] = down
        sums_ref[1024 + 256 * block : 1280 + 256 * block, :] = up
    out_grad_ref[...] = dot(mixed_s[...].T, low_s[...])


def backward_kernel(
    in_ref, proj_ref, probs_ref, mixed_grad_ref, resid_grad_ref, gain_one_ref, w_qkv_ref, mask_ref,
    proj_grad_ref, inputs_ref, grad_ref, gain_grad_ref,
):
    mask = mask_ref[...]
    wide_mask = mask.astype(F32)

    def attend_back(i, carry):
        units = []
        for n in range(AHEAD):
            pair = i * AHEAD + n
            rows = pl.ds(pl.multiple_of(pair * 128, 128), 128)
            for side in range(2):
                lanes = slice(128 * side, 128 * side + 128)
                parts = [proj_ref[rows, 256 * m + 128 * side : 256 * m + 128 * side + 128] for m in range(3)]
                parts += [probs_ref[2 * pair + side], mixed_grad_ref[rows, lanes]]
                units.append((pair, rows, side, parts))
        results = [attend_unit_back(*parts, mask, wide_mask) for _, _, _, parts in units]
        for (_, rows, side, _), grads in zip(units, results):
            for m in range(3):
                proj_grad_ref[rows, 256 * m + 128 * side : 256 * m + 128 * side + 128] = grads[m]
        return carry

    lax.fori_loop(0, 8 // AHEAD, attend_back, 0)

    gain_one = gain_one_ref[...]

    def head(i, gain_grad):
        rows = pl.ds(pl.multiple_of(i * 512, 512), 512)
        normed, inverse = norm(in_ref[rows, :].astype(F32))
        inputs_ref[rows, :] = (normed * gain_one).astype(BF16)
        in_grad = dot_nt(proj_grad_ref[rows, :], w_qkv_ref[...])
        grad_ref[rows, :] = resid_grad_ref[rows, :] + norm_back(in_grad, normed, inverse, gain_one)
        return gain_grad + fold_rows(in_grad * normed)

    gain_grad_ref[...] = lax.fori_loop(0, 2, head, jnp.zeros((8, C), F32), unroll=2)


def sums_kernel(
    place_ref, xs_ref, inputs_ref, proj_grad_ref, grad_ref, gain_one_grad_ref, gain_two_grad_ref,
    out_grad_ref, tail_ref,
    keep_ref, send_ref,
    head_s, small_s,
):
    core = place_ref[1]

    def taps(g, sums):
        j, p = g // 8, g % 8
        grad = grad_ref[pl.ds(pl.multiple_of(g * 64, 64), 64), :]
        return tuple(
            sums[3 * u + v] + fold_rows(grad * xs_ref[j + v, p + u].astype(F32))
            for u in range(3)
            for v in range(3)
        )

    kernel_grad = lax.fori_loop(0, 16, taps, (jnp.zeros((8, C), F32),) * 9, unroll=4)

    inputs_turned = inputs_ref[...].T
    for block in range(3):
        terms = dot(inputs_turned, proj_grad_ref[:, 256 * block : 256 * block + 256])
        head_s[256 * block : 256 * block + 256, :] = terms.astype(BF16)
    head_s[768:1024, :] = out_grad_ref[...].astype(BF16)
    small = [jnp.sum(term, axis=0, keepdims=True) for term in kernel_grad]
    small.append(jnp.sum(gain_one_grad_ref[...], axis=0, keepdims=True))
    small.append(jnp.sum(gain_two_grad_ref[...], axis=0, keepdims=True))
    small.append(jnp.zeros((5, C), F32))
    small_s[...] = jnp.concatenate(small, axis=0)
    for ref, half in ((keep_ref, core), (send_ref, 1 - core)):
        for k in range(32):
            tail = pl.ds(pl.multiple_of(half * 1024 + 32 * k, 32), 32)
            head = pl.ds(pl.multiple_of(half * 512 + 16 * k, 16), 16)
            ref[k, 0:32, :] = tail_ref[tail, :]
            ref[k, 32:48, :] = head_s[head, :]
        rows = small_s[pl.ds(pl.multiple_of(half * 8, 8), 8), :]
        ref[32, 0:16, :] = jnp.concatenate([rows, rows], axis=0).astype(BF16)
        ref[32, 16:48, :] = jnp.zeros((32, C), BF16)


def pieces_kernel(grad_ref, keep_ref, swapped_ref, perm_ref, out_ref):
    perm = perm_ref[...]
    edge = jnp.zeros((8, C), F32)
    small = keep_ref[32, 0:16, :].astype(F32) + swapped_ref[32, 0:16, :].astype(F32)
    for r in range(4):
        parts = [grad_ref[64 * g + 16 * r : 64 * g + 16 * r + 16, :] for g in range(16)]
        for j in range(2):
            lowest = 64 * (8 * j + 7) + 16 * r - 8
            parts.append(grad_ref[lowest : lowest + 8, :] if r > 0 else edge)
        for j in range(2):
            highest = 64 * 8 * j + 16 * r + 16
            parts.append(grad_ref[highest : highest + 8, :] if r < 3 else edge)
        parts.append(small[0:8] if r == 0 else edge)
        parts.append(jnp.zeros((88, C), F32))
        tokens = jnp.concatenate(parts, axis=0).astype(BF16)
        moved = dot(perm, tokens).reshape(8, PIECE, C)
        pieces = slice(8 * r, 8 * r + 8)
        sums = keep_ref[pieces].astype(F32) + swapped_ref[pieces].astype(F32)
        joined = jnp.concatenate([moved, sums], axis=1)
        out_ref[r] = joined.reshape(8 * JOINED, C).astype(BF16)


def partial_kernel(factor, x_ref, out_ref):
    total = jnp.zeros((SHARE, C), F32)
    for r in range(4):
        pieces = jnp.sum(x_ref[r].astype(F32).reshape(8, JOINED, C), axis=0)
        total = total + jnp.concatenate([pieces[PIECE:], pieces[32:40]], axis=0)
    out_ref[...] = total * factor


def total_kernel(mine_ref, other_ref, out_ref):
    total = mine_ref[...] + other_ref[...]
    rows = jnp.concatenate([total] * 8, axis=0).astype(BF16)
    for r in range(4):
        out_ref[r] = rows


def unpack_kernel(pieces_ref, main_ref, edges_ref, tile_ref, first_ref, last_ref):
    for block in range(4):
        pieces = pieces_ref[block].astype(F32).reshape(8, JOINED, C)
        pieces = pieces[:, :PIECE].reshape(8 * PIECE, C).astype(BF16)
        columns = dot(main_ref[...], pieces).astype(BF16)
        tile_ref[:, 16 * block : 16 * block + 16, :] = columns.reshape(18, 16, C)
        if block == 0:
            first_ref[...] = dot(edges_ref[0], pieces).astype(BF16)
        if block == 3:
            last_ref[...] = dot(edges_ref[1], pieces).astype(BF16)


def tile_kernel(tile_ref, left_ref, right_ref, dw_ref, out_ref, wide):
    wide[:, 8:72, :] = tile_ref[...].astype(F32)
    left = left_ref[...].astype(F32)
    right = right_ref[...].astype(F32)
    for i in range(18):
        wide[i, 7:8, :] = left[i : i + 1]
        wide[i, 72:73, :] = right[i : i + 1]

    def row(i, carry):
        rows = [wide[i + 2 - u] for u in range(3)]
        total = wide[i + 1, 8:72, :]
        for v in range(3):
            term = dw_ref[v : v + 1, :] * rows[0]
            for u in range(1, 3):
                term = term + dw_ref[3 * u + v : 3 * u + v + 1, :] * rows[u]
            total = total + term[9 - v : 73 - v, :]
        out_ref[0, i] = total
        return carry

    lax.fori_loop(0, 16, row, 0)


def outputs_kernel(
    place_ref, mine_ref, other_ref,
    kernel_ref, gain_one_ref, qkv_ref, out_ref, gain_two_ref, up_ref, down_ref,
):
    own = place_ref[1] == 0
    for r in range(4):
        mine = mine_ref[r].astype(F32).reshape(8, SHARE, C)
        other = other_ref[r].astype(F32).reshape(8, SHARE, C)
        lower = jnp.where(own, mine, other)
        upper = jnp.where(own, other, mine)
        down_ref[256 * r : 256 * r + 256, :] = lower[:, 0:32].reshape(256, C)
        up_ref[:, 256 * r : 256 * r + 256] = upper[:, 0:32].reshape(256, C)
        rows = slice(128 * (r % 2), 128 * (r % 2) + 128)
        block = r // 2
        qkv_ref[rows, 256 * block : 256 * block + 256] = lower[:, 32:48].reshape(128, C)
        if r < 2:
            qkv_ref[rows, 512:768] = upper[:, 32:48].reshape(128, C)
        else:
            out_ref[rows, :] = upper[:, 32:48].reshape(128, C)
        if r == 0:
            small = [side[c, 52:53] for side in (lower, upper) for c in range(8)]
            small = jnp.concatenate(small, axis=0)
            for u in range(3):
                kernel_ref[u] = small[3 * u : 3 * u + 3]
            gain_one_ref[...] = small[9:10]
            gain_two_ref[...] = small[10:11]


VMEM = pl.BlockSpec(memory_space=pltpu.VMEM)
SMEM = pl.BlockSpec(memory_space=pltpu.SMEM)


def call(kernel, outs, operands, scratch=(), scalars=0, flops=0, moved=0, limit=24):
    return pl.pallas_call(
        kernel,
        out_shape=tuple(jax.ShapeDtypeStruct(shape, dtype) for shape, dtype in outs),
        in_specs=[SMEM] * scalars + [VMEM] * (len(operands) - scalars),
        out_specs=tuple(VMEM for _ in outs),
        scratch_shapes=[pltpu.VMEM(shape, dtype) for shape, dtype in scratch],
        compiler_params=pltpu.CompilerParams(vmem_limit_bytes=limit * 2**20),
        cost_estimate=pl.CostEstimate(flops=flops, bytes_accessed=moved, transcendentals=0),
    )(*operands)


def local(input_map, dw_kernel, gain_one, w_qkv, w_out, gain_two, w_up, w_down, cotangent):
    owner = lax.axis_index("row") * 8 + lax.axis_index("col")
    core = lax.axis_index("core")
    place = jnp.stack([owner, core]).astype(jnp.int32)
    dw_rows = dw_kernel.reshape(9, C).astype(F32)
    mask = jnp.asarray(head_mask(), BF16)

    def exchange(stacked):
        return lax.all_to_all(stacked, ("row", "col"), split_axis=0, concat_axis=0, tiled=True)

    def swap(values, axis):
        return lax.ppermute(values, axis, [(0, 1), (1, 0)])

    def shift(values, axis, step):
        size = lax.axis_size(axis)
        pairs = [(i, i + step) for i in range(size) if 0 <= i + step < size]
        return lax.ppermute(values, axis, pairs)

    (packed,) = call(
        pack_kernel,
        [((32, 6, 16, C), BF16)],
        [input_map[0], cotangent[0], jnp.asarray(tile_to_columns(), BF16)],
        flops=4 * 10**8,
        moved=4 * 10**6,
        limit=60,
    )
    arrived = exchange(packed)

    (
        xs, start, projected, probs, mixed_grad, resid_grad, tail_sums, out_grad, gain_two_grad,
    ) = call(
        forward_kernel,
        [
            ((4, 10, 64, C), BF16),
            ((TOKENS, C), BF16),
            ((TOKENS, 3 * C), BF16),
            ((16, 256, 128), BF16),
            ((TOKENS, C), BF16),
            ((TOKENS, C), F32),
            ((2048, C), BF16),
            ((C, C), F32),
            ((8, C), F32),
        ],
        [
            place, arrived, jnp.asarray(sources_to_groups(), BF16), dw_rows,
            gain_one.reshape(1, C), w_qkv, w_out, gain_two.reshape(1, C), w_up, w_down, mask,
        ],
        [
            ((TOKENS, C), BF16),
            ((TOKENS, C), BF16),
            ((TOKENS, C), BF16),
            ((TOKENS, C), BF16),
            ((TOKENS, FF), BF16),
            ((TOKENS, FF), BF16),
        ],
        scalars=1,
        flops=8 * 10**9,
        moved=12 * 10**6,
        limit=40,
    )

    proj_grad, inputs, grad, gain_one_grad = call(
        backward_kernel,
        [((TOKENS, 3 * C), BF16), ((TOKENS, C), BF16), ((TOKENS, C), F32), ((8, C), F32)],
        [start, projected, probs, mixed_grad, resid_grad, gain_one.reshape(1, C), w_qkv, mask],
        flops=5 * 10**9,
        moved=8 * 10**6,
        limit=32,
    )
    keep, send = call(
        sums_kernel,
        [((33, SUMS, C), BF16), ((33, SUMS, C), BF16)],
        [place, xs, inputs, proj_grad, grad, gain_one_grad, gain_two_grad, out_grad, tail_sums],
        [((1024, C), BF16), ((16, C), F32)],
        scalars=1,
    )
    (pieces,) = call(
        pieces_kernel,
        [((4, 8 * JOINED, C), BF16)],
        [grad, keep, swap(send, "core"), jnp.asarray(groups_to_pieces(), BF16)],
    )
    back = exchange(pieces.reshape(32, JOINED, C)).reshape(4, 8 * JOINED, C)
    factor = 1.0 / math.sqrt(TOKENS * 128)
    (partial,) = call(
        lambda x_ref, out_ref: partial_kernel(factor, x_ref, out_ref),
        [((SHARE, C), F32)],
        [back],
    )
    main, edges = (jnp.asarray(t, BF16) for t in pieces_to_tile())
    tile, first, last = call(
        unpack_kernel,
        [((18, 64, C), BF16), ((32, C), BF16), ((32, C), BF16)],
        [back, main, edges],
    )
    left, right = shift(last, "col", 1), shift(first, "col", -1)
    (shared,) = call(
        total_kernel,
        [((4, 8 * SHARE, C), BF16)],
        [partial, swap(partial, "yh")],
    )
    mine = exchange(shared.reshape(32, SHARE, C)).reshape(4, 8 * SHARE, C)
    (input_grad,) = call(
        tile_kernel,
        [((1, 16, 64, C), F32)],
        [tile, left, right, dw_rows],
        [((18, 80, C), F32)],
    )
    mine, input_grad = lax.optimization_barrier((mine, input_grad))
    other = swap(mine, "core")
    kernel_grad, gain_one_grad, qkv_grad, out_sum, gain_two_sum, up_grad, down_grad = call(
        outputs_kernel,
        [
            ((3, 3, C), F32),
            ((1, C), F32),
            ((C, 3 * C), F32),
            ((C, C), F32),
            ((1, C), F32),
            ((C, FF), F32),
            ((FF, C), F32),
        ],
        [place, mine, other],
        scalars=1,
        flops=10**6,
        moved=5 * 10**6,
    )
    return (
        input_grad,
        kernel_grad,
        gain_one_grad.reshape(C),
        qkv_grad,
        out_sum,
        gain_two_sum.reshape(C),
        up_grad,
        down_grad,
    )


def solution(mesh):
    cores = Mesh(mesh.devices.reshape(2, 2, 4, 8), ("yh", "core", "row", "col"))
    split = P(("yh", "core"), "row", "col", None)
    in_specs = (split, P(), P(), P(), P(), P(), P(), P(), split)
    out_specs = (split, P(), P(), P(), P(), P(), P(), P())
    return jax.shard_map(local, mesh=cores, in_specs=in_specs, out_specs=out_specs, check_vma=False)
```

```python
import math

import jax
import jax.numpy as jnp
import numpy as np
from jax import lax
from jax.experimental import pallas as pl
from jax.experimental.pallas import tpu as pltpu
from jax.sharding import Mesh
from jax.sharding import PartitionSpec as P

HEADS = 8
C = 256
FF = 1024
PIECE = 40
SUMS = 48
JOINED = PIECE + SUMS
SHARE = SUMS + 8
norm_eps = 1e-05
gelu_coef = 0.7978845608028654
cubic_coef = 0.044715
HEAD_SCALE = 1.0 / math.sqrt(C // HEADS)
TOKENS = 1024
AHEAD = 8
CHUNK = 1024
ROWS = 64
SPAN = 16

F32 = jnp.float32
BF16 = jnp.bfloat16


def positions(size):
    return tuple(lax.broadcasted_iota(jnp.int32, (size, size), axis) for axis in range(2))


def as_matrix(chosen):
    return jnp.where(chosen, 1.0, 0.0).astype(BF16)


def tile_to_columns():
    to, of = positions(256)
    return as_matrix(((to >> 4) == (of & 15)) & ((to & 15) == (of >> 4)))


def sources_to_groups(shift):
    to, of = positions(128)
    same = ((to >> 4) == (of & 7)) & (((to >> 3) & 1) == ((of >> 3) & 1))
    return as_matrix(same & ((of >> 4) == (to & 7) + shift))


def head_mask():
    row, lane = positions(256)
    return as_matrix((row >> 6) == ((lane >> 5) & 3))


def turned_head_mask():
    lane, row = (lax.broadcasted_iota(jnp.int32, (128, 256), axis) for axis in range(2))
    return as_matrix((row >> 6) == (lane >> 5))


def groups_to_pieces():
    out = np.zeros((8 * PIECE, 384), np.float32)
    for c in range(8):
        for j in range(2):
            out[c * PIECE + 18 * j, 256 + 8 * j + c] = 1
            out[c * PIECE + 18 * j + 17, 272 + 8 * j + c] = 1
            for row in range(16):
                a, p = divmod(row, 8)
                out[c * PIECE + 18 * j + 1 + row, (j * 8 + p) * 16 + a * 8 + c] = 1
        out[c * PIECE + 36, 288 + c] = 1
    return out


def pieces_to_tile():
    main = np.zeros((288, 8 * PIECE), np.float32)
    edges = np.zeros((2, 32, 8 * PIECE), np.float32)
    for row in range(18):
        for q in range(16):
            main[row * 16 + q, (q // 2) * PIECE + (q % 2) * 18 + row] = 1
        edges[0, row, row] = 1
        edges[1, row, 7 * PIECE + 18 + row] = 1
    return main, edges


def dot(a, b):
    return lax.dot_general(a, b, (((1,), (0,)), ((), ())), preferred_element_type=F32)


def dot_nt(a, b):
    return lax.dot_general(a, b, (((1,), (1,)), ((), ())), preferred_element_type=F32)


def dot_tn(a, b):
    return lax.dot_general(a, b, (((0,), (0,)), ((), ())), preferred_element_type=F32)


def norm(values):
    center = values - jnp.mean(values, axis=-1, keepdims=True)
    inverse = lax.rsqrt(jnp.mean(center * center, axis=-1, keepdims=True) + norm_eps)
    return center * inverse, inverse


def norm_back(upstream, normed, inverse, gain):
    scaled = upstream * gain
    return inverse * (
        scaled
        - jnp.mean(scaled, axis=-1, keepdims=True)
        - normed * jnp.mean(scaled * normed, axis=-1, keepdims=True)
    )


def fold_rows(values):
    return jnp.sum(values.reshape(-1, 8, values.shape[-1]), axis=0)


def side_by_side(rows):
    return jnp.concatenate([rows[0:64], rows[64:128]], axis=1)


def stacked(rows):
    return jnp.concatenate([rows[:, 0:128], rows[:, 128:256]], axis=0)


def block_diagonal(rows):
    zeros = jnp.zeros((64, 128), rows.dtype)
    upper = jnp.concatenate([rows[0:64], zeros], axis=1)
    return jnp.concatenate([upper, jnp.concatenate([zeros, rows[64:128]], axis=1)], axis=0)


def by_head(rows, mask):
    return jnp.concatenate([side_by_side(rows)] * 4, axis=0) * mask


def by_lane_half(columns, lower):
    return jnp.concatenate([columns * lower, columns * (1 - lower)], axis=0)


def by_head_turned(columns, lower, turned_mask):
    swapped = jnp.concatenate([columns[:, 64:128], columns[:, 0:64]], axis=1)
    parts = []
    for first, second in ((columns, swapped), (swapped, columns)):
        part = first * lower + second * (1 - lower)
        parts.append(jnp.concatenate([part, part], axis=1) * turned_mask)
    return jnp.concatenate(parts, axis=0)


def own_half(blocks, lower):
    return jnp.where(lower, blocks[0:128], blocks[128:256]).astype(BF16)


def lane_half():
    return lax.broadcasted_iota(jnp.int32, (1, 128), 1) < 64


def attend_unit(query_turned, key, value_turned, lower, mask, turned_mask):
    low = lower.astype(F32).astype(BF16)
    scores = dot(by_head(key, mask), by_lane_half(query_turned, low)).reshape(4, 64, 128) * HEAD_SCALE
    expos = jnp.exp(scores - jnp.max(scores, axis=1, keepdims=True))
    probs = expos * (1.0 / jnp.sum(expos, axis=1, keepdims=True))
    probs = probs.reshape(256, 128).astype(BF16)
    mixed = dot(by_head_turned(value_turned, low, turned_mask), probs)
    return probs, own_half(mixed, lower)


def attend_unit_back(
    query, key_turned, value, probs, upstream, upstream_turned, lower, mask, turned_mask, wide_mask
):
    low = lower.astype(F32).astype(BF16)
    wide = probs.astype(F32).reshape(4, 64, 128)
    prob_grad = dot(by_head(value, mask), by_lane_half(upstream_turned, low)).reshape(4, 64, 128)
    centre = jnp.sum(wide * prob_grad, axis=1, keepdims=True)
    score_grad = (wide * (prob_grad - centre) * HEAD_SCALE).reshape(256, 128).astype(BF16)
    query_grad = own_half(dot(by_head_turned(key_turned, low, turned_mask), score_grad), lower)
    key_grad = jnp.sum((dot(score_grad, block_diagonal(query)) * wide_mask).reshape(4, 64, 256), axis=0)
    value_grad = jnp.sum((dot(probs, block_diagonal(upstream)) * wide_mask).reshape(4, 64, 256), axis=0)
    return query_grad, stacked(key_grad).astype(BF16), stacked(value_grad).astype(BF16)


def pack_kernel(x_ref, cot_ref, out_ref):
    perm = tile_to_columns()
    for block in range(4):
        tokens = x_ref[:, 16 * block : 16 * block + 16, :].reshape(256, C)
        columns = dot(perm, tokens).astype(BF16).reshape(16, 16, C)
        tokens = cot_ref[:, 16 * block : 16 * block + 16, :].reshape(256, C)
        cot_columns = dot(perm, tokens).astype(BF16).reshape(16, 16, C)
        for i in range(16):
            q = 16 * block + i
            k, odd = divmod(q, 2)
            out_ref[k, 4 + odd] = cot_columns[i]
            if odd:
                out_ref[k, 2] = columns[i]
                out_ref[(k + 1) % 32, 0] = columns[i]
            else:
                out_ref[k, 1] = columns[i]
                out_ref[(k - 1) % 32, 3] = columns[i]


def store_halves(core, lower, upper, keep_ref, send_ref, rows):
    keep_ref[rows, :] = jnp.where(core == 0, lower, upper).astype(BF16)
    send_ref[rows, :] = jnp.where(core == 0, upper, lower).astype(BF16)


def forward_kernel(
    place_ref, x_ref, dw_ref, gain_one_ref, w_qkv_ref, w_out_ref, gain_two_ref,
    w_up_ref, w_down_ref,
    xs_ref, in_ref, proj_ref, key_turned_ref, probs_ref, mixed_grad_ref, resid_grad_ref, keep_ref, send_ref,
    out_grad_ref, gain_grad_ref,
    cot_s, mixed_s, two_s, low_s, act_s, pre_s, turned_s, mixed_turned_s,
    narrow_s, normed_s, wide_s, cot_wide_s,
):
    owner = place_ref[0]
    core = place_ref[1]
    first = sources_to_groups(jnp.where(owner == 0, -1, 0))
    last = sources_to_groups(jnp.where(owner == 31, 1, 0))
    plain = sources_to_groups(0)

    for r in range(4):
        for j in range(4):
            perm = first if j == 0 else (last if j == 3 else plain)
            tokens = x_ref[8 * r : 8 * r + 8, j].reshape(128, C)
            moved = dot(perm, tokens).astype(BF16).reshape(8, 16, C)
            for p in range(8):
                xs_ref[j, p + 1, 16 * r : 16 * r + 16, :] = moved[p]
    edge = jnp.zeros((8, C), F32)
    for j in range(4):
        lowest = xs_ref[j, 8].astype(F32)
        xs_ref[j, 0] = jnp.concatenate([edge, lowest[:56]], axis=0).astype(BF16)
        highest = xs_ref[j, 1].astype(F32)
        xs_ref[j, 9] = jnp.concatenate([highest[8:], edge], axis=0).astype(BF16)

    gain_one = gain_one_ref[...]

    def conv(g, carry):
        j, p = g // 8, g % 8
        total = xs_ref[j + 1, p + 1].astype(F32)
        for u in range(3):
            for v in range(3):
                total = total + dw_ref[3 * u + v : 3 * u + v + 1, :] * xs_ref[j + v, p + u].astype(F32)
        start = total.astype(BF16)
        rows = pl.ds(pl.multiple_of(g * 64, 64), 64)
        in_ref[rows, :] = start
        normed, _ = norm(start.astype(F32))
        two_s[rows, :] = (normed * gain_one).astype(BF16)
        return carry

    lax.fori_loop(0, 16, conv, 0, unroll=16)

    def project(i, carry):
        rows = pl.ds(pl.multiple_of(i * 256, 256), 256)
        proj_ref[rows, :] = dot(two_s[rows, :], w_qkv_ref[...]).astype(BF16)
        return carry

    lax.fori_loop(0, 4, project, 0)

    turned_s[0:256, :] = proj_ref[:, 0:256].T
    turned_s[256:512, :] = proj_ref[:, 512:768].T
    key_turned_ref[...] = proj_ref[:, 256:512].T
    mask = head_mask()
    turned_mask = turned_head_mask()
    lower = lane_half()

    def attend(i, carry):
        units = []
        for n in range(AHEAD):
            pair = i * AHEAD + n
            rows = pl.ds(pl.multiple_of(pair * 128, 128), 128)
            for side in range(2):
                lanes = slice(128 * side, 128 * side + 128)
                query = turned_s[lanes, rows]
                key = proj_ref[rows, 256 + 128 * side : 384 + 128 * side]
                value = turned_s[256 + 128 * side : 384 + 128 * side, rows]
                units.append((2 * pair + side, lanes, rows, (query, key, value)))
        results = [attend_unit(*parts, lower, mask, turned_mask) for _, _, _, parts in units]
        for (unit, lanes, rows, _), (probs, mixed) in zip(units, results):
            probs_ref[unit] = probs
            mixed_turned_s[lanes, rows] = mixed
        return carry

    lax.fori_loop(0, 8 // AHEAD, attend, 0)
    mixed_s[...] = mixed_turned_s[...].T

    for r in range(4):
        for j in range(2):
            tokens = x_ref[8 * r : 8 * r + 8, 4 + j].reshape(128, C)
            moved = dot(plain, tokens).astype(BF16).reshape(8, 16, C)
            for p in range(8):
                cot_s[(j * 8 + p) * 64 + 16 * r : (j * 8 + p) * 64 + 16 * r + 16, :] = moved[p]

    gain_two = gain_two_ref[...]

    def tail(i, gain_grad):
        rows = pl.ds(pl.multiple_of(i * CHUNK, CHUNK), CHUNK)
        narrow_s[...] = dot(mixed_s[rows, :], w_out_ref[...])
        inverses = []
        for n in range(CHUNK // ROWS):
            part = slice(ROWS * n, ROWS * n + ROWS)
            own = pl.ds(pl.multiple_of(i * CHUNK + ROWS * n, ROWS), ROWS)
            normed, inverse = norm(in_ref[own, :].astype(F32) + narrow_s[part, :])
            inverses.append(inverse)
            normed_s[part, :] = normed
            two_s[own, :] = (normed * gain_two).astype(BF16)
        wide_s[...] = dot(two_s[rows, :], w_up_ref[...])
        cot_wide_s[...] = dot_nt(cot_s[rows, :], w_down_ref[...])
        for n in range(CHUNK // SPAN):
            part = slice(SPAN * n, SPAN * n + SPAN)
            own = pl.ds(pl.multiple_of(i * CHUNK + SPAN * n, SPAN), SPAN)
            for block in range(4):
                columns = slice(256 * block, 256 * block + 256)
                pre = wide_s[part, columns]
                square = pre * pre
                tangent = jnp.tanh(pre * (gelu_coef + (gelu_coef * cubic_coef) * square))
                half = 0.5 + 0.5 * tangent
                act = pre * half
                act_s[own, columns] = act.astype(BF16)
                slope = half + (act - act * half) * (
                    2.0 * gelu_coef + (6.0 * gelu_coef * cubic_coef) * square
                )
                pre_s[own, columns] = (cot_wide_s[part, columns] * slope).astype(BF16)
        narrow_s[...] = dot_nt(pre_s[rows, :], w_up_ref[...])
        for n in range(CHUNK // ROWS):
            part = slice(ROWS * n, ROWS * n + ROWS)
            own = pl.ds(pl.multiple_of(i * CHUNK + ROWS * n, ROWS), ROWS)
            in_grad = narrow_s[part, :]
            normed = normed_s[part, :]
            back = norm_back(in_grad, normed, inverses[n], gain_two)
            resid_grad = cot_s[own, :].astype(F32) + back
            resid_grad_ref[own, :] = resid_grad
            low_s[own, :] = resid_grad.astype(BF16)
            gain_grad = gain_grad + fold_rows(in_grad * normed)
        mixed_grad_ref[rows, :] = dot_nt(low_s[rows, :], w_out_ref[...]).astype(BF16)
        return gain_grad

    gain_grad = lax.fori_loop(0, TOKENS // CHUNK, tail, jnp.zeros((8, C), F32))
    gain_grad_ref[...] = gain_grad

    cot_turned = cot_s[...].T
    two_turned = two_s[...].T
    for block in range(4):
        columns = slice(256 * block, 256 * block + 256)
        down = dot(cot_turned, act_s[:, columns]).T
        up = dot(two_turned, pre_s[:, columns])
        store_halves(core, down, up, keep_ref, send_ref, slice(256 * block, 256 * block + 256))
    out_grad_ref[...] = dot(mixed_turned_s[...], low_s[...])


def backward_kernel(
    in_ref, proj_ref, key_turned_ref, probs_ref, mixed_grad_ref, resid_grad_ref, gain_one_ref,
    w_qkv_ref,
    proj_grad_ref, inputs_ref, grad_ref, gain_grad_ref,
    upstream_s, query_grad_s,
):
    upstream_s[...] = mixed_grad_ref[...].T
    mask = head_mask()
    wide_mask = mask.astype(F32)
    turned_mask = turned_head_mask()
    lower = lane_half()

    def attend_back(i, carry):
        units = []
        for n in range(AHEAD):
            pair = i * AHEAD + n
            rows = pl.ds(pl.multiple_of(pair * 128, 128), 128)
            for side in range(2):
                lanes = slice(128 * side, 128 * side + 128)
                parts = (
                    proj_ref[rows, lanes],
                    key_turned_ref[lanes, rows],
                    proj_ref[rows, 512 + 128 * side : 640 + 128 * side],
                    probs_ref[2 * pair + side],
                    mixed_grad_ref[rows, lanes],
                    upstream_s[lanes, rows],
                )
                units.append((side, lanes, rows, parts))
        results = [
            attend_unit_back(*parts, lower, mask, turned_mask, wide_mask) for _, _, _, parts in units
        ]
        for (side, lanes, rows, _), grads in zip(units, results):
            query_grad_s[lanes, rows] = grads[0]
            proj_grad_ref[rows, 256 + 128 * side : 384 + 128 * side] = grads[1]
            proj_grad_ref[rows, 512 + 128 * side : 640 + 128 * side] = grads[2]
        return carry

    lax.fori_loop(0, 8 // AHEAD, attend_back, 0)
    proj_grad_ref[:, 0:256] = query_grad_s[...].T

    gain_one = gain_one_ref[...]

    def head(i, gain_grad):
        rows = pl.ds(pl.multiple_of(i * 512, 512), 512)
        normed, inverse = norm(in_ref[rows, :].astype(F32))
        inputs_ref[rows, :] = (normed * gain_one).astype(BF16)
        in_grad = dot_nt(proj_grad_ref[rows, :], w_qkv_ref[...])
        grad_ref[rows, :] = resid_grad_ref[rows, :] + norm_back(in_grad, normed, inverse, gain_one)
        return gain_grad + fold_rows(in_grad * normed)

    gain_grad_ref[...] = lax.fori_loop(0, 2, head, jnp.zeros((8, C), F32), unroll=2)


def sums_kernel(
    place_ref, xs_ref, inputs_ref, proj_grad_ref, grad_ref, gain_one_grad_ref, gain_two_grad_ref,
    out_grad_ref,
    keep_ref, send_ref,
):
    core = place_ref[1]

    def taps(g, sums):
        j, p = g // 8, g % 8
        grad = grad_ref[pl.ds(pl.multiple_of(g * 64, 64), 64), :]
        return tuple(
            sums[3 * u + v] + fold_rows(grad * xs_ref[j + v, p + u].astype(F32))
            for u in range(3)
            for v in range(3)
        )

    kernel_grad = lax.fori_loop(0, 16, taps, (jnp.zeros((8, C), F32),) * 9, unroll=4)

    inputs_turned = inputs_ref[...].T
    terms = [
        dot(inputs_turned, proj_grad_ref[:, 256 * block : 256 * block + 256])
        for block in range(3)
    ]
    terms.append(out_grad_ref[...])
    for block in range(2):
        rows = slice(256 * block, 256 * block + 256)
        store_halves(core, terms[block], terms[2 + block], keep_ref, send_ref, rows)
    small = [jnp.sum(term, axis=0, keepdims=True) for term in kernel_grad]
    small.append(jnp.sum(gain_one_grad_ref[...], axis=0, keepdims=True))
    small.append(jnp.sum(gain_two_grad_ref[...], axis=0, keepdims=True))
    small.append(jnp.zeros((5, C), F32))
    lower, upper = jnp.concatenate(small[0:8], axis=0), jnp.concatenate(small[8:], axis=0)
    lower, upper = (jnp.concatenate([rows, rows], axis=0) for rows in (lower, upper))
    store_halves(core, lower, upper, keep_ref, send_ref, slice(512, 528))


def pieces_kernel(
    grad_ref, tail_ref, other_tail_ref, head_ref, other_head_ref, perm_ref, out_ref
):
    perm = perm_ref[...]
    edge = jnp.zeros((8, C), F32)
    small = head_ref[512:528, :].astype(F32) + other_head_ref[512:528, :].astype(F32)
    for r in range(4):
        parts = [grad_ref[64 * g + 16 * r : 64 * g + 16 * r + 16, :] for g in range(16)]
        for j in range(2):
            lowest = 64 * (8 * j + 7) + 16 * r - 8
            parts.append(grad_ref[lowest : lowest + 8, :] if r > 0 else edge)
        for j in range(2):
            highest = 64 * 8 * j + 16 * r + 16
            parts.append(grad_ref[highest : highest + 8, :] if r < 3 else edge)
        parts.append(small[0:8] if r == 0 else edge)
        parts.append(jnp.zeros((88, C), F32))
        tokens = jnp.concatenate(parts, axis=0).astype(BF16)
        moved = dot(perm, tokens).reshape(8, PIECE, C)
        rows = slice(256 * r, 256 * r + 256)
        tail = tail_ref[rows, :].astype(F32) + other_tail_ref[rows, :].astype(F32)
        rows = slice(128 * r, 128 * r + 128)
        head = head_ref[rows, :].astype(F32) + other_head_ref[rows, :].astype(F32)
        joined = [moved, tail.reshape(8, 32, C), head.reshape(8, 16, C)]
        joined = jnp.concatenate(joined, axis=1)
        out_ref[r] = joined.reshape(8 * JOINED, C).astype(BF16)


def partial_kernel(factor, x_ref, out_ref):
    total = jnp.zeros((SHARE, C), F32)
    for r in range(4):
        pieces = jnp.sum(x_ref[r].astype(F32).reshape(8, JOINED, C), axis=0)
        total = total + jnp.concatenate([pieces[PIECE:], pieces[32:40]], axis=0)
    out_ref[...] = total * factor


def total_kernel(mine_ref, other_ref, out_ref):
    total = mine_ref[...] + other_ref[...]
    rows = jnp.concatenate([total] * 8, axis=0).astype(BF16)
    for r in range(4):
        out_ref[r] = rows


def unpack_kernel(pieces_ref, main_ref, edges_ref, tile_ref, first_ref, last_ref):
    for block in range(4):
        pieces = pieces_ref[block].astype(F32).reshape(8, JOINED, C)
        pieces = pieces[:, :PIECE].reshape(8 * PIECE, C).astype(BF16)
        columns = dot(main_ref[...], pieces).astype(BF16)
        tile_ref[:, 16 * block : 16 * block + 16, :] = columns.reshape(18, 16, C)
        if block == 0:
            first_ref[...] = dot(edges_ref[0], pieces).astype(BF16)
        if block == 3:
            last_ref[...] = dot(edges_ref[1], pieces).astype(BF16)


def tile_kernel(tile_ref, left_ref, right_ref, dw_ref, out_ref, wide):
    wide[:, 8:72, :] = tile_ref[...].astype(F32)
    left = left_ref[...].astype(F32)
    right = right_ref[...].astype(F32)
    for i in range(18):
        wide[i, 7:8, :] = left[i : i + 1]
        wide[i, 72:73, :] = right[i : i + 1]

    def row(i, carry):
        rows = [wide[i + 2 - u] for u in range(3)]
        total = wide[i + 1, 8:72, :]
        for v in range(3):
            term = dw_ref[v : v + 1, :] * rows[0]
            for u in range(1, 3):
                term = term + dw_ref[3 * u + v : 3 * u + v + 1, :] * rows[u]
            total = total + term[9 - v : 73 - v, :]
        out_ref[0, i] = total
        return carry

    lax.fori_loop(0, 16, row, 0)


def outputs_kernel(
    place_ref, mine_ref, other_ref,
    kernel_ref, gain_one_ref, qkv_ref, out_ref, gain_two_ref, up_ref, down_ref,
):
    own = place_ref[1] == 0
    for r in range(4):
        mine = mine_ref[r].astype(F32).reshape(8, SHARE, C)
        other = other_ref[r].astype(F32).reshape(8, SHARE, C)
        lower = jnp.where(own, mine, other)
        upper = jnp.where(own, other, mine)
        down_ref[256 * r : 256 * r + 256, :] = lower[:, 0:32].reshape(256, C)
        up_ref[:, 256 * r : 256 * r + 256] = upper[:, 0:32].reshape(256, C)
        rows = slice(128 * (r % 2), 128 * (r % 2) + 128)
        block = r // 2
        qkv_ref[rows, 256 * block : 256 * block + 256] = lower[:, 32:48].reshape(128, C)
        if r < 2:
            qkv_ref[rows, 512:768] = upper[:, 32:48].reshape(128, C)
        else:
            out_ref[rows, :] = upper[:, 32:48].reshape(128, C)
        if r == 0:
            small = [side[c, 52:53] for side in (lower, upper) for c in range(8)]
            small = jnp.concatenate(small, axis=0)
            for u in range(3):
                kernel_ref[u] = small[3 * u : 3 * u + 3]
            gain_one_ref[...] = small[9:10]
            gain_two_ref[...] = small[10:11]


VMEM = pl.BlockSpec(memory_space=pltpu.VMEM)
SMEM = pl.BlockSpec(memory_space=pltpu.SMEM)


def call(kernel, outs, operands, scratch=(), scalars=0, flops=0, moved=0, limit=24):
    return pl.pallas_call(
        kernel,
        out_shape=tuple(jax.ShapeDtypeStruct(shape, dtype) for shape, dtype in outs),
        in_specs=[SMEM] * scalars + [VMEM] * (len(operands) - scalars),
        out_specs=tuple(VMEM for _ in outs),
        scratch_shapes=[pltpu.VMEM(shape, dtype) for shape, dtype in scratch],
        compiler_params=pltpu.CompilerParams(vmem_limit_bytes=limit * 2**20),
        cost_estimate=pl.CostEstimate(flops=flops, bytes_accessed=moved, transcendentals=0),
    )(*operands)


def local(input_map, dw_kernel, gain_one, w_qkv, w_out, gain_two, w_up, w_down, cotangent):
    owner = lax.axis_index("row") * 8 + lax.axis_index("col")
    core = lax.axis_index("core")
    place = jnp.stack([owner, core]).astype(jnp.int32)
    dw_rows = dw_kernel.reshape(9, C).astype(F32)

    def exchange(stacked):
        return lax.all_to_all(stacked, ("row", "col"), split_axis=0, concat_axis=0, tiled=True)

    def swap(values, axis):
        return lax.ppermute(values, axis, [(0, 1), (1, 0)])

    def shift(values, axis, step):
        size = lax.axis_size(axis)
        pairs = [(i, i + step) for i in range(size) if 0 <= i + step < size]
        return lax.ppermute(values, axis, pairs)

    (packed,) = call(
        pack_kernel,
        [((32, 6, 16, C), BF16)],
        [input_map[0], cotangent[0]],
        flops=4 * 10**8,
        moved=4 * 10**6,
        limit=60,
    )
    arrived = exchange(packed)

    (
        xs, start, projected, key_turned, probs, mixed_grad, resid_grad, tail_keep, tail_send,
        out_grad, gain_two_grad,
    ) = call(
        forward_kernel,
        [
            ((4, 10, 64, C), BF16),
            ((TOKENS, C), BF16),
            ((TOKENS, 3 * C), BF16),
            ((C, TOKENS), BF16),
            ((16, 256, 128), BF16),
            ((TOKENS, C), BF16),
            ((TOKENS, C), F32),
            ((1024, C), BF16),
            ((1024, C), BF16),
            ((C, C), F32),
            ((8, C), F32),
        ],
        [
            place, arrived, dw_rows,
            gain_one.reshape(1, C), w_qkv, w_out, gain_two.reshape(1, C), w_up, w_down,
        ],
        [
            ((TOKENS, C), BF16),
            ((TOKENS, C), BF16),
            ((TOKENS, C), BF16),
            ((TOKENS, C), BF16),
            ((TOKENS, FF), BF16),
            ((TOKENS, FF), BF16),
            ((2 * C, TOKENS), BF16),
            ((C, TOKENS), BF16),
            ((CHUNK, C), F32),
            ((CHUNK, C), F32),
            ((CHUNK, FF), F32),
            ((CHUNK, FF), F32),
        ],
        scalars=1,
        flops=8 * 10**9,
        moved=12 * 10**6,
        limit=36,
    )

    proj_grad, inputs, grad, gain_one_grad = call(
        backward_kernel,
        [((TOKENS, 3 * C), BF16), ((TOKENS, C), BF16), ((TOKENS, C), F32), ((8, C), F32)],
        [
            start, projected, key_turned, probs, mixed_grad, resid_grad, gain_one.reshape(1, C), w_qkv,
        ],
        [((C, TOKENS), BF16), ((C, TOKENS), BF16)],
        flops=5 * 10**9,
        moved=8 * 10**6,
        limit=32,
    )
    keep, send = call(
        sums_kernel,
        [((528, C), BF16), ((528, C), BF16)],
        [place, xs, inputs, proj_grad, grad, gain_one_grad, gain_two_grad, out_grad],
        scalars=1,
    )
    (pieces,) = call(
        pieces_kernel,
        [((4, 8 * JOINED, C), BF16)],
        [
            grad, tail_keep, swap(tail_send, "core"), keep, swap(send, "core"),
            jnp.asarray(groups_to_pieces(), BF16),
        ],
    )
    back = exchange(pieces.reshape(32, JOINED, C)).reshape(4, 8 * JOINED, C)
    factor = 1.0 / math.sqrt(TOKENS * 128)
    (partial,) = call(
        lambda x_ref, out_ref: partial_kernel(factor, x_ref, out_ref),
        [((SHARE, C), F32)],
        [back],
    )
    main, edges = (jnp.asarray(t, BF16) for t in pieces_to_tile())
    tile, first, last = call(
        unpack_kernel,
        [((18, 64, C), BF16), ((32, C), BF16), ((32, C), BF16)],
        [back, main, edges],
    )
    left, right = shift(last, "col", 1), shift(first, "col", -1)
    (shared,) = call(
        total_kernel,
        [((4, 8 * SHARE, C), BF16)],
        [partial, swap(partial, "yh")],
    )
    mine = exchange(shared.reshape(32, SHARE, C)).reshape(4, 8 * SHARE, C)
    (input_grad,) = call(
        tile_kernel,
        [((1, 16, 64, C), F32)],
        [tile, left, right, dw_rows],
        [((18, 80, C), F32)],
    )
    mine, input_grad = lax.optimization_barrier((mine, input_grad))
    other = swap(mine, "core")
    kernel_grad, gain_one_grad, qkv_grad, out_sum, gain_two_sum, up_grad, down_grad = call(
        outputs_kernel,
        [
            ((3, 3, C), F32),
            ((1, C), F32),
            ((C, 3 * C), F32),
            ((C, C), F32),
            ((1, C), F32),
            ((C, FF), F32),
            ((FF, C), F32),
        ],
        [place, mine, other],
        scalars=1,
        flops=10**6,
        moved=5 * 10**6,
    )
    return (
        input_grad,
        kernel_grad,
        gain_one_grad.reshape(C),
        qkv_grad,
        out_sum,
        gain_two_sum.reshape(C),
        up_grad,
        down_grad,
    )


def solution(mesh):
    cores = Mesh(mesh.devices.reshape(2, 2, 4, 8), ("yh", "core", "row", "col"))
    split = P(("yh", "core"), "row", "col", None)
    in_specs = (split, P(), P(), P(), P(), P(), P(), P(), split)
    out_specs = (split, P(), P(), P(), P(), P(), P(), P())
    return jax.shard_map(local, mesh=cores, in_specs=in_specs, out_specs=out_specs, check_vma=False)
```

```python
import math

import jax
import jax.numpy as jnp
import numpy as np
from jax import lax
from jax.experimental import pallas as pl
from jax.experimental.pallas import tpu as pltpu
from jax.sharding import Mesh
from jax.sharding import PartitionSpec as P

HEADS = 8
C = 256
FF = 1024
PIECE = 40
SUMS = 48
JOINED = PIECE + SUMS
SHARE = SUMS + 8
norm_eps = 1e-05
gelu_coef = 0.7978845608028654
cubic_coef = 0.044715
HEAD_SCALE = 1.0 / math.sqrt(C // HEADS)
TOKENS = 1024
AHEAD = 8
CHUNK = 1024
ROWS = 64
SPAN = 16

F32 = jnp.float32
BF16 = jnp.bfloat16


def positions(size):
    return tuple(lax.broadcasted_iota(jnp.int32, (size, size), axis) for axis in range(2))


def as_matrix(chosen):
    return jnp.where(chosen, 1.0, 0.0).astype(BF16)


def tile_to_columns():
    to, of = positions(256)
    return as_matrix(((to >> 4) == (of & 15)) & ((to & 15) == (of >> 4)))


def sources_to_groups(shift):
    to, of = positions(128)
    same = ((to >> 4) == (of & 7)) & (((to >> 3) & 1) == ((of >> 3) & 1))
    return as_matrix(same & ((of >> 4) == (to & 7) + shift))


def head_mask():
    row, lane = positions(256)
    return as_matrix((row >> 6) == ((lane >> 5) & 3))


def turned_head_mask():
    lane, row = (lax.broadcasted_iota(jnp.int32, (128, 256), axis) for axis in range(2))
    return as_matrix((row >> 6) == (lane >> 5))


def groups_to_pieces():
    out = np.zeros((8 * PIECE, 384), np.float32)
    for c in range(8):
        for j in range(2):
            out[c * PIECE + 18 * j, 256 + 8 * j + c] = 1
            out[c * PIECE + 18 * j + 17, 272 + 8 * j + c] = 1
            for row in range(16):
                a, p = divmod(row, 8)
                out[c * PIECE + 18 * j + 1 + row, (j * 8 + p) * 16 + a * 8 + c] = 1
        out[c * PIECE + 36, 288 + c] = 1
    return out


def pieces_to_tile():
    main = np.zeros((288, 8 * PIECE), np.float32)
    edges = np.zeros((2, 32, 8 * PIECE), np.float32)
    for row in range(18):
        for q in range(16):
            main[row * 16 + q, (q // 2) * PIECE + (q % 2) * 18 + row] = 1
        edges[0, row, row] = 1
        edges[1, row, 7 * PIECE + 18 + row] = 1
    return main, edges


def dot(a, b):
    return lax.dot_general(a, b, (((1,), (0,)), ((), ())), preferred_element_type=F32)


def dot_nt(a, b):
    return lax.dot_general(a, b, (((1,), (1,)), ((), ())), preferred_element_type=F32)


def dot_tn(a, b):
    return lax.dot_general(a, b, (((0,), (0,)), ((), ())), preferred_element_type=F32)


def norm(values):
    center = values - jnp.mean(values, axis=-1, keepdims=True)
    inverse = lax.rsqrt(jnp.mean(center * center, axis=-1, keepdims=True) + norm_eps)
    return center * inverse, inverse


def norm_back(upstream, normed, inverse, gain):
    scaled = upstream * gain
    return inverse * (
        scaled
        - jnp.mean(scaled, axis=-1, keepdims=True)
        - normed * jnp.mean(scaled * normed, axis=-1, keepdims=True)
    )


def fold_rows(values):
    return jnp.sum(values.reshape(-1, 8, values.shape[-1]), axis=0)


def side_by_side(rows):
    return jnp.concatenate([rows[0:64], rows[64:128]], axis=1)


def stacked(rows):
    return jnp.concatenate([rows[:, 0:128], rows[:, 128:256]], axis=0)


def block_diagonal(rows):
    zeros = jnp.zeros((64, 128), rows.dtype)
    upper = jnp.concatenate([rows[0:64], zeros], axis=1)
    return jnp.concatenate([upper, jnp.concatenate([zeros, rows[64:128]], axis=1)], axis=0)


def by_head(rows, mask):
    return jnp.concatenate([side_by_side(rows)] * 4, axis=0) * mask


def by_lane_half(columns, lower):
    return jnp.concatenate([columns * lower, columns * (1 - lower)], axis=0)


def by_head_turned(columns, lower, turned_mask):
    swapped = jnp.concatenate([columns[:, 64:128], columns[:, 0:64]], axis=1)
    parts = []
    for first, second in ((columns, swapped), (swapped, columns)):
        part = first * lower + second * (1 - lower)
        parts.append(jnp.concatenate([part, part], axis=1) * turned_mask)
    return jnp.concatenate(parts, axis=0)


def own_half(blocks, lower):
    return jnp.where(lower, blocks[0:128], blocks[128:256]).astype(BF16)


def lane_half():
    return lax.broadcasted_iota(jnp.int32, (1, 128), 1) < 64


def attend_unit(query_turned, key, value_turned, lower, mask, turned_mask):
    low = lower.astype(F32).astype(BF16)
    scores = dot(by_head(key, mask), by_lane_half(query_turned, low)).reshape(4, 64, 128) * HEAD_SCALE
    expos = jnp.exp(scores - jnp.max(scores, axis=1, keepdims=True))
    probs = expos * (1.0 / jnp.sum(expos, axis=1, keepdims=True))
    probs = probs.reshape(256, 128).astype(BF16)
    mixed = dot(by_head_turned(value_turned, low, turned_mask), probs)
    return probs, own_half(mixed, lower)


def attend_unit_back(
    query, key_turned, value, probs, upstream, upstream_turned, lower, mask, turned_mask, wide_mask
):
    low = lower.astype(F32).astype(BF16)
    wide = probs.astype(F32).reshape(4, 64, 128)
    prob_grad = dot(by_head(value, mask), by_lane_half(upstream_turned, low)).reshape(4, 64, 128)
    centre = jnp.sum(wide * prob_grad, axis=1, keepdims=True)
    score_grad = (wide * (prob_grad - centre) * HEAD_SCALE).reshape(256, 128).astype(BF16)
    query_grad = own_half(dot(by_head_turned(key_turned, low, turned_mask), score_grad), lower)
    key_grad = jnp.sum((dot(score_grad, block_diagonal(query)) * wide_mask).reshape(4, 64, 256), axis=0)
    value_grad = jnp.sum((dot(probs, block_diagonal(upstream)) * wide_mask).reshape(4, 64, 256), axis=0)
    return query_grad, stacked(key_grad).astype(BF16), stacked(value_grad).astype(BF16)


def pack_kernel(x_ref, cot_ref, out_ref):
    perm = tile_to_columns()
    for block in range(4):
        tokens = x_ref[:, 16 * block : 16 * block + 16, :].reshape(256, C)
        columns = dot(perm, tokens).astype(BF16).reshape(16, 16, C)
        tokens = cot_ref[:, 16 * block : 16 * block + 16, :].reshape(256, C)
        cot_columns = dot(perm, tokens).astype(BF16).reshape(16, 16, C)
        for i in range(16):
            q = 16 * block + i
            k, odd = divmod(q, 2)
            out_ref[k, 4 + odd] = cot_columns[i]
            if odd:
                out_ref[k, 2] = columns[i]
                out_ref[(k + 1) % 32, 0] = columns[i]
            else:
                out_ref[k, 1] = columns[i]
                out_ref[(k - 1) % 32, 3] = columns[i]


def store_halves(core, lower, upper, keep_ref, send_ref, rows):
    keep_ref[rows, :] = jnp.where(core == 0, lower, upper).astype(BF16)
    send_ref[rows, :] = jnp.where(core == 0, upper, lower).astype(BF16)


def forward_kernel(
    place_ref, x_ref, dw_ref, gain_one_ref, w_qkv_ref, w_out_ref, gain_two_ref,
    w_up_ref, w_down_ref,
    xs_ref, in_ref, inputs_ref, proj_ref, key_turned_ref, probs_ref, mixed_grad_ref, resid_grad_ref, keep_ref, send_ref,
    out_grad_ref, gain_grad_ref,
    cot_s, mixed_s, two_s, low_s, act_s, pre_s, turned_s, mixed_turned_s,
    narrow_s, normed_s, wide_s, cot_wide_s,
):
    owner = place_ref[0]
    core = place_ref[1]
    first = sources_to_groups(jnp.where(owner == 0, -1, 0))
    last = sources_to_groups(jnp.where(owner == 31, 1, 0))
    plain = sources_to_groups(0)

    for r in range(4):
        for j in range(4):
            perm = first if j == 0 else (last if j == 3 else plain)
            tokens = x_ref[8 * r : 8 * r + 8, j].reshape(128, C)
            moved = dot(perm, tokens).astype(BF16).reshape(8, 16, C)
            for p in range(8):
                xs_ref[j, p + 1, 16 * r : 16 * r + 16, :] = moved[p]
    edge = jnp.zeros((8, C), F32)
    for j in range(4):
        lowest = xs_ref[j, 8].astype(F32)
        xs_ref[j, 0] = jnp.concatenate([edge, lowest[:56]], axis=0).astype(BF16)
        highest = xs_ref[j, 1].astype(F32)
        xs_ref[j, 9] = jnp.concatenate([highest[8:], edge], axis=0).astype(BF16)

    gain_one = gain_one_ref[...]

    def conv(g):
        j, p = g // 8, g % 8
        total = xs_ref[j + 1, p + 1].astype(F32)
        for u in range(3):
            for v in range(3):
                total = total + dw_ref[3 * u + v : 3 * u + v + 1, :] * xs_ref[j + v, p + u].astype(F32)
        start = total.astype(BF16)
        rows = slice(64 * g, 64 * g + 64)
        in_ref[rows, :] = start
        normed, _ = norm(start.astype(F32))
        inputs_ref[rows, :] = (normed * gain_one).astype(BF16)


    for start in range(2):
        for g in range(8 * start, 8 * start + 8):
            conv(g)
        rows = slice(512 * start, 512 * start + 512)
        proj_ref[rows, :] = dot(inputs_ref[rows, :], w_qkv_ref[...]).astype(BF16)

    turned_s[0:256, :] = proj_ref[:, 0:256].T
    turned_s[256:512, :] = proj_ref[:, 512:768].T
    key_turned_ref[...] = proj_ref[:, 256:512].T
    mask = head_mask()
    turned_mask = turned_head_mask()
    lower = lane_half()

    def attend(i, carry):
        units = []
        for n in range(AHEAD):
            pair = i * AHEAD + n
            rows = pl.ds(pl.multiple_of(pair * 128, 128), 128)
            for side in range(2):
                lanes = slice(128 * side, 128 * side + 128)
                query = turned_s[lanes, rows]
                key = proj_ref[rows, 256 + 128 * side : 384 + 128 * side]
                value = turned_s[256 + 128 * side : 384 + 128 * side, rows]
                units.append((2 * pair + side, lanes, rows, (query, key, value)))
        results = [attend_unit(*parts, lower, mask, turned_mask) for _, _, _, parts in units]
        for (unit, lanes, rows, _), (probs, mixed) in zip(units, results):
            probs_ref[unit] = probs
            mixed_turned_s[lanes, rows] = mixed
        return carry

    lax.fori_loop(0, 8 // AHEAD, attend, 0)
    mixed_s[...] = mixed_turned_s[...].T

    for r in range(4):
        for j in range(2):
            tokens = x_ref[8 * r : 8 * r + 8, 4 + j].reshape(128, C)
            moved = dot(plain, tokens).astype(BF16).reshape(8, 16, C)
            for p in range(8):
                cot_s[(j * 8 + p) * 64 + 16 * r : (j * 8 + p) * 64 + 16 * r + 16, :] = moved[p]

    gain_two = gain_two_ref[...]

    def tail(i, gain_grad):
        rows = pl.ds(pl.multiple_of(i * CHUNK, CHUNK), CHUNK)
        narrow_s[...] = dot(mixed_s[rows, :], w_out_ref[...])
        inverses = []
        for n in range(CHUNK // ROWS):
            part = slice(ROWS * n, ROWS * n + ROWS)
            own = pl.ds(pl.multiple_of(i * CHUNK + ROWS * n, ROWS), ROWS)
            normed, inverse = norm(in_ref[own, :].astype(F32) + narrow_s[part, :])
            inverses.append(inverse)
            normed_s[part, :] = normed
            two_s[own, :] = (normed * gain_two).astype(BF16)
        wide_s[...] = dot(two_s[rows, :], w_up_ref[...])
        cot_wide_s[...] = dot_nt(cot_s[rows, :], w_down_ref[...])
        for n in range(CHUNK // SPAN):
            part = slice(SPAN * n, SPAN * n + SPAN)
            own = pl.ds(pl.multiple_of(i * CHUNK + SPAN * n, SPAN), SPAN)
            for block in range(4):
                columns = slice(256 * block, 256 * block + 256)
                pre = wide_s[part, columns]
                square = pre * pre
                tangent = jnp.tanh(pre * (gelu_coef + (gelu_coef * cubic_coef) * square))
                half = 0.5 + 0.5 * tangent
                act = pre * half
                act_s[own, columns] = act.astype(BF16)
                slope = half + (act - act * half) * (
                    2.0 * gelu_coef + (6.0 * gelu_coef * cubic_coef) * square
                )
                pre_s[own, columns] = (cot_wide_s[part, columns] * slope).astype(BF16)
        narrow_s[...] = dot_nt(pre_s[rows, :], w_up_ref[...])
        for n in range(CHUNK // ROWS):
            part = slice(ROWS * n, ROWS * n + ROWS)
            own = pl.ds(pl.multiple_of(i * CHUNK + ROWS * n, ROWS), ROWS)
            in_grad = narrow_s[part, :]
            normed = normed_s[part, :]
            back = norm_back(in_grad, normed, inverses[n], gain_two)
            resid_grad = cot_s[own, :].astype(F32) + back
            resid_grad_ref[own, :] = resid_grad
            low_s[own, :] = resid_grad.astype(BF16)
            gain_grad = gain_grad + fold_rows(in_grad * normed)
        mixed_grad_ref[rows, :] = dot_nt(low_s[rows, :], w_out_ref[...]).astype(BF16)
        return gain_grad

    gain_grad = lax.fori_loop(0, TOKENS // CHUNK, tail, jnp.zeros((8, C), F32))
    gain_grad_ref[...] = gain_grad

    cot_turned = cot_s[...].T
    two_turned = two_s[...].T
    for block in range(4):
        columns = slice(256 * block, 256 * block + 256)
        down = dot(cot_turned, act_s[:, columns]).T
        up = dot(two_turned, pre_s[:, columns])
        store_halves(core, down, up, keep_ref, send_ref, slice(256 * block, 256 * block + 256))
    out_grad_ref[...] = dot(mixed_turned_s[...], low_s[...])


def backward_kernel(
    place_ref, inputs_ref, proj_ref, key_turned_ref, probs_ref, mixed_grad_ref, out_grad_ref,
    proj_grad_ref, keep_ref, send_ref,
    upstream_s, query_grad_s,
):
    core = place_ref[1]
    upstream_s[...] = mixed_grad_ref[...].T
    mask = head_mask()
    wide_mask = mask.astype(F32)
    turned_mask = turned_head_mask()
    lower = lane_half()

    def attend_back(i, carry):
        units = []
        for n in range(AHEAD):
            pair = i * AHEAD + n
            rows = pl.ds(pl.multiple_of(pair * 128, 128), 128)
            for side in range(2):
                lanes = slice(128 * side, 128 * side + 128)
                parts = (
                    proj_ref[rows, lanes],
                    key_turned_ref[lanes, rows],
                    proj_ref[rows, 512 + 128 * side : 640 + 128 * side],
                    probs_ref[2 * pair + side],
                    mixed_grad_ref[rows, lanes],
                    upstream_s[lanes, rows],
                )
                units.append((side, lanes, rows, parts))
        results = [
            attend_unit_back(*parts, lower, mask, turned_mask, wide_mask) for _, _, _, parts in units
        ]
        for (side, lanes, rows, _), grads in zip(units, results):
            query_grad_s[lanes, rows] = grads[0]
            proj_grad_ref[rows, 256 + 128 * side : 384 + 128 * side] = grads[1]
            proj_grad_ref[rows, 512 + 128 * side : 640 + 128 * side] = grads[2]
        return carry

    lax.fori_loop(0, 8 // AHEAD, attend_back, 0)
    proj_grad_ref[:, 0:256] = query_grad_s[...].T

    inputs_turned = inputs_ref[...].T
    terms = [
        dot(inputs_turned, proj_grad_ref[:, 256 * block : 256 * block + 256])
        for block in range(3)
    ]
    terms.append(out_grad_ref[...])
    for block in range(2):
        rows = slice(256 * block, 256 * block + 256)
        store_halves(core, terms[block], terms[2 + block], keep_ref, send_ref, rows)


def head_kernel(
    xs_ref, in_ref, proj_grad_ref, resid_grad_ref, gain_two_grad_ref, gain_one_ref, w_qkv_ref,
    grad_ref, small_ref,
):
    gain_one = gain_one_ref[...]

    def head(i, gain_grad):
        rows = pl.ds(pl.multiple_of(i * 512, 512), 512)
        normed, inverse = norm(in_ref[rows, :].astype(F32))
        in_grad = dot_nt(proj_grad_ref[rows, :], w_qkv_ref[...])
        grad_ref[rows, :] = resid_grad_ref[rows, :] + norm_back(in_grad, normed, inverse, gain_one)
        return gain_grad + fold_rows(in_grad * normed)

    gain_grad = lax.fori_loop(0, 2, head, jnp.zeros((8, C), F32), unroll=2)

    def taps(g, sums):
        j, p = g // 8, g % 8
        grad = grad_ref[pl.ds(pl.multiple_of(g * 64, 64), 64), :]
        return tuple(
            sums[3 * u + v] + fold_rows(grad * xs_ref[j + v, p + u].astype(F32))
            for u in range(3)
            for v in range(3)
        )

    kernel_grad = lax.fori_loop(0, 16, taps, (jnp.zeros((8, C), F32),) * 9, unroll=4)
    small = [jnp.sum(term, axis=0, keepdims=True) for term in kernel_grad]
    small.append(jnp.sum(gain_grad, axis=0, keepdims=True))
    small.append(jnp.sum(gain_two_grad_ref[...], axis=0, keepdims=True))
    small.append(jnp.zeros((5, C), F32))
    small_ref[...] = jnp.concatenate(small, axis=0)


def pieces_kernel(
    grad_ref, small_ref, tail_ref, other_tail_ref, head_ref, other_head_ref, perm_ref, out_ref
):
    perm = perm_ref[...]
    edge = jnp.zeros((8, C), F32)
    for r in range(4):
        parts = [grad_ref[64 * g + 16 * r : 64 * g + 16 * r + 16, :] for g in range(16)]
        for j in range(2):
            lowest = 64 * (8 * j + 7) + 16 * r - 8
            parts.append(grad_ref[lowest : lowest + 8, :] if r > 0 else edge)
        for j in range(2):
            highest = 64 * 8 * j + 16 * r + 16
            parts.append(grad_ref[highest : highest + 8, :] if r < 3 else edge)
        parts.append(small_ref[8 * r : 8 * r + 8, :] if r < 2 else edge)
        parts.append(jnp.zeros((88, C), F32))
        tokens = jnp.concatenate(parts, axis=0).astype(BF16)
        moved = dot(perm, tokens).reshape(8, PIECE, C)
        rows = slice(256 * r, 256 * r + 256)
        tail = tail_ref[rows, :].astype(F32) + other_tail_ref[rows, :].astype(F32)
        rows = slice(128 * r, 128 * r + 128)
        head = head_ref[rows, :].astype(F32) + other_head_ref[rows, :].astype(F32)
        joined = [moved, tail.reshape(8, 32, C), head.reshape(8, 16, C)]
        joined = jnp.concatenate(joined, axis=1)
        out_ref[r] = joined.reshape(8 * JOINED, C).astype(BF16)


def partial_kernel(factor, x_ref, out_ref):
    total = jnp.zeros((SHARE, C), F32)
    for r in range(4):
        pieces = jnp.sum(x_ref[r].astype(F32).reshape(8, JOINED, C), axis=0)
        total = total + jnp.concatenate([pieces[PIECE:], pieces[32:40]], axis=0)
    out_ref[...] = total * factor


def total_kernel(mine_ref, other_ref, out_ref):
    total = mine_ref[...] + other_ref[...]
    rows = jnp.concatenate([total] * 8, axis=0).astype(BF16)
    for r in range(4):
        out_ref[r] = rows


def unpack_kernel(pieces_ref, main_ref, edges_ref, tile_ref, first_ref, last_ref):
    for block in range(4):
        pieces = pieces_ref[block].astype(F32).reshape(8, JOINED, C)
        pieces = pieces[:, :PIECE].reshape(8 * PIECE, C).astype(BF16)
        columns = dot(main_ref[...], pieces).astype(BF16)
        tile_ref[:, 16 * block : 16 * block + 16, :] = columns.reshape(18, 16, C)
        if block == 0:
            first_ref[...] = dot(edges_ref[0], pieces).astype(BF16)
        if block == 3:
            last_ref[...] = dot(edges_ref[1], pieces).astype(BF16)


def tile_kernel(tile_ref, left_ref, right_ref, dw_ref, out_ref, wide):
    wide[:, 8:72, :] = tile_ref[...].astype(F32)
    left = left_ref[...].astype(F32)
    right = right_ref[...].astype(F32)
    for i in range(18):
        wide[i, 7:8, :] = left[i : i + 1]
        wide[i, 72:73, :] = right[i : i + 1]

    def row(i, carry):
        rows = [wide[i + 2 - u] for u in range(3)]
        total = wide[i + 1, 8:72, :]
        for v in range(3):
            term = dw_ref[v : v + 1, :] * rows[0]
            for u in range(1, 3):
                term = term + dw_ref[3 * u + v : 3 * u + v + 1, :] * rows[u]
            total = total + term[9 - v : 73 - v, :]
        out_ref[0, i] = total
        return carry

    lax.fori_loop(0, 16, row, 0)


def outputs_kernel(
    place_ref, mine_ref, other_ref,
    kernel_ref, gain_one_ref, qkv_ref, out_ref, gain_two_ref, up_ref, down_ref,
):
    own = place_ref[1] == 0
    small = []
    for r in range(4):
        mine = mine_ref[r].astype(F32).reshape(8, SHARE, C)
        other = other_ref[r].astype(F32).reshape(8, SHARE, C)
        lower = jnp.where(own, mine, other)
        upper = jnp.where(own, other, mine)
        down_ref[256 * r : 256 * r + 256, :] = lower[:, 0:32].reshape(256, C)
        up_ref[:, 256 * r : 256 * r + 256] = upper[:, 0:32].reshape(256, C)
        rows = slice(128 * (r % 2), 128 * (r % 2) + 128)
        block = r // 2
        qkv_ref[rows, 256 * block : 256 * block + 256] = lower[:, 32:48].reshape(128, C)
        if r < 2:
            qkv_ref[rows, 512:768] = upper[:, 32:48].reshape(128, C)
        else:
            out_ref[rows, :] = upper[:, 32:48].reshape(128, C)
        if r < 2:
            small.append((mine + other)[:, 48:56])
    small = jnp.concatenate([part[c, 4:5] for part in small for c in range(8)], axis=0)
    for u in range(3):
        kernel_ref[u] = small[3 * u : 3 * u + 3]
    gain_one_ref[...] = small[9:10]
    gain_two_ref[...] = small[10:11]


VMEM = pl.BlockSpec(memory_space=pltpu.VMEM)
SMEM = pl.BlockSpec(memory_space=pltpu.SMEM)


def call(kernel, outs, operands, scratch=(), scalars=0, flops=0, moved=0, limit=24):
    return pl.pallas_call(
        kernel,
        out_shape=tuple(jax.ShapeDtypeStruct(shape, dtype) for shape, dtype in outs),
        in_specs=[SMEM] * scalars + [VMEM] * (len(operands) - scalars),
        out_specs=tuple(VMEM for _ in outs),
        scratch_shapes=[pltpu.VMEM(shape, dtype) for shape, dtype in scratch],
        compiler_params=pltpu.CompilerParams(vmem_limit_bytes=limit * 2**20),
        cost_estimate=pl.CostEstimate(flops=flops, bytes_accessed=moved, transcendentals=0),
    )(*operands)


def local(input_map, dw_kernel, gain_one, w_qkv, w_out, gain_two, w_up, w_down, cotangent):
    owner = lax.axis_index("row") * 8 + lax.axis_index("col")
    core = lax.axis_index("core")
    place = jnp.stack([owner, core]).astype(jnp.int32)
    dw_rows = dw_kernel.reshape(9, C).astype(F32)

    def exchange(stacked):
        return lax.all_to_all(stacked, ("row", "col"), split_axis=0, concat_axis=0, tiled=True)

    def swap(values, axis):
        return lax.ppermute(values, axis, [(0, 1), (1, 0)])

    def shift(values, axis, step):
        size = lax.axis_size(axis)
        pairs = [(i, i + step) for i in range(size) if 0 <= i + step < size]
        return lax.ppermute(values, axis, pairs)

    (packed,) = call(
        pack_kernel,
        [((32, 6, 16, C), BF16)],
        [input_map[0], cotangent[0]],
        flops=4 * 10**8,
        moved=4 * 10**6,
        limit=60,
    )
    arrived = exchange(packed)

    (
        xs, start, inputs, projected, key_turned, probs, mixed_grad, resid_grad, tail_keep, tail_send,
        out_grad, gain_two_grad,
    ) = call(
        forward_kernel,
        [
            ((4, 10, 64, C), BF16),
            ((TOKENS, C), BF16),
            ((TOKENS, C), BF16),
            ((TOKENS, 3 * C), BF16),
            ((C, TOKENS), BF16),
            ((16, 256, 128), BF16),
            ((TOKENS, C), BF16),
            ((TOKENS, C), F32),
            ((1024, C), BF16),
            ((1024, C), BF16),
            ((C, C), F32),
            ((8, C), F32),
        ],
        [
            place, arrived, dw_rows,
            gain_one.reshape(1, C), w_qkv, w_out, gain_two.reshape(1, C), w_up, w_down,
        ],
        [
            ((TOKENS, C), BF16),
            ((TOKENS, C), BF16),
            ((TOKENS, C), BF16),
            ((TOKENS, C), BF16),
            ((TOKENS, FF), BF16),
            ((TOKENS, FF), BF16),
            ((2 * C, TOKENS), BF16),
            ((C, TOKENS), BF16),
            ((CHUNK, C), F32),
            ((CHUNK, C), F32),
            ((CHUNK, FF), F32),
            ((CHUNK, FF), F32),
        ],
        scalars=1,
        flops=8 * 10**9,
        moved=12 * 10**6,
        limit=36,
    )

    proj_grad, keep, send = call(
        backward_kernel,
        [((TOKENS, 3 * C), BF16), ((512, C), BF16), ((512, C), BF16)],
        [place, inputs, projected, key_turned, probs, mixed_grad, out_grad],
        [((C, TOKENS), BF16), ((C, TOKENS), BF16)],
        scalars=1,
        flops=5 * 10**9,
        moved=8 * 10**6,
        limit=32,
    )
    grad, small = call(
        head_kernel,
        [((TOKENS, C), F32), ((16, C), F32)],
        [xs, start, proj_grad, resid_grad, gain_two_grad, gain_one.reshape(1, C), w_qkv],
    )
    (pieces,) = call(
        pieces_kernel,
        [((4, 8 * JOINED, C), BF16)],
        [
            grad, small, tail_keep, swap(tail_send, "core"), keep, swap(send, "core"),
            jnp.asarray(groups_to_pieces(), BF16),
        ],
    )
    back = exchange(pieces.reshape(32, JOINED, C)).reshape(4, 8 * JOINED, C)
    factor = 1.0 / math.sqrt(TOKENS * 128)
    (partial,) = call(
        lambda x_ref, out_ref: partial_kernel(factor, x_ref, out_ref),
        [((SHARE, C), F32)],
        [back],
    )
    main, edges = (jnp.asarray(t, BF16) for t in pieces_to_tile())
    tile, first, last = call(
        unpack_kernel,
        [((18, 64, C), BF16), ((32, C), BF16), ((32, C), BF16)],
        [back, main, edges],
    )
    left, right = shift(last, "col", 1), shift(first, "col", -1)
    (shared,) = call(
        total_kernel,
        [((4, 8 * SHARE, C), BF16)],
        [partial, swap(partial, "yh")],
    )
    mine = exchange(shared.reshape(32, SHARE, C)).reshape(4, 8 * SHARE, C)
    (input_grad,) = call(
        tile_kernel,
        [((1, 16, 64, C), F32)],
        [tile, left, right, dw_rows],
        [((18, 80, C), F32)],
    )
    mine, input_grad = lax.optimization_barrier((mine, input_grad))
    other = swap(mine, "core")
    kernel_grad, gain_one_grad, qkv_grad, out_sum, gain_two_sum, up_grad, down_grad = call(
        outputs_kernel,
        [
            ((3, 3, C), F32),
            ((1, C), F32),
            ((C, 3 * C), F32),
            ((C, C), F32),
            ((1, C), F32),
            ((C, FF), F32),
            ((FF, C), F32),
        ],
        [place, mine, other],
        scalars=1,
        flops=10**6,
        moved=5 * 10**6,
    )
    return (
        input_grad,
        kernel_grad,
        gain_one_grad.reshape(C),
        qkv_grad,
        out_sum,
        gain_two_sum.reshape(C),
        up_grad,
        down_grad,
    )


def solution(mesh):
    cores = Mesh(mesh.devices.reshape(2, 2, 4, 8), ("yh", "core", "row", "col"))
    split = P(("yh", "core"), "row", "col", None)
    in_specs = (split, P(), P(), P(), P(), P(), P(), P(), split)
    out_specs = (split, P(), P(), P(), P(), P(), P(), P())
    return jax.shard_map(local, mesh=cores, in_specs=in_specs, out_specs=out_specs, check_vma=False)
```

```python
import math

import jax
import jax.numpy as jnp
import numpy as np
from jax import lax
from jax.experimental import pallas as pl
from jax.experimental.pallas import tpu as pltpu
from jax.sharding import Mesh
from jax.sharding import PartitionSpec as P

HEADS = 8
C = 256
FF = 1024
PIECE = 40
SUMS = 48
JOINED = PIECE + SUMS
SHARE = SUMS + 8
norm_eps = 1e-05
gelu_coef = 0.7978845608028654
cubic_coef = 0.044715
HEAD_SCALE = 1.0 / math.sqrt(C // HEADS)
TOKENS = 1024
AHEAD = 8
CHUNK = 1024
ROWS = 64
SPAN = 16

F32 = jnp.float32
BF16 = jnp.bfloat16


def positions(size):
    return tuple(lax.broadcasted_iota(jnp.int32, (size, size), axis) for axis in range(2))


def as_matrix(chosen):
    return jnp.where(chosen, 1.0, 0.0).astype(BF16)


def tile_to_columns():
    to, of = positions(256)
    return as_matrix(((to >> 4) == (of & 15)) & ((to & 15) == (of >> 4)))


def sources_to_groups(shift):
    to, of = positions(128)
    same = ((to >> 4) == (of & 7)) & (((to >> 3) & 1) == ((of >> 3) & 1))
    return as_matrix(same & ((of >> 4) == (to & 7) + shift))


def head_mask():
    row, lane = positions(256)
    return as_matrix((row >> 6) == ((lane >> 5) & 3))


def turned_head_mask():
    lane, row = (lax.broadcasted_iota(jnp.int32, (128, 256), axis) for axis in range(2))
    return as_matrix((row >> 6) == (lane >> 5))


def groups_to_pieces():
    out = np.zeros((8 * PIECE, 384), np.float32)
    for c in range(8):
        for j in range(2):
            out[c * PIECE + 18 * j, 256 + 8 * j + c] = 1
            out[c * PIECE + 18 * j + 17, 272 + 8 * j + c] = 1
            for row in range(16):
                a, p = divmod(row, 8)
                out[c * PIECE + 18 * j + 1 + row, (j * 8 + p) * 16 + a * 8 + c] = 1
        out[c * PIECE + 36, 288 + c] = 1
    return out


def pieces_to_tile():
    main = np.zeros((288, 8 * PIECE), np.float32)
    edges = np.zeros((2, 32, 8 * PIECE), np.float32)
    for row in range(18):
        for q in range(16):
            main[row * 16 + q, (q // 2) * PIECE + (q % 2) * 18 + row] = 1
        edges[0, row, row] = 1
        edges[1, row, 7 * PIECE + 18 + row] = 1
    return main, edges


def dot(a, b):
    return lax.dot_general(a, b, (((1,), (0,)), ((), ())), preferred_element_type=F32)


def dot_nt(a, b):
    return lax.dot_general(a, b, (((1,), (1,)), ((), ())), preferred_element_type=F32)


def dot_tn(a, b):
    return lax.dot_general(a, b, (((0,), (0,)), ((), ())), preferred_element_type=F32)


def norm(values):
    center = values - jnp.mean(values, axis=-1, keepdims=True)
    inverse = lax.rsqrt(jnp.mean(center * center, axis=-1, keepdims=True) + norm_eps)
    return center * inverse, inverse


def norm_back(upstream, normed, inverse, gain):
    scaled = upstream * gain
    return inverse * (
        scaled
        - jnp.mean(scaled, axis=-1, keepdims=True)
        - normed * jnp.mean(scaled * normed, axis=-1, keepdims=True)
    )


def fold_rows(values):
    return jnp.sum(values.reshape(-1, 8, values.shape[-1]), axis=0)


def side_by_side(rows):
    return jnp.concatenate([rows[0:64], rows[64:128]], axis=1)


def stacked(rows):
    return jnp.concatenate([rows[:, 0:128], rows[:, 128:256]], axis=0)


def block_diagonal(rows):
    zeros = jnp.zeros((64, 128), rows.dtype)
    upper = jnp.concatenate([rows[0:64], zeros], axis=1)
    return jnp.concatenate([upper, jnp.concatenate([zeros, rows[64:128]], axis=1)], axis=0)


def by_head(rows, mask):
    return jnp.concatenate([side_by_side(rows)] * 4, axis=0) * mask


def by_lane_half(columns, lower):
    return jnp.concatenate([columns * lower, columns * (1 - lower)], axis=0)


def by_head_turned(columns, lower, turned_mask):
    swapped = jnp.concatenate([columns[:, 64:128], columns[:, 0:64]], axis=1)
    parts = []
    for first, second in ((columns, swapped), (swapped, columns)):
        part = first * lower + second * (1 - lower)
        parts.append(jnp.concatenate([part, part], axis=1) * turned_mask)
    return jnp.concatenate(parts, axis=0)


def own_half(blocks, lower):
    return jnp.where(lower, blocks[0:128], blocks[128:256]).astype(BF16)


def lane_half():
    return lax.broadcasted_iota(jnp.int32, (1, 128), 1) < 64


def attend_unit(query_turned, key, value_turned, lower, mask, turned_mask):
    low = lower.astype(F32).astype(BF16)
    scores = dot(by_head(key, mask), by_lane_half(query_turned, low)).reshape(4, 64, 128) * HEAD_SCALE
    expos = jnp.exp(scores - jnp.max(scores, axis=1, keepdims=True))
    probs = expos * (1.0 / jnp.sum(expos, axis=1, keepdims=True))
    probs = probs.reshape(256, 128).astype(BF16)
    mixed = dot(by_head_turned(value_turned, low, turned_mask), probs)
    return probs, own_half(mixed, lower)


def attend_unit_back(
    query, key_turned, value, probs, upstream, upstream_turned, lower, mask, turned_mask, wide_mask
):
    low = lower.astype(F32).astype(BF16)
    wide = probs.astype(F32).reshape(4, 64, 128)
    prob_grad = dot(by_head(value, mask), by_lane_half(upstream_turned, low)).reshape(4, 64, 128)
    centre = jnp.sum(wide * prob_grad, axis=1, keepdims=True)
    score_grad = (wide * (prob_grad - centre) * HEAD_SCALE).reshape(256, 128).astype(BF16)
    query_grad = own_half(dot(by_head_turned(key_turned, low, turned_mask), score_grad), lower)
    key_grad = jnp.sum((dot(score_grad, block_diagonal(query)) * wide_mask).reshape(4, 64, 256), axis=0)
    value_grad = jnp.sum((dot(probs, block_diagonal(upstream)) * wide_mask).reshape(4, 64, 256), axis=0)
    return query_grad, stacked(key_grad).astype(BF16), stacked(value_grad).astype(BF16)


def pack_kernel(x_ref, cot_ref, out_ref):
    perm = tile_to_columns()
    for block in range(4):
        tokens = x_ref[:, 16 * block : 16 * block + 16, :].reshape(256, C)
        columns = dot(perm, tokens).astype(BF16).reshape(16, 16, C)
        tokens = cot_ref[:, 16 * block : 16 * block + 16, :].reshape(256, C)
        cot_columns = dot(perm, tokens).astype(BF16).reshape(16, 16, C)
        for i in range(16):
            q = 16 * block + i
            k, odd = divmod(q, 2)
            out_ref[k, 4 + odd] = cot_columns[i]
            if odd:
                out_ref[k, 2] = columns[i]
                out_ref[(k + 1) % 32, 0] = columns[i]
            else:
                out_ref[k, 1] = columns[i]
                out_ref[(k - 1) % 32, 3] = columns[i]


def store_halves(core, lower, upper, keep_ref, send_ref, rows):
    keep_ref[rows, :] = jnp.where(core == 0, lower, upper).astype(BF16)
    send_ref[rows, :] = jnp.where(core == 0, upper, lower).astype(BF16)


def forward_kernel(
    place_ref, x_ref, dw_ref, gain_one_ref, w_qkv_ref, w_out_ref, gain_two_ref,
    w_up_ref, w_down_ref,
    xs_ref, in_ref, inputs_ref, proj_ref, key_turned_ref, probs_ref, mixed_grad_ref, resid_grad_ref, keep_ref, send_ref,
    out_grad_ref, gain_grad_ref,
    cot_s, mixed_s, two_s, low_s, act_s, pre_s, turned_s, mixed_turned_s,
    narrow_s, normed_s, wide_s, cot_wide_s,
):
    owner = place_ref[0]
    core = place_ref[1]
    first = sources_to_groups(jnp.where(owner == 0, -1, 0))
    last = sources_to_groups(jnp.where(owner == 31, 1, 0))
    plain = sources_to_groups(0)

    for r in range(4):
        for j in range(4):
            perm = first if j == 0 else (last if j == 3 else plain)
            tokens = x_ref[8 * r : 8 * r + 8, j].reshape(128, C)
            moved = dot(perm, tokens).astype(BF16).reshape(8, 16, C)
            for p in range(8):
                xs_ref[j, p + 1, 16 * r : 16 * r + 16, :] = moved[p]
    edge = jnp.zeros((8, C), F32)
    for j in range(4):
        lowest = xs_ref[j, 8].astype(F32)
        xs_ref[j, 0] = jnp.concatenate([edge, lowest[:56]], axis=0).astype(BF16)
        highest = xs_ref[j, 1].astype(F32)
        xs_ref[j, 9] = jnp.concatenate([highest[8:], edge], axis=0).astype(BF16)

    gain_one = gain_one_ref[...]

    def conv(g):
        j, p = g // 8, g % 8
        total = xs_ref[j + 1, p + 1].astype(F32)
        for u in range(3):
            for v in range(3):
                total = total + dw_ref[3 * u + v : 3 * u + v + 1, :] * xs_ref[j + v, p + u].astype(F32)
        start = total.astype(BF16)
        rows = slice(64 * g, 64 * g + 64)
        in_ref[rows, :] = start
        normed, _ = norm(start.astype(F32))
        inputs_ref[rows, :] = (normed * gain_one).astype(BF16)


    for start in range(2):
        for g in range(8 * start, 8 * start + 8):
            conv(g)
        rows = slice(512 * start, 512 * start + 512)
        proj_ref[rows, :] = dot(inputs_ref[rows, :], w_qkv_ref[...]).astype(BF16)

    turned_s[0:256, :] = proj_ref[:, 0:256].T
    turned_s[256:512, :] = proj_ref[:, 512:768].T
    key_turned_ref[...] = proj_ref[:, 256:512].T
    mask = head_mask()
    turned_mask = turned_head_mask()
    lower = lane_half()

    def attend(i, carry):
        units = []
        for n in range(AHEAD):
            pair = i * AHEAD + n
            rows = pl.ds(pl.multiple_of(pair * 128, 128), 128)
            for side in range(2):
                lanes = slice(128 * side, 128 * side + 128)
                query = turned_s[lanes, rows]
                key = proj_ref[rows, 256 + 128 * side : 384 + 128 * side]
                value = turned_s[256 + 128 * side : 384 + 128 * side, rows]
                units.append((2 * pair + side, lanes, rows, (query, key, value)))
        results = [attend_unit(*parts, lower, mask, turned_mask) for _, _, _, parts in units]
        for (unit, lanes, rows, _), (probs, mixed) in zip(units, results):
            probs_ref[unit] = probs
            mixed_turned_s[lanes, rows] = mixed
        return carry

    lax.fori_loop(0, 8 // AHEAD, attend, 0)
    mixed_s[...] = mixed_turned_s[...].T

    for r in range(4):
        for j in range(2):
            tokens = x_ref[8 * r : 8 * r + 8, 4 + j].reshape(128, C)
            moved = dot(plain, tokens).astype(BF16).reshape(8, 16, C)
            for p in range(8):
                cot_s[(j * 8 + p) * 64 + 16 * r : (j * 8 + p) * 64 + 16 * r + 16, :] = moved[p]

    gain_two = gain_two_ref[...]

    def tail(i, gain_grad):
        rows = pl.ds(pl.multiple_of(i * CHUNK, CHUNK), CHUNK)
        narrow_s[...] = dot(mixed_s[rows, :], w_out_ref[...])
        inverses = []
        for n in range(CHUNK // ROWS):
            part = slice(ROWS * n, ROWS * n + ROWS)
            own = pl.ds(pl.multiple_of(i * CHUNK + ROWS * n, ROWS), ROWS)
            normed, inverse = norm(in_ref[own, :].astype(F32) + narrow_s[part, :])
            inverses.append(inverse)
            normed_s[part, :] = normed
            two_s[own, :] = (normed * gain_two).astype(BF16)
        wide_s[...] = dot(two_s[rows, :], w_up_ref[...])
        cot_wide_s[...] = dot_nt(cot_s[rows, :], w_down_ref[...])
        for n in range(CHUNK // SPAN):
            part = slice(SPAN * n, SPAN * n + SPAN)
            own = pl.ds(pl.multiple_of(i * CHUNK + SPAN * n, SPAN), SPAN)
            for block in range(4):
                columns = slice(256 * block, 256 * block + 256)
                pre = wide_s[part, columns]
                square = pre * pre
                tangent = jnp.tanh(pre * (gelu_coef + (gelu_coef * cubic_coef) * square))
                half = 0.5 + 0.5 * tangent
                act = pre * half
                act_s[own, columns] = act.astype(BF16)
                slope = half + (act - act * half) * (
                    2.0 * gelu_coef + (6.0 * gelu_coef * cubic_coef) * square
                )
                pre_s[own, columns] = (cot_wide_s[part, columns] * slope).astype(BF16)
        narrow_s[...] = dot_nt(pre_s[rows, :], w_up_ref[...])
        for n in range(CHUNK // ROWS):
            part = slice(ROWS * n, ROWS * n + ROWS)
            own = pl.ds(pl.multiple_of(i * CHUNK + ROWS * n, ROWS), ROWS)
            in_grad = narrow_s[part, :]
            normed = normed_s[part, :]
            back = norm_back(in_grad, normed, inverses[n], gain_two)
            resid_grad = cot_s[own, :].astype(F32) + back
            resid_grad_ref[own, :] = resid_grad
            low_s[own, :] = resid_grad.astype(BF16)
            gain_grad = gain_grad + fold_rows(in_grad * normed)
        mixed_grad_ref[rows, :] = dot_nt(low_s[rows, :], w_out_ref[...]).astype(BF16)
        return gain_grad

    gain_grad = lax.fori_loop(0, TOKENS // CHUNK, tail, jnp.zeros((8, C), F32))
    gain_grad_ref[...] = gain_grad

    cot_turned = cot_s[...].T
    two_turned = two_s[...].T
    for block in range(4):
        columns = slice(256 * block, 256 * block + 256)
        down = dot(cot_turned, act_s[:, columns]).T
        up = dot(two_turned, pre_s[:, columns])
        store_halves(core, down, up, keep_ref, send_ref, slice(256 * block, 256 * block + 256))
    out_grad_ref[...] = dot(mixed_turned_s[...], low_s[...])


def backward_kernel(
    place_ref, inputs_ref, proj_ref, key_turned_ref, probs_ref, mixed_grad_ref, out_grad_ref,
    proj_grad_ref, keep_ref, send_ref,
    upstream_s, query_grad_s,
):
    core = place_ref[1]
    upstream_s[...] = mixed_grad_ref[...].T
    mask = head_mask()
    wide_mask = mask.astype(F32)
    turned_mask = turned_head_mask()
    lower = lane_half()

    def attend_back(i, carry):
        units = []
        for n in range(AHEAD):
            pair = i * AHEAD + n
            rows = pl.ds(pl.multiple_of(pair * 128, 128), 128)
            for side in range(2):
                lanes = slice(128 * side, 128 * side + 128)
                parts = (
                    proj_ref[rows, lanes],
                    key_turned_ref[lanes, rows],
                    proj_ref[rows, 512 + 128 * side : 640 + 128 * side],
                    probs_ref[2 * pair + side],
                    mixed_grad_ref[rows, lanes],
                    upstream_s[lanes, rows],
                )
                units.append((side, lanes, rows, parts))
        results = [
            attend_unit_back(*parts, lower, mask, turned_mask, wide_mask) for _, _, _, parts in units
        ]
        for (side, lanes, rows, _), grads in zip(units, results):
            query_grad_s[lanes, rows] = grads[0]
            proj_grad_ref[rows, 256 + 128 * side : 384 + 128 * side] = grads[1]
            proj_grad_ref[rows, 512 + 128 * side : 640 + 128 * side] = grads[2]
        return carry

    lax.fori_loop(0, 8 // AHEAD, attend_back, 0)
    proj_grad_ref[:, 0:256] = query_grad_s[...].T

    inputs_turned = inputs_ref[...].T
    terms = [
        dot(inputs_turned, proj_grad_ref[:, 256 * block : 256 * block + 256])
        for block in range(3)
    ]
    terms.append(out_grad_ref[...])
    for block in range(2):
        rows = slice(256 * block, 256 * block + 256)
        store_halves(core, terms[block], terms[2 + block], keep_ref, send_ref, rows)


def head_kernel(
    xs_ref, in_ref, proj_grad_ref, resid_grad_ref, gain_two_grad_ref, gain_one_ref, w_qkv_ref,
    grad_ref, small_ref,
):
    gain_one = gain_one_ref[...]

    def head(i, gain_grad):
        rows = pl.ds(pl.multiple_of(i * 512, 512), 512)
        normed, inverse = norm(in_ref[rows, :].astype(F32))
        in_grad = dot_nt(proj_grad_ref[rows, :], w_qkv_ref[...])
        grad_ref[rows, :] = resid_grad_ref[rows, :] + norm_back(in_grad, normed, inverse, gain_one)
        return gain_grad + fold_rows(in_grad * normed)

    gain_grad = lax.fori_loop(0, 2, head, jnp.zeros((8, C), F32), unroll=2)

    def taps(g, sums):
        j, p = g // 8, g % 8
        grad = grad_ref[pl.ds(pl.multiple_of(g * 64, 64), 64), :]
        return tuple(
            sums[3 * u + v] + fold_rows(grad * xs_ref[j + v, p + u].astype(F32))
            for u in range(3)
            for v in range(3)
        )

    kernel_grad = lax.fori_loop(0, 16, taps, (jnp.zeros((8, C), F32),) * 9, unroll=16)
    small = [jnp.sum(term, axis=0, keepdims=True) for term in kernel_grad]
    small.append(jnp.sum(gain_grad, axis=0, keepdims=True))
    small.append(jnp.sum(gain_two_grad_ref[...], axis=0, keepdims=True))
    small.append(jnp.zeros((5, C), F32))
    small_ref[...] = jnp.concatenate(small, axis=0)


def pieces_kernel(
    grad_ref, small_ref, tail_ref, other_tail_ref, head_ref, other_head_ref, perm_ref, out_ref
):
    perm = perm_ref[...]
    edge = jnp.zeros((8, C), F32)
    for r in range(4):
        parts = [grad_ref[64 * g + 16 * r : 64 * g + 16 * r + 16, :] for g in range(16)]
        for j in range(2):
            lowest = 64 * (8 * j + 7) + 16 * r - 8
            parts.append(grad_ref[lowest : lowest + 8, :] if r > 0 else edge)
        for j in range(2):
            highest = 64 * 8 * j + 16 * r + 16
            parts.append(grad_ref[highest : highest + 8, :] if r < 3 else edge)
        parts.append(small_ref[8 * r : 8 * r + 8, :] if r < 2 else edge)
        parts.append(jnp.zeros((88, C), F32))
        tokens = jnp.concatenate(parts, axis=0).astype(BF16)
        moved = dot(perm, tokens).reshape(8, PIECE, C)
        rows = slice(256 * r, 256 * r + 256)
        tail = tail_ref[rows, :].astype(F32) + other_tail_ref[rows, :].astype(F32)
        rows = slice(128 * r, 128 * r + 128)
        head = head_ref[rows, :].astype(F32) + other_head_ref[rows, :].astype(F32)
        joined = [moved, tail.reshape(8, 32, C), head.reshape(8, 16, C)]
        joined = jnp.concatenate(joined, axis=1)
        out_ref[r] = joined.reshape(8 * JOINED, C).astype(BF16)


def partial_kernel(factor, x_ref, out_ref):
    total = jnp.zeros((SHARE, C), F32)
    for r in range(4):
        pieces = jnp.sum(x_ref[r].astype(F32).reshape(8, JOINED, C), axis=0)
        total = total + jnp.concatenate([pieces[PIECE:], pieces[32:40]], axis=0)
    out_ref[...] = (total * factor).astype(BF16)


def total_kernel(mine_ref, other_ref, out_ref):
    total = mine_ref[...].astype(F32) + other_ref[...].astype(F32)
    rows = jnp.concatenate([total] * 8, axis=0).astype(BF16)
    for r in range(4):
        out_ref[r] = rows


def unpack_kernel(pieces_ref, main_ref, edges_ref, tile_ref, first_ref, last_ref):
    for block in range(4):
        pieces = pieces_ref[block].astype(F32).reshape(8, JOINED, C)
        pieces = pieces[:, :PIECE].reshape(8 * PIECE, C).astype(BF16)
        columns = dot(main_ref[...], pieces).astype(BF16)
        tile_ref[:, 16 * block : 16 * block + 16, :] = columns.reshape(18, 16, C)
        if block == 0:
            first_ref[...] = dot(edges_ref[0], pieces).astype(BF16)
        if block == 3:
            last_ref[...] = dot(edges_ref[1], pieces).astype(BF16)


def tile_kernel(tile_ref, left_ref, right_ref, dw_ref, out_ref, wide):
    wide[:, 8:72, :] = tile_ref[...].astype(F32)
    left = left_ref[...].astype(F32)
    right = right_ref[...].astype(F32)
    for i in range(18):
        wide[i, 7:8, :] = left[i : i + 1]
        wide[i, 72:73, :] = right[i : i + 1]

    def row(i, carry):
        rows = [wide[i + 2 - u] for u in range(3)]
        total = wide[i + 1, 8:72, :]
        for v in range(3):
            term = dw_ref[v : v + 1, :] * rows[0]
            for u in range(1, 3):
                term = term + dw_ref[3 * u + v : 3 * u + v + 1, :] * rows[u]
            total = total + term[9 - v : 73 - v, :]
        out_ref[0, i] = total
        return carry

    lax.fori_loop(0, 16, row, 0)


def write_half(half, rows, qkv_ref, out_ref, up_ref, down_ref, tall, wide, sems):
    values = rows[...].astype(F32)
    tail = values[:, 0:32].reshape(1024, C)
    head = values[:, 32:48].reshape(512, C)

    def run(pairs):
        copies = [pltpu.make_async_copy(*pair, sems.at[i]) for i, pair in enumerate(pairs)]
        for copy in copies:
            copy.start()
        for copy in copies:
            copy.wait()

    @pl.when(half == 0)
    def _():
        tall[...] = tail
        wide[:, 0:256] = head[0:256]
        wide[:, 256:512] = head[256:512]
        run([(tall, down_ref), (wide.at[:, 0:512], qkv_ref.at[:, 0:512])])

    @pl.when(half == 1)
    def _():
        for block in range(4):
            wide[:, 256 * block : 256 * block + 256] = tail[256 * block : 256 * block + 256]
        tall[0:512, :] = head
        run([
            (wide, up_ref),
            (tall.at[0:256, :], qkv_ref.at[:, 512:768]),
            (tall.at[256:512, :], out_ref),
        ])


def first_outputs_kernel(place_ref, mine_ref, *refs):
    write_half(place_ref[1], mine_ref, *refs)


def outputs_kernel(
    place_ref, mine_ref, other_ref, qkv_in, out_in, up_in, down_in,
    kernel_ref, gain_one_ref, gain_two_ref, qkv_ref, out_ref, up_ref, down_ref,
    tall, wide, sems, kernel_s, gain_one_s, gain_two_s, small_sems,
):
    small = mine_ref[0:16].astype(F32) + other_ref[0:16].astype(F32)
    small = jnp.concatenate([small[k, 52:53] for k in range(16)], axis=0)
    for u in range(3):
        kernel_s[u] = small[3 * u : 3 * u + 3]
    gain_one_s[...] = small[9:10]
    gain_two_s[...] = small[10:11]
    pairs = ((kernel_s, kernel_ref), (gain_one_s, gain_one_ref), (gain_two_s, gain_two_ref))
    copies = [pltpu.make_async_copy(*pair, small_sems.at[i]) for i, pair in enumerate(pairs)]
    for copy in copies:
        copy.start()
    half = 1 - place_ref[1]
    write_half(half, other_ref, qkv_ref, out_ref, up_ref, down_ref, tall, wide, sems)
    for copy in copies:
        copy.wait()


VMEM = pl.BlockSpec(memory_space=pltpu.VMEM)
SMEM = pl.BlockSpec(memory_space=pltpu.SMEM)
HBM = pl.BlockSpec(memory_space=pl.ANY)


def call(kernel, outs, operands, scratch=(), scalars=0, flops=0, moved=0, limit=24):
    return pl.pallas_call(
        kernel,
        out_shape=tuple(jax.ShapeDtypeStruct(shape, dtype) for shape, dtype in outs),
        in_specs=[SMEM] * scalars + [VMEM] * (len(operands) - scalars),
        out_specs=tuple(VMEM for _ in outs),
        scratch_shapes=[pltpu.VMEM(shape, dtype) for shape, dtype in scratch],
        compiler_params=pltpu.CompilerParams(vmem_limit_bytes=limit * 2**20),
        cost_estimate=pl.CostEstimate(flops=flops, bytes_accessed=moved, transcendentals=0),
    )(*operands)


def local(input_map, dw_kernel, gain_one, w_qkv, w_out, gain_two, w_up, w_down, cotangent):
    owner = lax.axis_index("row") * 8 + lax.axis_index("col")
    core = lax.axis_index("core")
    place = jnp.stack([owner, core]).astype(jnp.int32)
    dw_rows = dw_kernel.reshape(9, C).astype(F32)

    def exchange(stacked):
        return lax.all_to_all(stacked, ("row", "col"), split_axis=0, concat_axis=0, tiled=True)

    def swap(values, axis):
        return lax.ppermute(values, axis, [(0, 1), (1, 0)])

    def shift(values, axis, step):
        size = lax.axis_size(axis)
        pairs = [(i, i + step) for i in range(size) if 0 <= i + step < size]
        return lax.ppermute(values, axis, pairs)

    (packed,) = call(
        pack_kernel,
        [((32, 6, 16, C), BF16)],
        [input_map[0], cotangent[0]],
        flops=4 * 10**8,
        moved=4 * 10**6,
        limit=60,
    )
    arrived = exchange(packed)

    (
        xs, start, inputs, projected, key_turned, probs, mixed_grad, resid_grad, tail_keep, tail_send,
        out_grad, gain_two_grad,
    ) = call(
        forward_kernel,
        [
            ((4, 10, 64, C), BF16),
            ((TOKENS, C), BF16),
            ((TOKENS, C), BF16),
            ((TOKENS, 3 * C), BF16),
            ((C, TOKENS), BF16),
            ((16, 256, 128), BF16),
            ((TOKENS, C), BF16),
            ((TOKENS, C), F32),
            ((1024, C), BF16),
            ((1024, C), BF16),
            ((C, C), F32),
            ((8, C), F32),
        ],
        [
            place, arrived, dw_rows,
            gain_one.reshape(1, C), w_qkv, w_out, gain_two.reshape(1, C), w_up, w_down,
        ],
        [
            ((TOKENS, C), BF16),
            ((TOKENS, C), BF16),
            ((TOKENS, C), BF16),
            ((TOKENS, C), BF16),
            ((TOKENS, FF), BF16),
            ((TOKENS, FF), BF16),
            ((2 * C, TOKENS), BF16),
            ((C, TOKENS), BF16),
            ((CHUNK, C), F32),
            ((CHUNK, C), F32),
            ((CHUNK, FF), F32),
            ((CHUNK, FF), F32),
        ],
        scalars=1,
        flops=8 * 10**9,
        moved=12 * 10**6,
        limit=36,
    )

    proj_grad, keep, send = call(
        backward_kernel,
        [((TOKENS, 3 * C), BF16), ((512, C), BF16), ((512, C), BF16)],
        [place, inputs, projected, key_turned, probs, mixed_grad, out_grad],
        [((C, TOKENS), BF16), ((C, TOKENS), BF16)],
        scalars=1,
        flops=5 * 10**9,
        moved=8 * 10**6,
        limit=32,
    )
    grad, small = call(
        head_kernel,
        [((TOKENS, C), F32), ((16, C), F32)],
        [xs, start, proj_grad, resid_grad, gain_two_grad, gain_one.reshape(1, C), w_qkv],
    )
    (pieces,) = call(
        pieces_kernel,
        [((4, 8 * JOINED, C), BF16)],
        [
            grad, small, tail_keep, swap(tail_send, "core"), keep, swap(send, "core"),
            jnp.asarray(groups_to_pieces(), BF16),
        ],
    )
    back = exchange(pieces.reshape(32, JOINED, C)).reshape(4, 8 * JOINED, C)
    factor = 1.0 / math.sqrt(TOKENS * 128)
    (partial,) = call(
        lambda x_ref, out_ref: partial_kernel(factor, x_ref, out_ref),
        [((SHARE, C), BF16)],
        [back],
    )
    main, edges = (jnp.asarray(t, BF16) for t in pieces_to_tile())
    tile, first, last = call(
        unpack_kernel,
        [((18, 64, C), BF16), ((32, C), BF16), ((32, C), BF16)],
        [back, main, edges],
    )
    left, right = shift(last, "col", 1), shift(first, "col", -1)
    (shared,) = call(
        total_kernel,
        [((4, 8 * SHARE, C), BF16)],
        [partial, swap(partial, "yh")],
    )
    mine = exchange(shared.reshape(32, SHARE, C))
    (input_grad,) = call(
        tile_kernel,
        [((1, 16, 64, C), F32)],
        [tile, left, right, dw_rows],
        [((18, 80, C), F32)],
    )
    mine, input_grad = lax.optimization_barrier((mine, input_grad))
    other = swap(mine, "core")
    large = tuple(jax.ShapeDtypeStruct(n, F32) for n in ((C, 3 * C), (C, C), (C, FF), (FF, C)))
    small = tuple(jax.ShapeDtypeStruct(n, F32) for n in ((3, 3, C), (1, C), (1, C)))
    scratch = [pltpu.VMEM((FF, C), F32), pltpu.VMEM((C, FF), F32), pltpu.SemaphoreType.DMA((3,))]
    settings = dict(compiler_params=pltpu.CompilerParams(vmem_limit_bytes=24 * 2**20))
    begun = pl.pallas_call(
        first_outputs_kernel,
        out_shape=large,
        in_specs=[SMEM, VMEM],
        out_specs=(HBM,) * 4,
        scratch_shapes=scratch,
        **settings,
    )(place, mine)
    kernel_grad, gain_one_grad, gain_two_sum, qkv_grad, out_sum, up_grad, down_grad = pl.pallas_call(
        outputs_kernel,
        out_shape=small + large,
        in_specs=[SMEM, VMEM, VMEM] + [HBM] * 4,
        out_specs=(HBM,) * 7,
        scratch_shapes=scratch
        + [pltpu.VMEM(part.shape, F32) for part in small]
        + [pltpu.SemaphoreType.DMA((3,))],
        input_output_aliases={3: 3, 4: 4, 5: 5, 6: 6},
        **settings,
    )(place, mine, other, *begun)
    return (
        input_grad,
        kernel_grad,
        gain_one_grad.reshape(C),
        qkv_grad,
        out_sum,
        gain_two_sum.reshape(C),
        up_grad,
        down_grad,
    )


def solution(mesh):
    cores = Mesh(mesh.devices.reshape(2, 2, 4, 8), ("yh", "core", "row", "col"))
    split = P(("yh", "core"), "row", "col", None)
    in_specs = (split, P(), P(), P(), P(), P(), P(), P(), split)
    out_specs = (split, P(), P(), P(), P(), P(), P(), P())
    return jax.shard_map(local, mesh=cores, in_specs=in_specs, out_specs=out_specs, check_vma=False)
```

```python
import math

import jax
import jax.numpy as jnp
import numpy as np
from jax import lax
from jax.experimental import pallas as pl
from jax.experimental.pallas import tpu as pltpu
from jax.sharding import Mesh
from jax.sharding import PartitionSpec as P

HEADS = 8
C = 256
FF = 1024
PIECE = 40
SUMS = 48
JOINED = PIECE + SUMS
SHARE = SUMS + 8
norm_eps = 1e-05
gelu_coef = 0.7978845608028654
cubic_coef = 0.044715
HEAD_SCALE = 1.0 / math.sqrt(C // HEADS)
TOKENS = 1024
AHEAD = 8
CHUNK = 512
ROWS = 64
SPAN = 16

F32 = jnp.float32
BF16 = jnp.bfloat16


def positions(size):
    return tuple(lax.broadcasted_iota(jnp.int32, (size, size), axis) for axis in range(2))


def as_matrix(chosen):
    return jnp.where(chosen, 1.0, 0.0).astype(BF16)


def tile_to_columns():
    to, of = positions(256)
    return as_matrix(((to >> 4) == (of & 15)) & ((to & 15) == (of >> 4)))


def sources_to_groups(shift):
    to, of = positions(128)
    same = ((to >> 4) == (of & 7)) & (((to >> 3) & 1) == ((of >> 3) & 1))
    return as_matrix(same & ((of >> 4) == (to & 7) + shift))


def head_mask():
    row, lane = positions(256)
    return as_matrix((row >> 6) == ((lane >> 5) & 3))


def turned_head_mask():
    lane, row = (lax.broadcasted_iota(jnp.int32, (128, 256), axis) for axis in range(2))
    return as_matrix((row >> 6) == (lane >> 5))


def groups_to_pieces():
    out = np.zeros((8 * PIECE, 384), np.float32)
    for c in range(8):
        for j in range(2):
            out[c * PIECE + 18 * j, 256 + 8 * j + c] = 1
            out[c * PIECE + 18 * j + 17, 272 + 8 * j + c] = 1
            for row in range(16):
                a, p = divmod(row, 8)
                out[c * PIECE + 18 * j + 1 + row, (j * 8 + p) * 16 + a * 8 + c] = 1
        out[c * PIECE + 36, 288 + c] = 1
    return out


def pieces_to_tile():
    main = np.zeros((288, 8 * PIECE), np.float32)
    edges = np.zeros((2, 32, 8 * PIECE), np.float32)
    for row in range(18):
        for q in range(16):
            main[row * 16 + q, (q // 2) * PIECE + (q % 2) * 18 + row] = 1
        edges[0, row, row] = 1
        edges[1, row, 7 * PIECE + 18 + row] = 1
    return main, edges


def dot(a, b):
    return lax.dot_general(a, b, (((1,), (0,)), ((), ())), preferred_element_type=F32)


def dot_nt(a, b):
    return lax.dot_general(a, b, (((1,), (1,)), ((), ())), preferred_element_type=F32)


def dot_tn(a, b):
    return lax.dot_general(a, b, (((0,), (0,)), ((), ())), preferred_element_type=F32)


def norm(values):
    center = values - jnp.mean(values, axis=-1, keepdims=True)
    inverse = lax.rsqrt(jnp.mean(center * center, axis=-1, keepdims=True) + norm_eps)
    return center * inverse, inverse


def norm_back(upstream, normed, inverse, gain):
    scaled = upstream * gain
    return inverse * (
        scaled
        - jnp.mean(scaled, axis=-1, keepdims=True)
        - normed * jnp.mean(scaled * normed, axis=-1, keepdims=True)
    )


def fold_rows(values):
    return jnp.sum(values.reshape(-1, 8, values.shape[-1]), axis=0)


def side_by_side(rows):
    return jnp.concatenate([rows[0:64], rows[64:128]], axis=1)


def stacked(rows):
    return jnp.concatenate([rows[:, 0:128], rows[:, 128:256]], axis=0)


def block_diagonal(rows):
    zeros = jnp.zeros((64, 128), rows.dtype)
    upper = jnp.concatenate([rows[0:64], zeros], axis=1)
    return jnp.concatenate([upper, jnp.concatenate([zeros, rows[64:128]], axis=1)], axis=0)


def by_head(rows, mask):
    return jnp.concatenate([side_by_side(rows)] * 4, axis=0) * mask


def by_lane_half(columns, lower):
    return jnp.concatenate([columns * lower, columns * (1 - lower)], axis=0)


def by_head_turned(columns, lower, turned_mask):
    swapped = jnp.concatenate([columns[:, 64:128], columns[:, 0:64]], axis=1)
    parts = []
    for first, second in ((columns, swapped), (swapped, columns)):
        part = first * lower + second * (1 - lower)
        parts.append(jnp.concatenate([part, part], axis=1) * turned_mask)
    return jnp.concatenate(parts, axis=0)


def own_half(blocks, lower):
    return jnp.where(lower, blocks[0:128], blocks[128:256]).astype(BF16)


def lane_half():
    return lax.broadcasted_iota(jnp.int32, (1, 128), 1) < 64


def attend_unit(query_turned, key, value_turned, lower, mask, turned_mask):
    low = lower.astype(F32).astype(BF16)
    scores = dot(by_head(key, mask), by_lane_half(query_turned, low)).reshape(4, 64, 128) * HEAD_SCALE
    expos = jnp.exp(scores - jnp.max(scores, axis=1, keepdims=True))
    probs = expos * (1.0 / jnp.sum(expos, axis=1, keepdims=True))
    probs = probs.reshape(256, 128).astype(BF16)
    mixed = dot(by_head_turned(value_turned, low, turned_mask), probs)
    return probs, own_half(mixed, lower)


def attend_unit_back(
    query, key_turned, value, probs, upstream, upstream_turned, lower, mask, turned_mask, wide_mask
):
    low = lower.astype(F32).astype(BF16)
    wide = probs.astype(F32).reshape(4, 64, 128)
    prob_grad = dot(by_head(value, mask), by_lane_half(upstream_turned, low)).reshape(4, 64, 128)
    centre = jnp.sum(wide * prob_grad, axis=1, keepdims=True)
    score_grad = (wide * (prob_grad - centre) * HEAD_SCALE).reshape(256, 128).astype(BF16)
    query_grad = own_half(dot(by_head_turned(key_turned, low, turned_mask), score_grad), lower)
    key_grad = jnp.sum((dot(score_grad, block_diagonal(query)) * wide_mask).reshape(4, 64, 256), axis=0)
    value_grad = jnp.sum((dot(probs, block_diagonal(upstream)) * wide_mask).reshape(4, 64, 256), axis=0)
    return query_grad, stacked(key_grad).astype(BF16), stacked(value_grad).astype(BF16)


def pack_kernel(x_ref, cot_ref, out_ref):
    perm = tile_to_columns()
    for block in range(4):
        tokens = x_ref[:, 16 * block : 16 * block + 16, :].reshape(256, C)
        columns = dot(perm, tokens).astype(BF16).reshape(16, 16, C)
        tokens = cot_ref[:, 16 * block : 16 * block + 16, :].reshape(256, C)
        cot_columns = dot(perm, tokens).astype(BF16).reshape(16, 16, C)
        for i in range(16):
            q = 16 * block + i
            k, odd = divmod(q, 2)
            out_ref[k, 4 + odd] = cot_columns[i]
            if odd:
                out_ref[k, 2] = columns[i]
                out_ref[(k + 1) % 32, 0] = columns[i]
            else:
                out_ref[k, 1] = columns[i]
                out_ref[(k - 1) % 32, 3] = columns[i]


def store_halves(core, lower, upper, keep_ref, send_ref, rows):
    keep_ref[rows, :] = jnp.where(core == 0, lower, upper).astype(BF16)
    send_ref[rows, :] = jnp.where(core == 0, upper, lower).astype(BF16)


def forward_kernel(
    place_ref, x_ref, dw_ref, gain_one_ref, w_qkv_ref, w_out_ref, gain_two_ref,
    w_up_ref, w_down_ref,
    xs_ref, in_ref, inputs_ref, proj_ref, key_turned_ref, probs_ref, mixed_grad_ref, resid_grad_ref, keep_ref, send_ref,
    out_grad_ref, gain_grad_ref,
    cot_s, mixed_s, two_s, low_s, act_s, pre_s, turned_s, mixed_turned_s,
    narrow_s, normed_s, wide_s, cot_wide_s,
):
    owner = place_ref[0]
    core = place_ref[1]
    first = sources_to_groups(jnp.where(owner == 0, -1, 0))
    last = sources_to_groups(jnp.where(owner == 31, 1, 0))
    plain = sources_to_groups(0)

    for r in range(4):
        for j in range(4):
            perm = first if j == 0 else (last if j == 3 else plain)
            tokens = x_ref[8 * r : 8 * r + 8, j].reshape(128, C)
            moved = dot(perm, tokens).astype(BF16).reshape(8, 16, C)
            for p in range(8):
                xs_ref[j, p + 1, 16 * r : 16 * r + 16, :] = moved[p]
    edge = jnp.zeros((8, C), F32)
    for j in range(4):
        lowest = xs_ref[j, 8].astype(F32)
        xs_ref[j, 0] = jnp.concatenate([edge, lowest[:56]], axis=0).astype(BF16)
        highest = xs_ref[j, 1].astype(F32)
        xs_ref[j, 9] = jnp.concatenate([highest[8:], edge], axis=0).astype(BF16)

    gain_one = gain_one_ref[...]

    def conv(g):
        j, p = g // 8, g % 8
        total = xs_ref[j + 1, p + 1].astype(F32)
        for u in range(3):
            for v in range(3):
                total = total + dw_ref[3 * u + v : 3 * u + v + 1, :] * xs_ref[j + v, p + u].astype(F32)
        start = total.astype(BF16)
        rows = slice(64 * g, 64 * g + 64)
        in_ref[rows, :] = start
        normed, _ = norm(start.astype(F32))
        inputs_ref[rows, :] = (normed * gain_one).astype(BF16)


    for start in range(2):
        for g in range(8 * start, 8 * start + 8):
            conv(g)
        rows = slice(512 * start, 512 * start + 512)
        proj_ref[rows, :] = dot(inputs_ref[rows, :], w_qkv_ref[...]).astype(BF16)

    turned_s[0:256, :] = proj_ref[:, 0:256].T
    turned_s[256:512, :] = proj_ref[:, 512:768].T
    key_turned_ref[...] = proj_ref[:, 256:512].T
    mask = head_mask()
    turned_mask = turned_head_mask()
    lower = lane_half()

    def attend(i, carry):
        units = []
        for n in range(AHEAD):
            pair = i * AHEAD + n
            rows = pl.ds(pl.multiple_of(pair * 128, 128), 128)
            for side in range(2):
                lanes = slice(128 * side, 128 * side + 128)
                query = turned_s[lanes, rows]
                key = proj_ref[rows, 256 + 128 * side : 384 + 128 * side]
                value = turned_s[256 + 128 * side : 384 + 128 * side, rows]
                units.append((2 * pair + side, lanes, rows, (query, key, value)))
        results = [attend_unit(*parts, lower, mask, turned_mask) for _, _, _, parts in units]
        for (unit, lanes, rows, _), (probs, mixed) in zip(units, results):
            probs_ref[unit] = probs
            mixed_turned_s[lanes, rows] = mixed
        return carry

    lax.fori_loop(0, 8 // AHEAD, attend, 0)
    mixed_s[...] = mixed_turned_s[...].T

    for r in range(4):
        for j in range(2):
            tokens = x_ref[8 * r : 8 * r + 8, 4 + j].reshape(128, C)
            moved = dot(plain, tokens).astype(BF16).reshape(8, 16, C)
            for p in range(8):
                cot_s[(j * 8 + p) * 64 + 16 * r : (j * 8 + p) * 64 + 16 * r + 16, :] = moved[p]

    gain_two = gain_two_ref[...]

    inverses = {}

    def resid_part(start):
        rows = slice(start, start + CHUNK)
        narrow_s[rows, :] = dot(mixed_s[rows, :], w_out_ref[...])
        for first in range(start, start + CHUNK, ROWS):
            own = slice(first, first + ROWS)
            normed, inverses[first] = norm(in_ref[own, :].astype(F32) + narrow_s[own, :])
            normed_s[own, :] = normed
            two_s[own, :] = (normed * gain_two).astype(BF16)

    def wide_part(start):
        rows = slice(start, start + CHUNK)
        wide_s[rows, :] = dot(two_s[rows, :], w_up_ref[...])
        cot_wide_s[rows, :] = dot_nt(cot_s[rows, :], w_down_ref[...])

    def gelu_part(start):
        for first in range(start, start + CHUNK, SPAN):
            own = slice(first, first + SPAN)
            for block in range(4):
                columns = slice(256 * block, 256 * block + 256)
                pre = wide_s[own, columns]
                square = pre * pre
                tangent = jnp.tanh(pre * (gelu_coef + (gelu_coef * cubic_coef) * square))
                half = 0.5 + 0.5 * tangent
                act = pre * half
                act_s[own, columns] = act.astype(BF16)
                slope = half + (act - act * half) * (
                    2.0 * gelu_coef + (6.0 * gelu_coef * cubic_coef) * square
                )
                pre_s[own, columns] = (cot_wide_s[own, columns] * slope).astype(BF16)

    def narrow_part(start):
        rows = slice(start, start + CHUNK)
        narrow_s[rows, :] = dot_nt(pre_s[rows, :], w_up_ref[...])

    def back_part(start, gain_grad):
        for first in range(start, start + CHUNK, ROWS):
            own = slice(first, first + ROWS)
            in_grad = narrow_s[own, :]
            normed = normed_s[own, :]
            back = norm_back(in_grad, normed, inverses[first], gain_two)
            resid_grad = cot_s[own, :].astype(F32) + back
            resid_grad_ref[own, :] = resid_grad
            low_s[own, :] = resid_grad.astype(BF16)
            gain_grad = gain_grad + fold_rows(in_grad * normed)
        return gain_grad

    def last_part(start):
        rows = slice(start, start + CHUNK)
        mixed_grad_ref[rows, :] = dot_nt(low_s[rows, :], w_out_ref[...]).astype(BF16)

    gain_grad = jnp.zeros((8, C), F32)
    starts = list(range(0, TOKENS, CHUNK))
    steps = len(starts)
    resid_part(starts[0])
    wide_part(starts[0])
    for n in range(steps):
        if n + 1 < steps:
            resid_part(starts[n + 1])
            wide_part(starts[n + 1])
        gelu_part(starts[n])
        narrow_part(starts[n])
        if n > 0:
            gain_grad = back_part(starts[n - 1], gain_grad)
            last_part(starts[n - 1])
    cot_turned = cot_s[...].T
    two_turned = two_s[...].T
    for block in range(4):
        columns = slice(256 * block, 256 * block + 256)
        down = dot(cot_turned, act_s[:, columns]).T
        up = dot(two_turned, pre_s[:, columns])
        store_halves(core, down, up, keep_ref, send_ref, slice(256 * block, 256 * block + 256))
    gain_grad = back_part(starts[-1], gain_grad)
    last_part(starts[-1])
    gain_grad_ref[...] = gain_grad

    out_grad_ref[...] = dot(mixed_turned_s[...], low_s[...])


def backward_kernel(
    place_ref, inputs_ref, proj_ref, key_turned_ref, probs_ref, mixed_grad_ref, out_grad_ref,
    proj_grad_ref, keep_ref, send_ref,
    upstream_s, query_grad_s,
):
    core = place_ref[1]
    upstream_s[...] = mixed_grad_ref[...].T
    mask = head_mask()
    wide_mask = mask.astype(F32)
    turned_mask = turned_head_mask()
    lower = lane_half()

    def attend_back(i, carry):
        units = []
        for n in range(AHEAD):
            pair = i * AHEAD + n
            rows = pl.ds(pl.multiple_of(pair * 128, 128), 128)
            for side in range(2):
                lanes = slice(128 * side, 128 * side + 128)
                parts = (
                    proj_ref[rows, lanes],
                    key_turned_ref[lanes, rows],
                    proj_ref[rows, 512 + 128 * side : 640 + 128 * side],
                    probs_ref[2 * pair + side],
                    mixed_grad_ref[rows, lanes],
                    upstream_s[lanes, rows],
                )
                units.append((side, lanes, rows, parts))
        results = [
            attend_unit_back(*parts, lower, mask, turned_mask, wide_mask) for _, _, _, parts in units
        ]
        for (side, lanes, rows, _), grads in zip(units, results):
            query_grad_s[lanes, rows] = grads[0]
            proj_grad_ref[rows, 256 + 128 * side : 384 + 128 * side] = grads[1]
            proj_grad_ref[rows, 512 + 128 * side : 640 + 128 * side] = grads[2]
        return carry

    lax.fori_loop(0, 8 // AHEAD, attend_back, 0)
    proj_grad_ref[:, 0:256] = query_grad_s[...].T

    inputs_turned = inputs_ref[...].T
    terms = [
        dot(inputs_turned, proj_grad_ref[:, 256 * block : 256 * block + 256])
        for block in range(3)
    ]
    terms.append(out_grad_ref[...])
    for block in range(2):
        rows = slice(256 * block, 256 * block + 256)
        store_halves(core, terms[block], terms[2 + block], keep_ref, send_ref, rows)


def head_kernel(
    xs_ref, in_ref, proj_grad_ref, resid_grad_ref, gain_two_grad_ref, gain_one_ref, w_qkv_ref,
    grad_ref, small_ref,
):
    gain_one = gain_one_ref[...]

    def head(i, gain_grad):
        rows = pl.ds(pl.multiple_of(i * 512, 512), 512)
        normed, inverse = norm(in_ref[rows, :].astype(F32))
        in_grad = dot_nt(proj_grad_ref[rows, :], w_qkv_ref[...])
        grad_ref[rows, :] = resid_grad_ref[rows, :] + norm_back(in_grad, normed, inverse, gain_one)
        return gain_grad + fold_rows(in_grad * normed)

    gain_grad = lax.fori_loop(0, 2, head, jnp.zeros((8, C), F32), unroll=2)

    def taps(g, sums):
        j, p = g // 8, g % 8
        grad = grad_ref[pl.ds(pl.multiple_of(g * 64, 64), 64), :]
        return tuple(
            sums[3 * u + v] + fold_rows(grad * xs_ref[j + v, p + u].astype(F32))
            for u in range(3)
            for v in range(3)
        )

    kernel_grad = lax.fori_loop(0, 16, taps, (jnp.zeros((8, C), F32),) * 9, unroll=16)
    small = [jnp.sum(term, axis=0, keepdims=True) for term in kernel_grad]
    small.append(jnp.sum(gain_grad, axis=0, keepdims=True))
    small.append(jnp.sum(gain_two_grad_ref[...], axis=0, keepdims=True))
    small.append(jnp.zeros((5, C), F32))
    small_ref[...] = jnp.concatenate(small, axis=0)


def pieces_kernel(
    grad_ref, small_ref, tail_ref, other_tail_ref, head_ref, other_head_ref, perm_ref, out_ref
):
    perm = perm_ref[...]
    edge = jnp.zeros((8, C), F32)
    for r in range(4):
        parts = [grad_ref[64 * g + 16 * r : 64 * g + 16 * r + 16, :] for g in range(16)]
        for j in range(2):
            lowest = 64 * (8 * j + 7) + 16 * r - 8
            parts.append(grad_ref[lowest : lowest + 8, :] if r > 0 else edge)
        for j in range(2):
            highest = 64 * 8 * j + 16 * r + 16
            parts.append(grad_ref[highest : highest + 8, :] if r < 3 else edge)
        parts.append(small_ref[8 * r : 8 * r + 8, :] if r < 2 else edge)
        parts.append(jnp.zeros((88, C), F32))
        tokens = jnp.concatenate(parts, axis=0).astype(BF16)
        moved = dot(perm, tokens).reshape(8, PIECE, C)
        rows = slice(256 * r, 256 * r + 256)
        tail = tail_ref[rows, :].astype(F32) + other_tail_ref[rows, :].astype(F32)
        rows = slice(128 * r, 128 * r + 128)
        head = head_ref[rows, :].astype(F32) + other_head_ref[rows, :].astype(F32)
        joined = [moved, tail.reshape(8, 32, C), head.reshape(8, 16, C)]
        joined = jnp.concatenate(joined, axis=1)
        out_ref[r] = joined.reshape(8 * JOINED, C).astype(BF16)


def partial_kernel(factor, x_ref, out_ref):
    total = jnp.zeros((SHARE, C), F32)
    for r in range(4):
        pieces = jnp.sum(x_ref[r].astype(F32).reshape(8, JOINED, C), axis=0)
        total = total + jnp.concatenate([pieces[PIECE:], pieces[32:40]], axis=0)
    out_ref[...] = (total * factor).astype(BF16)


def total_kernel(mine_ref, other_ref, out_ref):
    total = mine_ref[...].astype(F32) + other_ref[...].astype(F32)
    rows = jnp.concatenate([total] * 8, axis=0).astype(BF16)
    for r in range(4):
        out_ref[r] = rows


def unpack_kernel(pieces_ref, main_ref, edges_ref, tile_ref, first_ref, last_ref):
    for block in range(4):
        pieces = pieces_ref[block].astype(F32).reshape(8, JOINED, C)
        pieces = pieces[:, :PIECE].reshape(8 * PIECE, C).astype(BF16)
        columns = dot(main_ref[...], pieces).astype(BF16)
        tile_ref[:, 16 * block : 16 * block + 16, :] = columns.reshape(18, 16, C)
        if block == 0:
            first_ref[...] = dot(edges_ref[0], pieces).astype(BF16)
        if block == 3:
            last_ref[...] = dot(edges_ref[1], pieces).astype(BF16)


def tile_kernel(tile_ref, left_ref, right_ref, dw_ref, out_ref, wide):
    wide[:, 8:72, :] = tile_ref[...].astype(F32)
    left = left_ref[...].astype(F32)
    right = right_ref[...].astype(F32)
    for i in range(18):
        wide[i, 7:8, :] = left[i : i + 1]
        wide[i, 72:73, :] = right[i : i + 1]

    def row(i, carry):
        rows = [wide[i + 2 - u] for u in range(3)]
        total = wide[i + 1, 8:72, :]
        for v in range(3):
            term = dw_ref[v : v + 1, :] * rows[0]
            for u in range(1, 3):
                term = term + dw_ref[3 * u + v : 3 * u + v + 1, :] * rows[u]
            total = total + term[9 - v : 73 - v, :]
        out_ref[0, i] = total
        return carry

    lax.fori_loop(0, 16, row, 0)


def write_half(half, rows, qkv_ref, out_ref, up_ref, down_ref, tall, wide, sems):
    values = rows[...].astype(F32)
    tail = values[:, 0:32].reshape(1024, C)
    head = values[:, 32:48].reshape(512, C)

    def run(pairs):
        copies = [pltpu.make_async_copy(*pair, sems.at[i]) for i, pair in enumerate(pairs)]
        for copy in copies:
            copy.start()
        for copy in copies:
            copy.wait()

    @pl.when(half == 0)
    def _():
        tall[...] = tail
        wide[:, 0:256] = head[0:256]
        wide[:, 256:512] = head[256:512]
        run([(tall, down_ref), (wide.at[:, 0:512], qkv_ref.at[:, 0:512])])

    @pl.when(half == 1)
    def _():
        for block in range(4):
            wide[:, 256 * block : 256 * block + 256] = tail[256 * block : 256 * block + 256]
        tall[0:512, :] = head
        run([
            (wide, up_ref),
            (tall.at[0:256, :], qkv_ref.at[:, 512:768]),
            (tall.at[256:512, :], out_ref),
        ])


def first_outputs_kernel(place_ref, mine_ref, *refs):
    write_half(place_ref[1], mine_ref, *refs)


def outputs_kernel(
    place_ref, mine_ref, other_ref, qkv_in, out_in, up_in, down_in,
    kernel_ref, gain_one_ref, gain_two_ref, qkv_ref, out_ref, up_ref, down_ref,
    tall, wide, sems, kernel_s, gain_one_s, gain_two_s, small_sems,
):
    small = mine_ref[0:16].astype(F32) + other_ref[0:16].astype(F32)
    small = jnp.concatenate([small[k, 52:53] for k in range(16)], axis=0)
    for u in range(3):
        kernel_s[u] = small[3 * u : 3 * u + 3]
    gain_one_s[...] = small[9:10]
    gain_two_s[...] = small[10:11]
    pairs = ((kernel_s, kernel_ref), (gain_one_s, gain_one_ref), (gain_two_s, gain_two_ref))
    copies = [pltpu.make_async_copy(*pair, small_sems.at[i]) for i, pair in enumerate(pairs)]
    for copy in copies:
        copy.start()
    half = 1 - place_ref[1]
    write_half(half, other_ref, qkv_ref, out_ref, up_ref, down_ref, tall, wide, sems)
    for copy in copies:
        copy.wait()


VMEM = pl.BlockSpec(memory_space=pltpu.VMEM)
SMEM = pl.BlockSpec(memory_space=pltpu.SMEM)
HBM = pl.BlockSpec(memory_space=pl.ANY)


def call(kernel, outs, operands, scratch=(), scalars=0, flops=0, moved=0, limit=24):
    return pl.pallas_call(
        kernel,
        out_shape=tuple(jax.ShapeDtypeStruct(shape, dtype) for shape, dtype in outs),
        in_specs=[SMEM] * scalars + [VMEM] * (len(operands) - scalars),
        out_specs=tuple(VMEM for _ in outs),
        scratch_shapes=[pltpu.VMEM(shape, dtype) for shape, dtype in scratch],
        compiler_params=pltpu.CompilerParams(vmem_limit_bytes=limit * 2**20),
        cost_estimate=pl.CostEstimate(flops=flops, bytes_accessed=moved, transcendentals=0),
    )(*operands)


def local(input_map, dw_kernel, gain_one, w_qkv, w_out, gain_two, w_up, w_down, cotangent):
    owner = lax.axis_index("row") * 8 + lax.axis_index("col")
    core = lax.axis_index("core")
    place = jnp.stack([owner, core]).astype(jnp.int32)
    dw_rows = dw_kernel.reshape(9, C).astype(F32)

    def exchange(stacked):
        return lax.all_to_all(stacked, ("row", "col"), split_axis=0, concat_axis=0, tiled=True)

    def swap(values, axis):
        return lax.ppermute(values, axis, [(0, 1), (1, 0)])

    def shift(values, axis, step):
        size = lax.axis_size(axis)
        pairs = [(i, i + step) for i in range(size) if 0 <= i + step < size]
        return lax.ppermute(values, axis, pairs)

    (packed,) = call(
        pack_kernel,
        [((32, 6, 16, C), BF16)],
        [input_map[0], cotangent[0]],
        flops=4 * 10**8,
        moved=4 * 10**6,
        limit=60,
    )
    arrived = exchange(packed)

    (
        xs, start, inputs, projected, key_turned, probs, mixed_grad, resid_grad, tail_keep, tail_send,
        out_grad, gain_two_grad,
    ) = call(
        forward_kernel,
        [
            ((4, 10, 64, C), BF16),
            ((TOKENS, C), BF16),
            ((TOKENS, C), BF16),
            ((TOKENS, 3 * C), BF16),
            ((C, TOKENS), BF16),
            ((16, 256, 128), BF16),
            ((TOKENS, C), BF16),
            ((TOKENS, C), F32),
            ((1024, C), BF16),
            ((1024, C), BF16),
            ((C, C), F32),
            ((8, C), F32),
        ],
        [
            place, arrived, dw_rows,
            gain_one.reshape(1, C), w_qkv, w_out, gain_two.reshape(1, C), w_up, w_down,
        ],
        [
            ((TOKENS, C), BF16),
            ((TOKENS, C), BF16),
            ((TOKENS, C), BF16),
            ((TOKENS, C), BF16),
            ((TOKENS, FF), BF16),
            ((TOKENS, FF), BF16),
            ((2 * C, TOKENS), BF16),
            ((C, TOKENS), BF16),
            ((TOKENS, C), F32),
            ((TOKENS, C), F32),
            ((TOKENS, FF), F32),
            ((TOKENS, FF), F32),
        ],
        scalars=1,
        flops=8 * 10**9,
        moved=12 * 10**6,
        limit=36,
    )

    proj_grad, keep, send = call(
        backward_kernel,
        [((TOKENS, 3 * C), BF16), ((512, C), BF16), ((512, C), BF16)],
        [place, inputs, projected, key_turned, probs, mixed_grad, out_grad],
        [((C, TOKENS), BF16), ((C, TOKENS), BF16)],
        scalars=1,
        flops=5 * 10**9,
        moved=8 * 10**6,
        limit=32,
    )
    grad, small = call(
        head_kernel,
        [((TOKENS, C), F32), ((16, C), F32)],
        [xs, start, proj_grad, resid_grad, gain_two_grad, gain_one.reshape(1, C), w_qkv],
    )
    (pieces,) = call(
        pieces_kernel,
        [((4, 8 * JOINED, C), BF16)],
        [
            grad, small, tail_keep, swap(tail_send, "core"), keep, swap(send, "core"),
            jnp.asarray(groups_to_pieces(), BF16),
        ],
    )
    back = exchange(pieces.reshape(32, JOINED, C)).reshape(4, 8 * JOINED, C)
    factor = 1.0 / math.sqrt(TOKENS * 128)
    (partial,) = call(
        lambda x_ref, out_ref: partial_kernel(factor, x_ref, out_ref),
        [((SHARE, C), BF16)],
        [back],
    )
    main, edges = (jnp.asarray(t, BF16) for t in pieces_to_tile())
    tile, first, last = call(
        unpack_kernel,
        [((18, 64, C), BF16), ((32, C), BF16), ((32, C), BF16)],
        [back, main, edges],
    )
    left, right = shift(last, "col", 1), shift(first, "col", -1)
    (shared,) = call(
        total_kernel,
        [((4, 8 * SHARE, C), BF16)],
        [partial, swap(partial, "yh")],
    )
    mine = exchange(shared.reshape(32, SHARE, C))
    (input_grad,) = call(
        tile_kernel,
        [((1, 16, 64, C), F32)],
        [tile, left, right, dw_rows],
        [((18, 80, C), F32)],
    )
    mine, input_grad = lax.optimization_barrier((mine, input_grad))
    other = swap(mine, "core")
    large = tuple(jax.ShapeDtypeStruct(n, F32) for n in ((C, 3 * C), (C, C), (C, FF), (FF, C)))
    small = tuple(jax.ShapeDtypeStruct(n, F32) for n in ((3, 3, C), (1, C), (1, C)))
    scratch = [pltpu.VMEM((FF, C), F32), pltpu.VMEM((C, FF), F32), pltpu.SemaphoreType.DMA((3,))]
    settings = dict(compiler_params=pltpu.CompilerParams(vmem_limit_bytes=24 * 2**20))
    begun = pl.pallas_call(
        first_outputs_kernel,
        out_shape=large,
        in_specs=[SMEM, VMEM],
        out_specs=(HBM,) * 4,
        scratch_shapes=scratch,
        **settings,
    )(place, mine)
    kernel_grad, gain_one_grad, gain_two_sum, qkv_grad, out_sum, up_grad, down_grad = pl.pallas_call(
        outputs_kernel,
        out_shape=small + large,
        in_specs=[SMEM, VMEM, VMEM] + [HBM] * 4,
        out_specs=(HBM,) * 7,
        scratch_shapes=scratch
        + [pltpu.VMEM(part.shape, F32) for part in small]
        + [pltpu.SemaphoreType.DMA((3,))],
        input_output_aliases={3: 3, 4: 4, 5: 5, 6: 6},
        **settings,
    )(place, mine, other, *begun)
    return (
        input_grad,
        kernel_grad,
        gain_one_grad.reshape(C),
        qkv_grad,
        out_sum,
        gain_two_sum.reshape(C),
        up_grad,
        down_grad,
    )


def solution(mesh):
    cores = Mesh(mesh.devices.reshape(2, 2, 4, 8), ("yh", "core", "row", "col"))
    split = P(("yh", "core"), "row", "col", None)
    in_specs = (split, P(), P(), P(), P(), P(), P(), P(), split)
    out_specs = (split, P(), P(), P(), P(), P(), P(), P())
    return jax.shard_map(local, mesh=cores, in_specs=in_specs, out_specs=out_specs, check_vma=False)
```

```python
import math

import jax
import jax.numpy as jnp
import numpy as np
from jax import lax
from jax.experimental import pallas as pl
from jax.experimental.pallas import tpu as pltpu
from jax.sharding import Mesh
from jax.sharding import PartitionSpec as P

HEADS = 8
C = 256
FF = 1024
PIECE = 40
SUMS = 48
JOINED = PIECE + SUMS
SHARE = SUMS + 8
norm_eps = 1e-05
gelu_coef = 0.7978845608028654
cubic_coef = 0.044715
HEAD_SCALE = 1.0 / math.sqrt(C // HEADS)
TOKENS = 1024
AHEAD = 8
CHUNK = 512
ROWS = 64
SPAN = 16

F32 = jnp.float32
BF16 = jnp.bfloat16


def positions(size):
    return tuple(lax.broadcasted_iota(jnp.int32, (size, size), axis) for axis in range(2))


def as_matrix(chosen):
    return jnp.where(chosen, 1.0, 0.0).astype(BF16)


def tile_to_columns():
    to, of = positions(256)
    return as_matrix(((to >> 4) == (of & 15)) & ((to & 15) == (of >> 4)))


def sources_to_groups(shift):
    to, of = positions(128)
    same = ((to >> 4) == (of & 7)) & (((to >> 3) & 1) == ((of >> 3) & 1))
    return as_matrix(same & ((of >> 4) == (to & 7) + shift))


def head_mask():
    row, lane = positions(256)
    return as_matrix((row >> 6) == ((lane >> 5) & 3))


def turned_head_mask():
    lane, row = (lax.broadcasted_iota(jnp.int32, (128, 256), axis) for axis in range(2))
    return as_matrix((row >> 6) == (lane >> 5))


def groups_to_pieces():
    out = np.zeros((8 * PIECE, 384), np.float32)
    for c in range(8):
        for j in range(2):
            out[c * PIECE + 18 * j, 256 + 8 * j + c] = 1
            out[c * PIECE + 18 * j + 17, 272 + 8 * j + c] = 1
            for row in range(16):
                a, p = divmod(row, 8)
                out[c * PIECE + 18 * j + 1 + row, (j * 8 + p) * 16 + a * 8 + c] = 1
        out[c * PIECE + 36, 288 + c] = 1
    return out


def pieces_to_tile():
    main = np.zeros((288, 8 * PIECE), np.float32)
    edges = np.zeros((2, 32, 8 * PIECE), np.float32)
    for row in range(18):
        for q in range(16):
            main[row * 16 + q, (q // 2) * PIECE + (q % 2) * 18 + row] = 1
        edges[0, row, row] = 1
        edges[1, row, 7 * PIECE + 18 + row] = 1
    return main, edges


def dot(a, b):
    return lax.dot_general(a, b, (((1,), (0,)), ((), ())), preferred_element_type=F32)


def dot_nt(a, b):
    return lax.dot_general(a, b, (((1,), (1,)), ((), ())), preferred_element_type=F32)


def dot_tn(a, b):
    return lax.dot_general(a, b, (((0,), (0,)), ((), ())), preferred_element_type=F32)


def norm(values):
    center = values - jnp.mean(values, axis=-1, keepdims=True)
    inverse = lax.rsqrt(jnp.mean(center * center, axis=-1, keepdims=True) + norm_eps)
    return center * inverse, inverse


def norm_back(upstream, normed, inverse, gain):
    scaled = upstream * gain
    return inverse * (
        scaled
        - jnp.mean(scaled, axis=-1, keepdims=True)
        - normed * jnp.mean(scaled * normed, axis=-1, keepdims=True)
    )


def fold_rows(values):
    return jnp.sum(values.reshape(-1, 8, values.shape[-1]), axis=0)


def side_by_side(rows):
    return jnp.concatenate([rows[0:64], rows[64:128]], axis=1)


def stacked(rows):
    return jnp.concatenate([rows[:, 0:128], rows[:, 128:256]], axis=0)


def block_diagonal(rows):
    zeros = jnp.zeros((64, 128), rows.dtype)
    upper = jnp.concatenate([rows[0:64], zeros], axis=1)
    return jnp.concatenate([upper, jnp.concatenate([zeros, rows[64:128]], axis=1)], axis=0)


def by_head(rows, mask):
    return jnp.concatenate([side_by_side(rows)] * 4, axis=0) * mask


def by_lane_half(columns, lower):
    return jnp.concatenate([columns * lower, columns * (1 - lower)], axis=0)


def by_head_turned(columns, lower, turned_mask):
    swapped = jnp.concatenate([columns[:, 64:128], columns[:, 0:64]], axis=1)
    parts = []
    for first, second in ((columns, swapped), (swapped, columns)):
        part = first * lower + second * (1 - lower)
        parts.append(jnp.concatenate([part, part], axis=1) * turned_mask)
    return jnp.concatenate(parts, axis=0)


def own_half(blocks, lower):
    return jnp.where(lower, blocks[0:128], blocks[128:256]).astype(BF16)


def lane_half():
    return lax.broadcasted_iota(jnp.int32, (1, 128), 1) < 64


def attend_unit(query_turned, key, value_turned, lower, mask, turned_mask):
    low = lower.astype(F32).astype(BF16)
    scores = dot(by_head(key, mask), by_lane_half(query_turned, low)).reshape(4, 64, 128) * HEAD_SCALE
    expos = jnp.exp(scores - jnp.max(scores, axis=1, keepdims=True))
    probs = expos * (1.0 / jnp.sum(expos, axis=1, keepdims=True))
    probs = probs.reshape(256, 128).astype(BF16)
    mixed = dot(by_head_turned(value_turned, low, turned_mask), probs)
    return probs, own_half(mixed, lower)


def attend_unit_back(
    query, key_turned, value, probs, upstream, upstream_turned, lower, mask, turned_mask, wide_mask
):
    low = lower.astype(F32).astype(BF16)
    wide = probs.astype(F32).reshape(4, 64, 128)
    prob_grad = dot(by_head(value, mask), by_lane_half(upstream_turned, low)).reshape(4, 64, 128)
    centre = jnp.sum(wide * prob_grad, axis=1, keepdims=True)
    score_grad = (wide * (prob_grad - centre) * HEAD_SCALE).reshape(256, 128).astype(BF16)
    query_grad = own_half(dot(by_head_turned(key_turned, low, turned_mask), score_grad), lower)
    key_grad = jnp.sum((dot(score_grad, block_diagonal(query)) * wide_mask).reshape(4, 64, 256), axis=0)
    value_grad = jnp.sum((dot(probs, block_diagonal(upstream)) * wide_mask).reshape(4, 64, 256), axis=0)
    return query_grad, stacked(key_grad).astype(BF16), stacked(value_grad).astype(BF16)


def pack_kernel(x_ref, cot_ref, out_ref):
    perm = tile_to_columns()
    for block in range(4):
        tokens = x_ref[:, 16 * block : 16 * block + 16, :].reshape(256, C)
        columns = dot(perm, tokens).astype(BF16).reshape(16, 16, C)
        tokens = cot_ref[:, 16 * block : 16 * block + 16, :].reshape(256, C)
        cot_columns = dot(perm, tokens).astype(BF16).reshape(16, 16, C)
        for i in range(16):
            q = 16 * block + i
            k, odd = divmod(q, 2)
            out_ref[k, 4 + odd] = cot_columns[i]
            if odd:
                out_ref[k, 2] = columns[i]
                out_ref[(k + 1) % 32, 0] = columns[i]
            else:
                out_ref[k, 1] = columns[i]
                out_ref[(k - 1) % 32, 3] = columns[i]


def store_halves(core, lower, upper, keep_ref, send_ref, rows):
    keep_ref[rows, :] = jnp.where(core == 0, lower, upper).astype(BF16)
    send_ref[rows, :] = jnp.where(core == 0, upper, lower).astype(BF16)


def forward_kernel(
    place_ref, x_ref, dw_ref, gain_one_ref, w_qkv_ref, w_out_ref, gain_two_ref,
    w_up_ref, w_down_ref,
    xs_ref, in_ref, inputs_ref, proj_ref, key_turned_ref, probs_ref, mixed_grad_ref, resid_grad_ref, keep_ref, send_ref,
    out_grad_ref, gain_grad_ref,
    cot_s, mixed_s, two_s, low_s, act_s, pre_s, turned_s, mixed_turned_s,
    narrow_s, normed_s, wide_s, cot_wide_s,
):
    owner = place_ref[0]
    core = place_ref[1]
    first = sources_to_groups(jnp.where(owner == 0, -1, 0))
    last = sources_to_groups(jnp.where(owner == 31, 1, 0))
    plain = sources_to_groups(0)

    for r in range(4):
        for j in range(4):
            perm = first if j == 0 else (last if j == 3 else plain)
            tokens = x_ref[8 * r : 8 * r + 8, j].reshape(128, C)
            moved = dot(perm, tokens).astype(BF16).reshape(8, 16, C)
            for p in range(8):
                xs_ref[j, p + 1, 16 * r : 16 * r + 16, :] = moved[p]
    edge = jnp.zeros((8, C), F32)
    for j in range(4):
        lowest = xs_ref[j, 8].astype(F32)
        xs_ref[j, 0] = jnp.concatenate([edge, lowest[:56]], axis=0).astype(BF16)
        highest = xs_ref[j, 1].astype(F32)
        xs_ref[j, 9] = jnp.concatenate([highest[8:], edge], axis=0).astype(BF16)

    gain_one = gain_one_ref[...]

    def conv(g):
        j, p = g // 8, g % 8
        total = xs_ref[j + 1, p + 1].astype(F32)
        for u in range(3):
            for v in range(3):
                total = total + dw_ref[3 * u + v : 3 * u + v + 1, :] * xs_ref[j + v, p + u].astype(F32)
        start = total.astype(BF16)
        rows = slice(64 * g, 64 * g + 64)
        in_ref[rows, :] = start
        normed, _ = norm(start.astype(F32))
        inputs_ref[rows, :] = (normed * gain_one).astype(BF16)


    for start in range(2):
        for g in range(8 * start, 8 * start + 8):
            conv(g)
        rows = slice(512 * start, 512 * start + 512)
        proj_ref[rows, :] = dot(inputs_ref[rows, :], w_qkv_ref[...]).astype(BF16)

    turned_s[0:256, :] = proj_ref[:, 0:256].T
    turned_s[256:512, :] = proj_ref[:, 512:768].T
    key_turned_ref[...] = proj_ref[:, 256:512].T
    mask = head_mask()
    turned_mask = turned_head_mask()
    lower = lane_half()

    def attend(i, carry):
        units = []
        for n in range(AHEAD):
            pair = i * AHEAD + n
            rows = pl.ds(pl.multiple_of(pair * 128, 128), 128)
            for side in range(2):
                lanes = slice(128 * side, 128 * side + 128)
                query = turned_s[lanes, rows]
                key = proj_ref[rows, 256 + 128 * side : 384 + 128 * side]
                value = turned_s[256 + 128 * side : 384 + 128 * side, rows]
                units.append((2 * pair + side, lanes, rows, (query, key, value)))
        results = [attend_unit(*parts, lower, mask, turned_mask) for _, _, _, parts in units]
        for (unit, lanes, rows, _), (probs, mixed) in zip(units, results):
            probs_ref[unit] = probs
            mixed_turned_s[lanes, rows] = mixed
        return carry

    lax.fori_loop(0, 8 // AHEAD, attend, 0)
    mixed_s[...] = mixed_turned_s[...].T

    for r in range(4):
        for j in range(2):
            tokens = x_ref[8 * r : 8 * r + 8, 4 + j].reshape(128, C)
            moved = dot(plain, tokens).astype(BF16).reshape(8, 16, C)
            for p in range(8):
                cot_s[(j * 8 + p) * 64 + 16 * r : (j * 8 + p) * 64 + 16 * r + 16, :] = moved[p]

    gain_two = gain_two_ref[...]

    inverses = {}

    def resid_part(start):
        rows = slice(start, start + CHUNK)
        narrow_s[rows, :] = dot(mixed_s[rows, :], w_out_ref[...])
        for first in range(start, start + CHUNK, ROWS):
            own = slice(first, first + ROWS)
            normed, inverses[first] = norm(in_ref[own, :].astype(F32) + narrow_s[own, :])
            normed_s[own, :] = normed
            two_s[own, :] = (normed * gain_two).astype(BF16)

    def wide_part(start):
        rows = slice(start, start + CHUNK)
        wide_s[rows, :] = dot(two_s[rows, :], w_up_ref[...])
        cot_wide_s[rows, :] = dot_nt(cot_s[rows, :], w_down_ref[...])

    def gelu_part(start):
        for first in range(start, start + CHUNK, SPAN):
            own = slice(first, first + SPAN)
            for block in range(4):
                columns = slice(256 * block, 256 * block + 256)
                pre = wide_s[own, columns]
                square = pre * pre
                tangent = jnp.tanh(pre * (gelu_coef + (gelu_coef * cubic_coef) * square))
                half = 0.5 + 0.5 * tangent
                act = pre * half
                act_s[own, columns] = act.astype(BF16)
                slope = half + (act - act * half) * (
                    2.0 * gelu_coef + (6.0 * gelu_coef * cubic_coef) * square
                )
                pre_s[own, columns] = (cot_wide_s[own, columns] * slope).astype(BF16)

    def narrow_part(start):
        rows = slice(start, start + CHUNK)
        narrow_s[rows, :] = dot_nt(pre_s[rows, :], w_up_ref[...])

    def back_part(start, gain_grad):
        for first in range(start, start + CHUNK, ROWS):
            own = slice(first, first + ROWS)
            in_grad = narrow_s[own, :]
            normed = normed_s[own, :]
            back = norm_back(in_grad, normed, inverses[first], gain_two)
            resid_grad = cot_s[own, :].astype(F32) + back
            resid_grad_ref[own, :] = resid_grad
            low_s[own, :] = resid_grad.astype(BF16)
            gain_grad = gain_grad + fold_rows(in_grad * normed)
        return gain_grad

    def last_part(start):
        rows = slice(start, start + CHUNK)
        mixed_grad_ref[rows, :] = dot_nt(low_s[rows, :], w_out_ref[...]).astype(BF16)

    gain_grad = jnp.zeros((8, C), F32)
    starts = list(range(0, TOKENS, CHUNK))
    steps = len(starts)
    resid_part(starts[0])
    wide_part(starts[0])
    for n in range(steps):
        if n + 1 < steps:
            resid_part(starts[n + 1])
            wide_part(starts[n + 1])
        gelu_part(starts[n])
        narrow_part(starts[n])
        if n > 0:
            gain_grad = back_part(starts[n - 1], gain_grad)
            last_part(starts[n - 1])
    cot_turned = cot_s[...].T
    two_turned = two_s[...].T
    for block in range(4):
        columns = slice(256 * block, 256 * block + 256)
        down = dot(cot_turned, act_s[:, columns]).T
        up = dot(two_turned, pre_s[:, columns])
        store_halves(core, down, up, keep_ref, send_ref, slice(256 * block, 256 * block + 256))
    gain_grad = back_part(starts[-1], gain_grad)
    last_part(starts[-1])
    gain_grad_ref[...] = gain_grad

    out_grad_ref[...] = dot(mixed_turned_s[...], low_s[...])


def backward_kernel(
    place_ref, inputs_ref, proj_ref, key_turned_ref, probs_ref, mixed_grad_ref, out_grad_ref,
    proj_grad_ref, keep_ref, send_ref,
    upstream_s, query_grad_s,
):
    core = place_ref[1]
    upstream_s[...] = mixed_grad_ref[...].T
    mask = head_mask()
    wide_mask = mask.astype(F32)
    turned_mask = turned_head_mask()
    lower = lane_half()

    def attend_back(i, carry):
        units = []
        for n in range(AHEAD):
            pair = i * AHEAD + n
            rows = pl.ds(pl.multiple_of(pair * 128, 128), 128)
            for side in range(2):
                lanes = slice(128 * side, 128 * side + 128)
                parts = (
                    proj_ref[rows, lanes],
                    key_turned_ref[lanes, rows],
                    proj_ref[rows, 512 + 128 * side : 640 + 128 * side],
                    probs_ref[2 * pair + side],
                    mixed_grad_ref[rows, lanes],
                    upstream_s[lanes, rows],
                )
                units.append((side, lanes, rows, parts))
        for side, lanes, rows, parts in units:
            grads = attend_unit_back(*parts, lower, mask, turned_mask, wide_mask)
            query_grad_s[lanes, rows] = grads[0]
            proj_grad_ref[rows, 256 + 128 * side : 384 + 128 * side] = grads[1]
            proj_grad_ref[rows, 512 + 128 * side : 640 + 128 * side] = grads[2]
        return carry

    lax.fori_loop(0, 8 // AHEAD, attend_back, 0)
    proj_grad_ref[:, 0:256] = query_grad_s[...].T

    inputs_turned = inputs_ref[...].T
    terms = [
        dot(inputs_turned, proj_grad_ref[:, 256 * block : 256 * block + 256])
        for block in range(3)
    ]
    terms.append(out_grad_ref[...])
    for block in range(2):
        rows = slice(256 * block, 256 * block + 256)
        store_halves(core, terms[block], terms[2 + block], keep_ref, send_ref, rows)


def head_kernel(
    xs_ref, in_ref, proj_grad_ref, resid_grad_ref, gain_two_grad_ref, gain_one_ref, w_qkv_ref,
    grad_ref, small_ref,
):
    gain_one = gain_one_ref[...]

    def head(i, gain_grad):
        rows = pl.ds(pl.multiple_of(i * 512, 512), 512)
        normed, inverse = norm(in_ref[rows, :].astype(F32))
        in_grad = dot_nt(proj_grad_ref[rows, :], w_qkv_ref[...])
        grad_ref[rows, :] = resid_grad_ref[rows, :] + norm_back(in_grad, normed, inverse, gain_one)
        return gain_grad + fold_rows(in_grad * normed)

    gain_grad = lax.fori_loop(0, 2, head, jnp.zeros((8, C), F32), unroll=2)

    def taps(g, sums):
        j, p = g // 8, g % 8
        grad = grad_ref[pl.ds(pl.multiple_of(g * 64, 64), 64), :]
        return tuple(
            sums[3 * u + v] + fold_rows(grad * xs_ref[j + v, p + u].astype(F32))
            for u in range(3)
            for v in range(3)
        )

    kernel_grad = lax.fori_loop(0, 16, taps, (jnp.zeros((8, C), F32),) * 9, unroll=16)
    small = [jnp.sum(term, axis=0, keepdims=True) for term in kernel_grad]
    small.append(jnp.sum(gain_grad, axis=0, keepdims=True))
    small.append(jnp.sum(gain_two_grad_ref[...], axis=0, keepdims=True))
    small.append(jnp.zeros((5, C), F32))
    small_ref[...] = jnp.concatenate(small, axis=0)


def pieces_kernel(
    grad_ref, small_ref, tail_ref, other_tail_ref, head_ref, other_head_ref, perm_ref, out_ref
):
    perm = perm_ref[...]
    edge = jnp.zeros((8, C), F32)
    for r in range(4):
        parts = [grad_ref[64 * g + 16 * r : 64 * g + 16 * r + 16, :] for g in range(16)]
        for j in range(2):
            lowest = 64 * (8 * j + 7) + 16 * r - 8
            parts.append(grad_ref[lowest : lowest + 8, :] if r > 0 else edge)
        for j in range(2):
            highest = 64 * 8 * j + 16 * r + 16
            parts.append(grad_ref[highest : highest + 8, :] if r < 3 else edge)
        parts.append(small_ref[8 * r : 8 * r + 8, :] if r < 2 else edge)
        parts.append(jnp.zeros((88, C), F32))
        tokens = jnp.concatenate(parts, axis=0).astype(BF16)
        moved = dot(perm, tokens).reshape(8, PIECE, C)
        rows = slice(256 * r, 256 * r + 256)
        tail = tail_ref[rows, :].astype(F32) + other_tail_ref[rows, :].astype(F32)
        rows = slice(128 * r, 128 * r + 128)
        head = head_ref[rows, :].astype(F32) + other_head_ref[rows, :].astype(F32)
        joined = [moved, tail.reshape(8, 32, C), head.reshape(8, 16, C)]
        joined = jnp.concatenate(joined, axis=1)
        out_ref[r] = joined.reshape(8 * JOINED, C).astype(BF16)


def partial_kernel(factor, x_ref, out_ref):
    total = jnp.zeros((SHARE, C), F32)
    for r in range(4):
        pieces = jnp.sum(x_ref[r].astype(F32).reshape(8, JOINED, C), axis=0)
        total = total + jnp.concatenate([pieces[PIECE:], pieces[32:40]], axis=0)
    out_ref[...] = (total * factor).astype(BF16)


def total_kernel(mine_ref, other_ref, out_ref):
    total = mine_ref[...].astype(F32) + other_ref[...].astype(F32)
    rows = jnp.concatenate([total] * 8, axis=0).astype(BF16)
    for r in range(4):
        out_ref[r] = rows


def unpack_kernel(pieces_ref, main_ref, edges_ref, tile_ref, first_ref, last_ref):
    for block in range(4):
        pieces = pieces_ref[block].astype(F32).reshape(8, JOINED, C)
        pieces = pieces[:, :PIECE].reshape(8 * PIECE, C).astype(BF16)
        columns = dot(main_ref[...], pieces).astype(BF16)
        tile_ref[:, 16 * block : 16 * block + 16, :] = columns.reshape(18, 16, C)
        if block == 0:
            first_ref[...] = dot(edges_ref[0], pieces).astype(BF16)
        if block == 3:
            last_ref[...] = dot(edges_ref[1], pieces).astype(BF16)


def tile_kernel(tile_ref, left_ref, right_ref, dw_ref, out_ref, wide):
    wide[:, 8:72, :] = tile_ref[...].astype(F32)
    left = left_ref[...].astype(F32)
    right = right_ref[...].astype(F32)
    for i in range(18):
        wide[i, 7:8, :] = left[i : i + 1]
        wide[i, 72:73, :] = right[i : i + 1]

    def row(i, carry):
        rows = [wide[i + 2 - u] for u in range(3)]
        total = wide[i + 1, 8:72, :]
        for v in range(3):
            term = dw_ref[v : v + 1, :] * rows[0]
            for u in range(1, 3):
                term = term + dw_ref[3 * u + v : 3 * u + v + 1, :] * rows[u]
            total = total + term[9 - v : 73 - v, :]
        out_ref[0, i] = total
        return carry

    lax.fori_loop(0, 16, row, 0)


def write_half(half, rows, qkv_ref, out_ref, up_ref, down_ref, tall, wide, sems):
    def run(copies):
        for copy in copies:
            copy.wait()

    def start(copies, source, target):
        copies.append(pltpu.make_async_copy(source, target, sems.at[len(copies)]))
        copies[-1].start()

    def part(block):
        values = rows[8 * block : 8 * block + 8].astype(F32)
        return values[:, 0:32].reshape(256, C), values[:, 32:48].reshape(128, C)

    @pl.when(half == 0)
    def _():
        copies = []
        for block in range(4):
            tail, head = part(block)
            own = slice(256 * block, 256 * block + 256)
            tall[own, :] = tail
            start(copies, tall.at[own, :], down_ref.at[own, :])
            own = slice(128 * (block % 2), 128 * (block % 2) + 128)
            wide[own, 256 * (block // 2) : 256 * (block // 2) + 256] = head
        start(copies, wide.at[:, 0:512], qkv_ref.at[:, 0:512])
        run(copies)

    @pl.when(half == 1)
    def _():
        copies = []
        for block in range(4):
            tail, head = part(block)
            wide[:, 256 * block : 256 * block + 256] = tail
            tall[128 * block : 128 * block + 128, :] = head
            if block == 1:
                start(copies, tall.at[0:256, :], qkv_ref.at[:, 512:768])
        for block in range(4):
            own = slice(64 * block, 64 * block + 64)
            start(copies, wide.at[own, :], up_ref.at[own, :])
        start(copies, tall.at[256:512, :], out_ref)
        run(copies)


def first_outputs_kernel(place_ref, mine_ref, *refs):
    write_half(place_ref[1], mine_ref, *refs)


def outputs_kernel(
    place_ref, mine_ref, other_ref, qkv_in, out_in, up_in, down_in,
    kernel_ref, gain_one_ref, gain_two_ref, qkv_ref, out_ref, up_ref, down_ref,
    tall, wide, sems, kernel_s, gain_one_s, gain_two_s, small_sems,
):
    small = mine_ref[0:16].astype(F32) + other_ref[0:16].astype(F32)
    small = jnp.concatenate([small[k, 52:53] for k in range(16)], axis=0)
    for u in range(3):
        kernel_s[u] = small[3 * u : 3 * u + 3]
    gain_one_s[...] = small[9:10]
    gain_two_s[...] = small[10:11]
    pairs = ((kernel_s, kernel_ref), (gain_one_s, gain_one_ref), (gain_two_s, gain_two_ref))
    copies = [pltpu.make_async_copy(*pair, small_sems.at[i]) for i, pair in enumerate(pairs)]
    for copy in copies:
        copy.start()
    half = 1 - place_ref[1]
    write_half(half, other_ref, qkv_ref, out_ref, up_ref, down_ref, tall, wide, sems)
    for copy in copies:
        copy.wait()


VMEM = pl.BlockSpec(memory_space=pltpu.VMEM)
SMEM = pl.BlockSpec(memory_space=pltpu.SMEM)
HBM = pl.BlockSpec(memory_space=pl.ANY)


def call(kernel, outs, operands, scratch=(), scalars=0, flops=0, moved=0, limit=24):
    return pl.pallas_call(
        kernel,
        out_shape=tuple(jax.ShapeDtypeStruct(shape, dtype) for shape, dtype in outs),
        in_specs=[SMEM] * scalars + [VMEM] * (len(operands) - scalars),
        out_specs=tuple(VMEM for _ in outs),
        scratch_shapes=[pltpu.VMEM(shape, dtype) for shape, dtype in scratch],
        compiler_params=pltpu.CompilerParams(vmem_limit_bytes=limit * 2**20),
        cost_estimate=pl.CostEstimate(flops=flops, bytes_accessed=moved, transcendentals=0),
    )(*operands)


def local(input_map, dw_kernel, gain_one, w_qkv, w_out, gain_two, w_up, w_down, cotangent):
    owner = lax.axis_index("row") * 8 + lax.axis_index("col")
    core = lax.axis_index("core")
    place = jnp.stack([owner, core]).astype(jnp.int32)
    dw_rows = dw_kernel.reshape(9, C).astype(F32)

    def exchange(stacked):
        return lax.all_to_all(stacked, ("row", "col"), split_axis=0, concat_axis=0, tiled=True)

    def swap(values, axis):
        return lax.ppermute(values, axis, [(0, 1), (1, 0)])

    def shift(values, axis, step):
        size = lax.axis_size(axis)
        pairs = [(i, i + step) for i in range(size) if 0 <= i + step < size]
        return lax.ppermute(values, axis, pairs)

    (packed,) = call(
        pack_kernel,
        [((32, 6, 16, C), BF16)],
        [input_map[0], cotangent[0]],
        flops=4 * 10**8,
        moved=4 * 10**6,
        limit=60,
    )
    arrived = exchange(packed)

    (
        xs, start, inputs, projected, key_turned, probs, mixed_grad, resid_grad, tail_keep, tail_send,
        out_grad, gain_two_grad,
    ) = call(
        forward_kernel,
        [
            ((4, 10, 64, C), BF16),
            ((TOKENS, C), BF16),
            ((TOKENS, C), BF16),
            ((TOKENS, 3 * C), BF16),
            ((C, TOKENS), BF16),
            ((16, 256, 128), BF16),
            ((TOKENS, C), BF16),
            ((TOKENS, C), F32),
            ((1024, C), BF16),
            ((1024, C), BF16),
            ((C, C), F32),
            ((8, C), F32),
        ],
        [
            place, arrived, dw_rows,
            gain_one.reshape(1, C), w_qkv, w_out, gain_two.reshape(1, C), w_up, w_down,
        ],
        [
            ((TOKENS, C), BF16),
            ((TOKENS, C), BF16),
            ((TOKENS, C), BF16),
            ((TOKENS, C), BF16),
            ((TOKENS, FF), BF16),
            ((TOKENS, FF), BF16),
            ((2 * C, TOKENS), BF16),
            ((C, TOKENS), BF16),
            ((TOKENS, C), F32),
            ((TOKENS, C), F32),
            ((TOKENS, FF), F32),
            ((TOKENS, FF), F32),
        ],
        scalars=1,
        flops=8 * 10**9,
        moved=12 * 10**6,
        limit=36,
    )

    proj_grad, keep, send = call(
        backward_kernel,
        [((TOKENS, 3 * C), BF16), ((512, C), BF16), ((512, C), BF16)],
        [place, inputs, projected, key_turned, probs, mixed_grad, out_grad],
        [((C, TOKENS), BF16), ((C, TOKENS), BF16)],
        scalars=1,
        flops=5 * 10**9,
        moved=8 * 10**6,
        limit=32,
    )
    grad, small = call(
        head_kernel,
        [((TOKENS, C), F32), ((16, C), F32)],
        [xs, start, proj_grad, resid_grad, gain_two_grad, gain_one.reshape(1, C), w_qkv],
    )
    (pieces,) = call(
        pieces_kernel,
        [((4, 8 * JOINED, C), BF16)],
        [
            grad, small, tail_keep, swap(tail_send, "core"), keep, swap(send, "core"),
            jnp.asarray(groups_to_pieces(), BF16),
        ],
    )
    back = exchange(pieces.reshape(32, JOINED, C)).reshape(4, 8 * JOINED, C)
    factor = 1.0 / math.sqrt(TOKENS * 128)
    (partial,) = call(
        lambda x_ref, out_ref: partial_kernel(factor, x_ref, out_ref),
        [((SHARE, C), BF16)],
        [back],
    )
    main, edges = (jnp.asarray(t, BF16) for t in pieces_to_tile())
    tile, first, last = call(
        unpack_kernel,
        [((18, 64, C), BF16), ((32, C), BF16), ((32, C), BF16)],
        [back, main, edges],
    )
    left, right = shift(last, "col", 1), shift(first, "col", -1)
    (shared,) = call(
        total_kernel,
        [((4, 8 * SHARE, C), BF16)],
        [partial, swap(partial, "yh")],
    )
    mine = exchange(shared.reshape(32, SHARE, C))
    (input_grad,) = call(
        tile_kernel,
        [((1, 16, 64, C), F32)],
        [tile, left, right, dw_rows],
        [((18, 80, C), F32)],
    )
    mine, input_grad = lax.optimization_barrier((mine, input_grad))
    other = swap(mine, "core")
    large = tuple(jax.ShapeDtypeStruct(n, F32) for n in ((C, 3 * C), (C, C), (C, FF), (FF, C)))
    small = tuple(jax.ShapeDtypeStruct(n, F32) for n in ((3, 3, C), (1, C), (1, C)))
    scratch = [pltpu.VMEM((FF, C), F32), pltpu.VMEM((C, FF), F32), pltpu.SemaphoreType.DMA((6,))]
    settings = dict(compiler_params=pltpu.CompilerParams(vmem_limit_bytes=24 * 2**20))
    begun = pl.pallas_call(
        first_outputs_kernel,
        out_shape=large,
        in_specs=[SMEM, VMEM],
        out_specs=(HBM,) * 4,
        scratch_shapes=scratch,
        **settings,
    )(place, mine)
    kernel_grad, gain_one_grad, gain_two_sum, qkv_grad, out_sum, up_grad, down_grad = pl.pallas_call(
        outputs_kernel,
        out_shape=small + large,
        in_specs=[SMEM, VMEM, VMEM] + [HBM] * 4,
        out_specs=(HBM,) * 7,
        scratch_shapes=scratch
        + [pltpu.VMEM(part.shape, F32) for part in small]
        + [pltpu.SemaphoreType.DMA((3,))],
        input_output_aliases={3: 3, 4: 4, 5: 5, 6: 6},
        **settings,
    )(place, mine, other, *begun)
    return (
        input_grad,
        kernel_grad,
        gain_one_grad.reshape(C),
        qkv_grad,
        out_sum,
        gain_two_sum.reshape(C),
        up_grad,
        down_grad,
    )


def solution(mesh):
    cores = Mesh(mesh.devices.reshape(2, 2, 4, 8), ("yh", "core", "row", "col"))
    split = P(("yh", "core"), "row", "col", None)
    in_specs = (split, P(), P(), P(), P(), P(), P(), P(), split)
    out_specs = (split, P(), P(), P(), P(), P(), P(), P())
    return jax.shard_map(local, mesh=cores, in_specs=in_specs, out_specs=out_specs, check_vma=False)
```

```python
import math

import jax
import jax.numpy as jnp
import numpy as np
from jax import lax
from jax.experimental import pallas as pl
from jax.experimental.pallas import tpu as pltpu
from jax.sharding import Mesh
from jax.sharding import PartitionSpec as P

HEADS = 8
C = 256
FF = 1024
PIECE = 40
SUMS = 48
JOINED = PIECE + SUMS
SHARE = SUMS + 8
norm_eps = 1e-05
gelu_coef = 0.7978845608028654
cubic_coef = 0.044715
HEAD_SCALE = 1.0 / math.sqrt(C // HEADS)
TOKENS = 1024
AHEAD = 8
CHUNK = 512
ROWS = 64
SPAN = 16

F32 = jnp.float32
BF16 = jnp.bfloat16


def positions(size):
    return tuple(lax.broadcasted_iota(jnp.int32, (size, size), axis) for axis in range(2))


def as_matrix(chosen):
    return jnp.where(chosen, 1.0, 0.0).astype(BF16)


def tile_to_columns():
    to, of = positions(256)
    return as_matrix(((to >> 4) == (of & 15)) & ((to & 15) == (of >> 4)))


def sources_to_groups(shift):
    to, of = positions(128)
    same = ((to >> 4) == (of & 7)) & (((to >> 3) & 1) == ((of >> 3) & 1))
    return as_matrix(same & ((of >> 4) == (to & 7) + shift))


def head_mask():
    row, lane = positions(256)
    return as_matrix((row >> 6) == ((lane >> 5) & 3))


def turned_head_mask():
    lane, row = (lax.broadcasted_iota(jnp.int32, (128, 256), axis) for axis in range(2))
    return as_matrix((row >> 6) == (lane >> 5))


def groups_to_pieces():
    out = np.zeros((8 * PIECE, 384), np.float32)
    for c in range(8):
        for j in range(2):
            out[c * PIECE + 18 * j, 256 + 8 * j + c] = 1
            out[c * PIECE + 18 * j + 17, 272 + 8 * j + c] = 1
            for row in range(16):
                a, p = divmod(row, 8)
                out[c * PIECE + 18 * j + 1 + row, (j * 8 + p) * 16 + a * 8 + c] = 1
        out[c * PIECE + 36, 288 + c] = 1
    return out


def pieces_to_tile():
    main = np.zeros((288, 8 * PIECE), np.float32)
    edges = np.zeros((2, 32, 8 * PIECE), np.float32)
    for row in range(18):
        for q in range(16):
            main[row * 16 + q, (q // 2) * PIECE + (q % 2) * 18 + row] = 1
        edges[0, row, row] = 1
        edges[1, row, 7 * PIECE + 18 + row] = 1
    return main, edges


def dot(a, b):
    return lax.dot_general(a, b, (((1,), (0,)), ((), ())), preferred_element_type=F32)


def dot_nt(a, b):
    return lax.dot_general(a, b, (((1,), (1,)), ((), ())), preferred_element_type=F32)


def dot_tn(a, b):
    return lax.dot_general(a, b, (((0,), (0,)), ((), ())), preferred_element_type=F32)


def norm(values):
    center = values - jnp.mean(values, axis=-1, keepdims=True)
    inverse = lax.rsqrt(jnp.mean(center * center, axis=-1, keepdims=True) + norm_eps)
    return center * inverse, inverse


def norm_back(upstream, normed, inverse, gain):
    scaled = upstream * gain
    return inverse * (
        scaled
        - jnp.mean(scaled, axis=-1, keepdims=True)
        - normed * jnp.mean(scaled * normed, axis=-1, keepdims=True)
    )


def fold_rows(values):
    return jnp.sum(values.reshape(-1, 8, values.shape[-1]), axis=0)


def side_by_side(rows):
    return jnp.concatenate([rows[0:64], rows[64:128]], axis=1)


def stacked(rows):
    return jnp.concatenate([rows[:, 0:128], rows[:, 128:256]], axis=0)


def block_diagonal(rows):
    zeros = jnp.zeros((64, 128), rows.dtype)
    upper = jnp.concatenate([rows[0:64], zeros], axis=1)
    return jnp.concatenate([upper, jnp.concatenate([zeros, rows[64:128]], axis=1)], axis=0)


def by_head(rows, mask):
    return jnp.concatenate([side_by_side(rows)] * 4, axis=0) * mask


def by_lane_half(columns, lower):
    return jnp.concatenate([columns * lower, columns * (1 - lower)], axis=0)


def by_head_turned(columns, lower, turned_mask):
    swapped = jnp.concatenate([columns[:, 64:128], columns[:, 0:64]], axis=1)
    parts = []
    for first, second in ((columns, swapped), (swapped, columns)):
        part = first * lower + second * (1 - lower)
        parts.append(jnp.concatenate([part, part], axis=1) * turned_mask)
    return jnp.concatenate(parts, axis=0)


def own_half(blocks, lower):
    return jnp.where(lower, blocks[0:128], blocks[128:256]).astype(BF16)


def lane_half():
    return lax.broadcasted_iota(jnp.int32, (1, 128), 1) < 64


def attend_unit(query_turned, key, value_turned, lower, mask, turned_mask):
    low = lower.astype(F32).astype(BF16)
    scores = dot(by_head(key, mask), by_lane_half(query_turned, low)).reshape(4, 64, 128) * HEAD_SCALE
    expos = jnp.exp(scores - jnp.max(scores, axis=1, keepdims=True))
    probs = expos * (1.0 / jnp.sum(expos, axis=1, keepdims=True))
    probs = probs.reshape(256, 128).astype(BF16)
    mixed = dot(by_head_turned(value_turned, low, turned_mask), probs)
    return probs, own_half(mixed, lower)


def attend_unit_back(
    query, key_turned, value, probs, upstream, upstream_turned, lower, mask, turned_mask, wide_mask
):
    low = lower.astype(F32).astype(BF16)
    wide = probs.astype(F32).reshape(4, 64, 128)
    prob_grad = dot(by_head(value, mask), by_lane_half(upstream_turned, low)).reshape(4, 64, 128)
    centre = jnp.sum(wide * prob_grad, axis=1, keepdims=True)
    score_grad = (wide * (prob_grad - centre) * HEAD_SCALE).reshape(256, 128).astype(BF16)
    query_grad = own_half(dot(by_head_turned(key_turned, low, turned_mask), score_grad), lower)
    key_grad = jnp.sum((dot(score_grad, block_diagonal(query)) * wide_mask).reshape(4, 64, 256), axis=0)
    value_grad = jnp.sum((dot(probs, block_diagonal(upstream)) * wide_mask).reshape(4, 64, 256), axis=0)
    return query_grad, stacked(key_grad).astype(BF16), stacked(value_grad).astype(BF16)


def pack_kernel(x_ref, cot_ref, out_ref):
    perm = tile_to_columns()
    for block in range(4):
        tokens = x_ref[:, 16 * block : 16 * block + 16, :].reshape(256, C)
        columns = dot(perm, tokens).astype(BF16).reshape(16, 16, C)
        tokens = cot_ref[:, 16 * block : 16 * block + 16, :].reshape(256, C)
        cot_columns = dot(perm, tokens).astype(BF16).reshape(16, 16, C)
        for i in range(16):
            q = 16 * block + i
            k, odd = divmod(q, 2)
            out_ref[k, 4 + odd] = cot_columns[i]
            if odd:
                out_ref[k, 2] = columns[i]
                out_ref[(k + 1) % 32, 0] = columns[i]
            else:
                out_ref[k, 1] = columns[i]
                out_ref[(k - 1) % 32, 3] = columns[i]


def store_halves(core, lower, upper, keep_ref, send_ref, rows):
    keep_ref[rows, :] = jnp.where(core == 0, lower, upper).astype(BF16)
    send_ref[rows, :] = jnp.where(core == 0, upper, lower).astype(BF16)


def forward_kernel(
    place_ref, x_ref, dw_ref, gain_one_ref, w_qkv_ref, w_out_ref, gain_two_ref,
    w_up_ref, w_down_ref,
    xs_ref, in_ref, inputs_ref, proj_ref, key_turned_ref, probs_ref, mixed_grad_ref, resid_grad_ref, keep_ref, send_ref,
    out_grad_ref, gain_grad_ref,
    cot_s, mixed_s, two_s, low_s, act_s, pre_s, turned_s, mixed_turned_s,
    narrow_s, normed_s, wide_s, cot_wide_s,
):
    owner = place_ref[0]
    core = place_ref[1]
    first = sources_to_groups(jnp.where(owner == 0, -1, 0))
    last = sources_to_groups(jnp.where(owner == 31, 1, 0))
    plain = sources_to_groups(0)

    for r in range(4):
        for j in range(4):
            perm = first if j == 0 else (last if j == 3 else plain)
            tokens = x_ref[8 * r : 8 * r + 8, j].reshape(128, C)
            moved = dot(perm, tokens).astype(BF16).reshape(8, 16, C)
            for p in range(8):
                xs_ref[j, p + 1, 16 * r : 16 * r + 16, :] = moved[p]
    edge = jnp.zeros((8, C), F32)
    for j in range(4):
        lowest = xs_ref[j, 8].astype(F32)
        xs_ref[j, 0] = jnp.concatenate([edge, lowest[:56]], axis=0).astype(BF16)
        highest = xs_ref[j, 1].astype(F32)
        xs_ref[j, 9] = jnp.concatenate([highest[8:], edge], axis=0).astype(BF16)

    gain_one = gain_one_ref[...]

    def conv(g):
        j, p = g // 8, g % 8
        total = xs_ref[j + 1, p + 1].astype(F32)
        for u in range(3):
            for v in range(3):
                total = total + dw_ref[3 * u + v : 3 * u + v + 1, :] * xs_ref[j + v, p + u].astype(F32)
        start = total.astype(BF16)
        rows = slice(64 * g, 64 * g + 64)
        in_ref[rows, :] = start
        normed, _ = norm(start.astype(F32))
        inputs_ref[rows, :] = (normed * gain_one).astype(BF16)


    for start in range(2):
        for g in range(8 * start, 8 * start + 8):
            conv(g)
        rows = slice(512 * start, 512 * start + 512)
        proj_ref[rows, :] = dot(inputs_ref[rows, :], w_qkv_ref[...]).astype(BF16)

    turned_s[0:256, :] = proj_ref[:, 0:256].T
    turned_s[256:512, :] = proj_ref[:, 512:768].T
    key_turned_ref[...] = proj_ref[:, 256:512].T
    mask = head_mask()
    turned_mask = turned_head_mask()
    lower = lane_half()

    def attend(i, carry):
        units = []
        for n in range(AHEAD):
            pair = i * AHEAD + n
            rows = pl.ds(pl.multiple_of(pair * 128, 128), 128)
            for side in range(2):
                lanes = slice(128 * side, 128 * side + 128)
                query = turned_s[lanes, rows]
                key = proj_ref[rows, 256 + 128 * side : 384 + 128 * side]
                value = turned_s[256 + 128 * side : 384 + 128 * side, rows]
                units.append((2 * pair + side, lanes, rows, (query, key, value)))
        results = [attend_unit(*parts, lower, mask, turned_mask) for _, _, _, parts in units]
        for (unit, lanes, rows, _), (probs, mixed) in zip(units, results):
            probs_ref[unit] = probs
            mixed_turned_s[lanes, rows] = mixed
        return carry

    lax.fori_loop(0, 8 // AHEAD, attend, 0)
    mixed_s[...] = mixed_turned_s[...].T

    for r in range(4):
        for j in range(2):
            tokens = x_ref[8 * r : 8 * r + 8, 4 + j].reshape(128, C)
            moved = dot(plain, tokens).astype(BF16).reshape(8, 16, C)
            for p in range(8):
                cot_s[(j * 8 + p) * 64 + 16 * r : (j * 8 + p) * 64 + 16 * r + 16, :] = moved[p]

    gain_two = gain_two_ref[...]

    inverses = {}

    def resid_part(start):
        rows = slice(start, start + CHUNK)
        narrow_s[rows, :] = dot(mixed_s[rows, :], w_out_ref[...])
        for first in range(start, start + CHUNK, ROWS):
            own = slice(first, first + ROWS)
            normed, inverses[first] = norm(in_ref[own, :].astype(F32) + narrow_s[own, :])
            normed_s[own, :] = normed
            two_s[own, :] = (normed * gain_two).astype(BF16)

    def wide_part(start):
        rows = slice(start, start + CHUNK)
        wide_s[rows, :] = dot(two_s[rows, :], w_up_ref[...])
        cot_wide_s[rows, :] = dot_nt(cot_s[rows, :], w_down_ref[...])

    def gelu_part(start):
        for first in range(start, start + CHUNK, SPAN):
            own = slice(first, first + SPAN)
            for block in range(4):
                columns = slice(256 * block, 256 * block + 256)
                pre = wide_s[own, columns]
                square = pre * pre
                tangent = jnp.tanh(pre * (gelu_coef + (gelu_coef * cubic_coef) * square))
                half = 0.5 + 0.5 * tangent
                act = pre * half
                act_s[own, columns] = act.astype(BF16)
                slope = half + (act - act * half) * (
                    2.0 * gelu_coef + (6.0 * gelu_coef * cubic_coef) * square
                )
                pre_s[own, columns] = (cot_wide_s[own, columns] * slope).astype(BF16)

    def narrow_part(start):
        rows = slice(start, start + CHUNK)
        narrow_s[rows, :] = dot_nt(pre_s[rows, :], w_up_ref[...])

    def back_part(start, gain_grad):
        for first in range(start, start + CHUNK, ROWS):
            own = slice(first, first + ROWS)
            in_grad = narrow_s[own, :]
            normed = normed_s[own, :]
            back = norm_back(in_grad, normed, inverses[first], gain_two)
            resid_grad = cot_s[own, :].astype(F32) + back
            resid_grad_ref[own, :] = resid_grad
            low_s[own, :] = resid_grad.astype(BF16)
            gain_grad = gain_grad + fold_rows(in_grad * normed)
        return gain_grad

    def last_part(start):
        rows = slice(start, start + CHUNK)
        mixed_grad_ref[rows, :] = dot_nt(low_s[rows, :], w_out_ref[...]).astype(BF16)

    gain_grad = jnp.zeros((8, C), F32)
    starts = list(range(0, TOKENS, CHUNK))
    steps = len(starts)
    resid_part(starts[0])
    wide_part(starts[0])
    for n in range(steps):
        if n + 1 < steps:
            resid_part(starts[n + 1])
            wide_part(starts[n + 1])
        gelu_part(starts[n])
        narrow_part(starts[n])
        if n > 0:
            gain_grad = back_part(starts[n - 1], gain_grad)
            last_part(starts[n - 1])
    cot_turned = cot_s[...].T
    two_turned = two_s[...].T
    for block in range(4):
        columns = slice(256 * block, 256 * block + 256)
        down = dot(cot_turned, act_s[:, columns]).T
        up = dot(two_turned, pre_s[:, columns])
        store_halves(core, down, up, keep_ref, send_ref, slice(256 * block, 256 * block + 256))
    gain_grad = back_part(starts[-1], gain_grad)
    last_part(starts[-1])
    gain_grad_ref[...] = gain_grad

    out_grad_ref[...] = dot(mixed_turned_s[...], low_s[...])


def backward_kernel(
    place_ref, inputs_ref, proj_ref, key_turned_ref, probs_ref, mixed_grad_ref, out_grad_ref,
    proj_grad_ref, keep_ref, send_ref,
    upstream_s, query_grad_s,
):
    core = place_ref[1]
    upstream_s[...] = mixed_grad_ref[...].T
    mask = head_mask()
    wide_mask = mask.astype(F32)
    turned_mask = turned_head_mask()
    lower = lane_half()

    def attend_back(i, carry):
        units = []
        for n in range(AHEAD):
            pair = i * AHEAD + n
            rows = pl.ds(pl.multiple_of(pair * 128, 128), 128)
            for side in range(2):
                lanes = slice(128 * side, 128 * side + 128)
                parts = (
                    proj_ref[rows, lanes],
                    key_turned_ref[lanes, rows],
                    proj_ref[rows, 512 + 128 * side : 640 + 128 * side],
                    probs_ref[2 * pair + side],
                    mixed_grad_ref[rows, lanes],
                    upstream_s[lanes, rows],
                )
                units.append((side, lanes, rows, parts))
        results = [
            attend_unit_back(*parts, lower, mask, turned_mask, wide_mask) for _, _, _, parts in units
        ]
        for (side, lanes, rows, _), grads in zip(units, results):
            query_grad_s[lanes, rows] = grads[0]
            proj_grad_ref[rows, 256 + 128 * side : 384 + 128 * side] = grads[1]
            proj_grad_ref[rows, 512 + 128 * side : 640 + 128 * side] = grads[2]
        return carry

    lax.fori_loop(0, 8 // AHEAD, attend_back, 0)
    proj_grad_ref[:, 0:256] = query_grad_s[...].T

    inputs_turned = inputs_ref[...].T
    terms = [
        dot(inputs_turned, proj_grad_ref[:, 256 * block : 256 * block + 256])
        for block in range(3)
    ]
    terms.append(out_grad_ref[...])
    for block in range(2):
        rows = slice(256 * block, 256 * block + 256)
        store_halves(core, terms[block], terms[2 + block], keep_ref, send_ref, rows)


def head_kernel(
    xs_ref, in_ref, proj_grad_ref, resid_grad_ref, gain_two_grad_ref, gain_one_ref, w_qkv_ref,
    grad_ref, small_ref,
):
    gain_one = gain_one_ref[...]

    def head(i, gain_grad):
        rows = pl.ds(pl.multiple_of(i * 512, 512), 512)
        normed, inverse = norm(in_ref[rows, :].astype(F32))
        in_grad = dot_nt(proj_grad_ref[rows, :], w_qkv_ref[...])
        grad_ref[rows, :] = resid_grad_ref[rows, :] + norm_back(in_grad, normed, inverse, gain_one)
        return gain_grad + fold_rows(in_grad * normed)

    gain_grad = lax.fori_loop(0, 2, head, jnp.zeros((8, C), F32), unroll=2)

    def taps(g, sums):
        j, p = g // 8, g % 8
        grad = grad_ref[pl.ds(pl.multiple_of(g * 64, 64), 64), :]
        return tuple(
            sums[3 * u + v] + fold_rows(grad * xs_ref[j + v, p + u].astype(F32))
            for u in range(3)
            for v in range(3)
        )

    kernel_grad = lax.fori_loop(0, 16, taps, (jnp.zeros((8, C), F32),) * 9, unroll=16)
    small = [jnp.sum(term, axis=0, keepdims=True) for term in kernel_grad]
    small.append(jnp.sum(gain_grad, axis=0, keepdims=True))
    small.append(jnp.sum(gain_two_grad_ref[...], axis=0, keepdims=True))
    small.append(jnp.zeros((5, C), F32))
    small_ref[...] = jnp.concatenate(small, axis=0)


def pieces_kernel(
    grad_ref, small_ref, tail_ref, other_tail_ref, head_ref, other_head_ref, perm_ref, out_ref
):
    perm = perm_ref[...]
    edge = jnp.zeros((8, C), F32)
    for r in range(4):
        parts = [grad_ref[64 * g + 16 * r : 64 * g + 16 * r + 16, :] for g in range(16)]
        for j in range(2):
            lowest = 64 * (8 * j + 7) + 16 * r - 8
            parts.append(grad_ref[lowest : lowest + 8, :] if r > 0 else edge)
        for j in range(2):
            highest = 64 * 8 * j + 16 * r + 16
            parts.append(grad_ref[highest : highest + 8, :] if r < 3 else edge)
        parts.append(small_ref[8 * r : 8 * r + 8, :] if r < 2 else edge)
        parts.append(jnp.zeros((88, C), F32))
        tokens = jnp.concatenate(parts, axis=0).astype(BF16)
        moved = dot(perm, tokens).reshape(8, PIECE, C)
        rows = slice(256 * r, 256 * r + 256)
        tail = tail_ref[rows, :].astype(F32) + other_tail_ref[rows, :].astype(F32)
        rows = slice(128 * r, 128 * r + 128)
        head = head_ref[rows, :].astype(F32) + other_head_ref[rows, :].astype(F32)
        joined = [moved, tail.reshape(8, 32, C), head.reshape(8, 16, C)]
        joined = jnp.concatenate(joined, axis=1)
        out_ref[r] = joined.reshape(8 * JOINED, C).astype(BF16)


def partial_kernel(factor, x_ref, out_ref):
    total = jnp.zeros((SHARE, C), F32)
    for r in range(4):
        pieces = jnp.sum(x_ref[r].astype(F32).reshape(8, JOINED, C), axis=0)
        total = total + jnp.concatenate([pieces[PIECE:], pieces[32:40]], axis=0)
    out_ref[...] = (total * factor).astype(BF16)


def total_kernel(mine_ref, other_ref, out_ref):
    total = mine_ref[...].astype(F32) + other_ref[...].astype(F32)
    rows = jnp.concatenate([total] * 8, axis=0).astype(BF16)
    for r in range(4):
        out_ref[r] = rows


def unpack_kernel(pieces_ref, main_ref, edges_ref, tile_ref, first_ref, last_ref):
    for block in range(4):
        pieces = pieces_ref[block].astype(F32).reshape(8, JOINED, C)
        pieces = pieces[:, :PIECE].reshape(8 * PIECE, C).astype(BF16)
        columns = dot(main_ref[...], pieces).astype(BF16)
        tile_ref[:, 16 * block : 16 * block + 16, :] = columns.reshape(18, 16, C)
        if block == 0:
            first_ref[...] = dot(edges_ref[0], pieces).astype(BF16)
        if block == 3:
            last_ref[...] = dot(edges_ref[1], pieces).astype(BF16)


def tile_kernel(tile_ref, left_ref, right_ref, dw_ref, out_ref, wide):
    wide[:, 8:72, :] = tile_ref[...].astype(F32)
    left = left_ref[...].astype(F32)
    right = right_ref[...].astype(F32)
    for i in range(18):
        wide[i, 7:8, :] = left[i : i + 1]
        wide[i, 72:73, :] = right[i : i + 1]

    def row(i, carry):
        rows = [wide[i + 2 - u] for u in range(3)]
        total = wide[i + 1, 8:72, :]
        for v in range(3):
            term = dw_ref[v : v + 1, :] * rows[0]
            for u in range(1, 3):
                term = term + dw_ref[3 * u + v : 3 * u + v + 1, :] * rows[u]
            total = total + term[9 - v : 73 - v, :]
        out_ref[0, i] = total
        return carry

    lax.fori_loop(0, 16, row, 0)


def write_half(half, rows, qkv_ref, out_ref, up_ref, down_ref, tall, wide, sems):
    values = rows[...].astype(F32)
    tail = values[:, 0:32].reshape(1024, C)
    head = values[:, 32:48].reshape(512, C)

    def run(pairs):
        copies = [pltpu.make_async_copy(*pair, sems.at[i]) for i, pair in enumerate(pairs)]
        for copy in copies:
            copy.start()
        for copy in copies:
            copy.wait()

    @pl.when(half == 0)
    def _():
        tall[...] = tail
        wide[:, 0:256] = head[0:256]
        wide[:, 256:512] = head[256:512]
        run([(tall, down_ref), (wide.at[:, 0:512], qkv_ref.at[:, 0:512])])

    @pl.when(half == 1)
    def _():
        for block in range(4):
            wide[:, 256 * block : 256 * block + 256] = tail[256 * block : 256 * block + 256]
        tall[0:512, :] = head
        run([
            (wide, up_ref),
            (tall.at[0:256, :], qkv_ref.at[:, 512:768]),
            (tall.at[256:512, :], out_ref),
        ])


def first_outputs_kernel(place_ref, mine_ref, *refs):
    write_half(place_ref[1], mine_ref, *refs)


def outputs_kernel(
    place_ref, mine_ref, other_ref, qkv_in, out_in, up_in, down_in,
    kernel_ref, gain_one_ref, gain_two_ref, qkv_ref, out_ref, up_ref, down_ref,
    tall, wide, sems, kernel_s, gain_one_s, gain_two_s, small_sems,
):
    small = mine_ref[0:16].astype(F32) + other_ref[0:16].astype(F32)
    small = jnp.concatenate([small[k, 52:53] for k in range(16)], axis=0)
    for u in range(3):
        kernel_s[u] = small[3 * u : 3 * u + 3]
    gain_one_s[...] = small[9:10]
    gain_two_s[...] = small[10:11]
    pairs = ((kernel_s, kernel_ref), (gain_one_s, gain_one_ref), (gain_two_s, gain_two_ref))
    copies = [pltpu.make_async_copy(*pair, small_sems.at[i]) for i, pair in enumerate(pairs)]
    for copy in copies:
        copy.start()
    half = 1 - place_ref[1]
    write_half(half, other_ref, qkv_ref, out_ref, up_ref, down_ref, tall, wide, sems)
    for copy in copies:
        copy.wait()


VMEM = pl.BlockSpec(memory_space=pltpu.VMEM)
SMEM = pl.BlockSpec(memory_space=pltpu.SMEM)
HBM = pl.BlockSpec(memory_space=pl.ANY)


def call(kernel, outs, operands, scratch=(), scalars=0, flops=0, moved=0, limit=24):
    return pl.pallas_call(
        kernel,
        out_shape=tuple(jax.ShapeDtypeStruct(shape, dtype) for shape, dtype in outs),
        in_specs=[SMEM] * scalars + [VMEM] * (len(operands) - scalars),
        out_specs=tuple(VMEM for _ in outs),
        scratch_shapes=[pltpu.VMEM(shape, dtype) for shape, dtype in scratch],
        compiler_params=pltpu.CompilerParams(vmem_limit_bytes=limit * 2**20),
        cost_estimate=pl.CostEstimate(flops=flops, bytes_accessed=moved, transcendentals=0),
    )(*operands)


def local(input_map, dw_kernel, gain_one, w_qkv, w_out, gain_two, w_up, w_down, cotangent):
    owner = lax.axis_index("row") * 8 + lax.axis_index("col")
    core = lax.axis_index("core")
    place = jnp.stack([owner, core]).astype(jnp.int32)
    dw_rows = dw_kernel.reshape(9, C).astype(F32)

    def exchange(stacked):
        return lax.all_to_all(stacked, ("row", "col"), split_axis=0, concat_axis=0, tiled=True)

    def swap(values, axis):
        return lax.ppermute(values, axis, [(0, 1), (1, 0)])

    def shift(values, axis, step):
        size = lax.axis_size(axis)
        pairs = [(i, i + step) for i in range(size) if 0 <= i + step < size]
        return lax.ppermute(values, axis, pairs)

    (packed,) = call(
        pack_kernel,
        [((32, 6, 16, C), BF16)],
        [input_map[0], cotangent[0]],
        flops=4 * 10**8,
        moved=4 * 10**6,
        limit=60,
    )
    packed, place, dw_rows = lax.optimization_barrier((packed, place, dw_rows))
    arrived = exchange(packed)

    (
        xs, start, inputs, projected, key_turned, probs, mixed_grad, resid_grad, tail_keep, tail_send,
        out_grad, gain_two_grad,
    ) = call(
        forward_kernel,
        [
            ((4, 10, 64, C), BF16),
            ((TOKENS, C), BF16),
            ((TOKENS, C), BF16),
            ((TOKENS, 3 * C), BF16),
            ((C, TOKENS), BF16),
            ((16, 256, 128), BF16),
            ((TOKENS, C), BF16),
            ((TOKENS, C), F32),
            ((1024, C), BF16),
            ((1024, C), BF16),
            ((C, C), F32),
            ((8, C), F32),
        ],
        [
            place, arrived, dw_rows,
            gain_one.reshape(1, C), w_qkv, w_out, gain_two.reshape(1, C), w_up, w_down,
        ],
        [
            ((TOKENS, C), BF16),
            ((TOKENS, C), BF16),
            ((TOKENS, C), BF16),
            ((TOKENS, C), BF16),
            ((TOKENS, FF), BF16),
            ((TOKENS, FF), BF16),
            ((2 * C, TOKENS), BF16),
            ((C, TOKENS), BF16),
            ((TOKENS, C), F32),
            ((TOKENS, C), F32),
            ((TOKENS, FF), F32),
            ((TOKENS, FF), F32),
        ],
        scalars=1,
        flops=8 * 10**9,
        moved=12 * 10**6,
        limit=36,
    )

    proj_grad, keep, send = call(
        backward_kernel,
        [((TOKENS, 3 * C), BF16), ((512, C), BF16), ((512, C), BF16)],
        [place, inputs, projected, key_turned, probs, mixed_grad, out_grad],
        [((C, TOKENS), BF16), ((C, TOKENS), BF16)],
        scalars=1,
        flops=5 * 10**9,
        moved=8 * 10**6,
        limit=32,
    )
    grad, small = call(
        head_kernel,
        [((TOKENS, C), F32), ((16, C), F32)],
        [xs, start, proj_grad, resid_grad, gain_two_grad, gain_one.reshape(1, C), w_qkv],
    )
    (pieces,) = call(
        pieces_kernel,
        [((4, 8 * JOINED, C), BF16)],
        [
            grad, small, tail_keep, swap(tail_send, "core"), keep, swap(send, "core"),
            jnp.asarray(groups_to_pieces(), BF16),
        ],
    )
    back = exchange(pieces.reshape(32, JOINED, C)).reshape(4, 8 * JOINED, C)
    factor = 1.0 / math.sqrt(TOKENS * 128)
    (partial,) = call(
        lambda x_ref, out_ref: partial_kernel(factor, x_ref, out_ref),
        [((SHARE, C), BF16)],
        [back],
    )
    main, edges = (jnp.asarray(t, BF16) for t in pieces_to_tile())
    tile, first, last = call(
        unpack_kernel,
        [((18, 64, C), BF16), ((32, C), BF16), ((32, C), BF16)],
        [back, main, edges],
    )
    left, right = shift(last, "col", 1), shift(first, "col", -1)
    (shared,) = call(
        total_kernel,
        [((4, 8 * SHARE, C), BF16)],
        [partial, swap(partial, "yh")],
    )
    mine = exchange(shared.reshape(32, SHARE, C))
    (input_grad,) = call(
        tile_kernel,
        [((1, 16, 64, C), F32)],
        [tile, left, right, dw_rows],
        [((18, 80, C), F32)],
    )
    mine, input_grad = lax.optimization_barrier((mine, input_grad))
    other = swap(mine, "core")
    large = tuple(jax.ShapeDtypeStruct(n, F32) for n in ((C, 3 * C), (C, C), (C, FF), (FF, C)))
    small = tuple(jax.ShapeDtypeStruct(n, F32) for n in ((3, 3, C), (1, C), (1, C)))
    scratch = [pltpu.VMEM((FF, C), F32), pltpu.VMEM((C, FF), F32), pltpu.SemaphoreType.DMA((3,))]
    settings = dict(compiler_params=pltpu.CompilerParams(vmem_limit_bytes=24 * 2**20))
    begun = pl.pallas_call(
        first_outputs_kernel,
        out_shape=large,
        in_specs=[SMEM, VMEM],
        out_specs=(HBM,) * 4,
        scratch_shapes=scratch,
        **settings,
    )(place, mine)
    kernel_grad, gain_one_grad, gain_two_sum, qkv_grad, out_sum, up_grad, down_grad = pl.pallas_call(
        outputs_kernel,
        out_shape=small + large,
        in_specs=[SMEM, VMEM, VMEM] + [HBM] * 4,
        out_specs=(HBM,) * 7,
        scratch_shapes=scratch
        + [pltpu.VMEM(part.shape, F32) for part in small]
        + [pltpu.SemaphoreType.DMA((3,))],
        input_output_aliases={3: 3, 4: 4, 5: 5, 6: 6},
        **settings,
    )(place, mine, other, *begun)
    return (
        input_grad,
        kernel_grad,
        gain_one_grad.reshape(C),
        qkv_grad,
        out_sum,
        gain_two_sum.reshape(C),
        up_grad,
        down_grad,
    )


def solution(mesh):
    cores = Mesh(mesh.devices.reshape(2, 2, 4, 8), ("yh", "core", "row", "col"))
    split = P(("yh", "core"), "row", "col", None)
    in_specs = (split, P(), P(), P(), P(), P(), P(), P(), split)
    out_specs = (split, P(), P(), P(), P(), P(), P(), P())
    return jax.shard_map(local, mesh=cores, in_specs=in_specs, out_specs=out_specs, check_vma=False)
```
